128 devices in a mesh: wide: 16 (over x, z), narrow: 8 (over y, core).
Axes of the slice: x: 4, y: 4, z: 4, core: 2. Of those that a mesh axis runs over, the one named last changes fastest.
Arguments:
- pressure: float32 [128, 128, 1024], P('wide', 'narrow'), may hold values from -6 to 6
- divergence: float32 [128, 128, 1024], P('wide', 'narrow'), may hold values from -6 to 6
- mobility: float32 [128, 128, 1024], P('wide', 'narrow'), may hold values from 0.1 to 10
Outputs:
- pressure_out: float32 [128, 128, 1024], P('wide', 'narrow')
- residual_out: float32 [128, 128, 1024], P('wide', 'narrow')
The draws below stay inside these ranges and needn't reach their ends.
All inputs are finite; a program needn't handle non-finite values.
Results may differ from the reference program's by a relative error of at most 0.00004.
Values sent between devices are 32-bit elements; how exact they have to be, the bound alone decides.
No kernel may reach another device: no remote copies, remote signals or barrier semaphores. Data moves between devices by JAX's collectives and lax.ppermute only.
A program may use at most 128 MiB of HBM per device.

```python
import math
import jax
import jax.numpy as jnp

NU = 2
NX = 128
NY = 128
NZ = 1024


def block_levels(key, dims, split, low, top_value):
    level, own = 1.0, jax.random.fold_in(key, 6)
    for dim, parts in split:
        draws = jnp.exp(jax.random.uniform(jax.random.fold_in(own, dim), (parts,), jnp.float32, low / len(split), top_value / len(split)))
        level = level * jnp.repeat(draws, dims[dim] // parts).reshape([-1 if axis == dim else 1 for axis in range(len(dims))])
    return level


def gaussian(key, shape, deviation, most, cuts=(), kind=jnp.bfloat16):
    drawn = jax.random.normal(key, shape, jnp.float32) * deviation
    if len(cuts) > 0:
        drawn = block_levels(key, shape, cuts, -0.22, 0.18) * drawn
    return jnp.clip(drawn, min=-most, max=most).astype(kind)


def setup_inputs(seed: int = 0) -> dict:
    arg_keys = jax.random.split(jax.random.key(seed), 4)
    return {
        "pressure": gaussian(arg_keys[0], (NX, NY, NZ), 1.0, 6.0, ((0, 16), (1, 8)), jnp.float32),
        "divergence": gaussian(arg_keys[1], (NX, NY, NZ), 1.0, 6.0, ((0, 16), (1, 8)), jnp.float32),
        "mobility": jnp.clip(jnp.exp(math.log(10.0) - 4.6051702 * jax.random.uniform(arg_keys[2], (NX, NY, NZ), jnp.float32) ** block_levels(arg_keys[2], (NX, NY, NZ), ((0, 16), (1, 8)), -0.2, 0.2)), 0.1, 10.0),
    }


OMEGA = 0.8
NEIGHBOURS = [(slice(2, None), slice(1, -1), slice(1, -1)), (slice(0, -2), slice(1, -1), slice(1, -1)), (slice(1, -1), slice(2, None), slice(1, -1)), (slice(1, -1), slice(0, -2), slice(1, -1)), (slice(1, -1), slice(1, -1), slice(2, None)), (slice(1, -1), slice(1, -1), slice(0, -2))]
MIDDLE = (slice(1, -1), slice(1, -1), slice(1, -1))

def apply_operator(field_pad, coeff_pad, factor):
    centre = field_pad[MIDDLE]
    weight = coeff_pad[MIDDLE]
    accumulated = jnp.zeros_like(centre)
    for offset in NEIGHBOURS:
        accumulated = accumulated + 0.5 * (weight + coeff_pad[offset]) * (centre - field_pad[offset])
    return factor * accumulated

def diagonal_of(coeff_pad, factor):
    weight = coeff_pad[MIDDLE]
    accumulated = jnp.zeros_like(weight)
    for offset in NEIGHBOURS:
        accumulated = accumulated + 0.5 * (weight + coeff_pad[offset])
    return factor * accumulated

def coarsen(values):
    first, second, third = values.shape
    return values.reshape(first // 2, 2, second // 2, 2, third // 2, 2).mean(axis=(1, 3, 5))

def refine(values):
    return jnp.repeat(jnp.repeat(jnp.repeat(values, 2, axis=0), 2, axis=1), 2, axis=2)

def dense_solve(source, coeff, factor):
    coeff_pad = jnp.pad(coeff, 1)
    count = source.size
    basis = jnp.eye(count, dtype=jnp.float32).reshape((count,) + source.shape)
    matrix = jax.vmap(lambda column: apply_operator(jnp.pad(column, 1), coeff_pad, factor).reshape(-1))(basis)
    lower = jnp.linalg.cholesky(matrix)
    solved = jax.scipy.linalg.cho_solve((lower, True), source.reshape(-1))
    return solved.reshape(source.shape)

def relax(field, source, coeff_pad, diagonal, factor):
    for sweep in range(NU):
        field = field + OMEGA * (source - apply_operator(jnp.pad(field, 1), coeff_pad, factor)) / diagonal
    return field

def cycle(field, source, coeff, level):
    factor = 0.25 ** level
    if level == 6:
        return dense_solve(source, coeff, factor)
    coeff_pad = jnp.pad(coeff, 1)
    diagonal = diagonal_of(coeff_pad, factor)
    field = relax(field, source, coeff_pad, diagonal, factor)
    leftover = source - apply_operator(jnp.pad(field, 1), coeff_pad, factor)
    coarse_source = coarsen(leftover)
    correction = cycle(jnp.zeros_like(coarse_source), coarse_source, coarsen(coeff), level + 1)
    field = field + refine(correction)
    return relax(field, source, coeff_pad, diagonal, factor)

def reference(pressure, divergence, mobility):
    result = cycle(pressure, divergence, mobility, 0)
    leftover = divergence - apply_operator(jnp.pad(result, 1), jnp.pad(mobility, 1), 1.0)
    return (result, leftover)
```

```python
import jax
import jax.numpy as jnp
from jax import lax
from jax.experimental import pallas as pl
from jax.experimental.pallas import tpu as pltpu
from jax.sharding import Mesh, PartitionSpec as P

OMEGA = 0.8
AX = ("wide", "ny", "core")
F32 = jnp.float32
LIMIT = 48 * 1024 * 1024


def iota(shape, dim):
    return lax.broadcasted_iota(jnp.int32, shape, dim)


def following(x, dim):
    return pltpu.roll(x, x.shape[dim] - 1, dim)


def preceding(x, dim):
    return pltpu.roll(x, 1, dim)


def add_z_ends(out, c, v):
    length = out.shape[1]
    lane = iota((out.shape[0], 128), 1)
    if length == 128:
        return out + jnp.where((lane == 0) | (lane == 127), 0.5 * c * v, 0.0)
    low = out[:, :128] + jnp.where(lane == 0, 0.5 * c[:, :128] * v[:, :128], 0.0)
    high = out[:, -128:] + jnp.where(lane == 127, 0.5 * c[:, -128:] * v[:, -128:], 0.0)
    parts = [low, high] if length == 256 else [low, out[:, 128:-128], high]
    return jnp.concatenate(parts, axis=1)


def row_operator(v, below, above, c, fa_below, fa_above, fb, fz):
    gb = fb * (following(v, 0) - v)
    gz = fz * (following(v, 1) - v)
    out = fa_above * (v - above) + fa_below * (v - below)
    out = out + (preceding(gb, 0) - gb) + (preceding(gz, 1) - gz)
    return add_z_ends(out, c, v)


def row_diagonal(c, fa_below, fa_above, fb, fz):
    out = fa_above + fa_below + (fb + preceding(fb, 0)) + (fz + preceding(fz, 1))
    return add_z_ends(out, c, jnp.ones_like(c))


def half_compress(low, high, dim):
    length = low.shape[dim]
    at = iota(low.shape, dim)
    index = (2 * at) % length
    first = jnp.take_along_axis(low, index, axis=dim)
    if high is None:
        return jnp.where(at < length // 2, first, 0.0)
    return jnp.where(at < length // 2, first, jnp.take_along_axis(high, index, axis=dim))


def pair_sums(x, dim, tile):
    x = x + following(x, dim)
    count = x.shape[dim] // tile

    def piece(r, l, t):
        if dim == 0:
            return x[8 * t : 8 * t + 8, 128 * l : 128 * l + 128]
        return x[8 * r : 8 * r + 8, 128 * t : 128 * t + 128]

    rows, lanes = x.shape[0] // 8, x.shape[1] // 128
    half = max(count // 2, 1)
    if dim == 0:
        out = [
            [half_compress(piece(0, l, 2 * t), piece(0, l, 2 * t + 1) if count > 1 else None, 0) for l in range(lanes)]
            for t in range(half)
        ]
    else:
        out = [
            [half_compress(piece(r, 0, 2 * t), piece(r, 0, 2 * t + 1) if count > 1 else None, 1) for t in range(half)]
            for r in range(rows)
        ]
    joined = [line[0] if len(line) == 1 else jnp.concatenate(line, axis=1) for line in out]
    return joined[0] if len(joined) == 1 else jnp.concatenate(joined, axis=0)


def coarse_sum(first, second):
    return pair_sums(pair_sums(first + second, 0, 8), 1, 128)


def repeat_lanes(x, block):
    source = block // 2
    index = iota((8, 128), 1) // 2 + 64 * (block % 2)
    return jnp.take_along_axis(x[:, 128 * source : 128 * source + 128], index, axis=1)


def take_rows(x, index):
    pieces = [
        jnp.take_along_axis(x[:, k : k + 128], index, axis=0) for k in range(0, x.shape[1], 128)
    ]
    return pieces[0] if len(pieces) == 1 else jnp.concatenate(pieces, axis=1)


def widen(x, blocks):
    pieces = [repeat_lanes(x, k) for k in range(blocks)]
    return pieces[0] if len(pieces) == 1 else jnp.concatenate(pieces, axis=1)


def scalars():
    wide, ny, core = lax.axis_index("wide"), lax.axis_index("ny"), lax.axis_index("core")
    sizes = [lax.axis_size(name) for name in AX]
    narrow = ny * sizes[2] + core
    inside = [
        jnp.where(flag, 1.0, 0.0).astype(F32)
        for flag in (wide > 0, wide < sizes[0] - 1, narrow > 0, narrow < sizes[1] * sizes[2] - 1)
    ]
    return wide, narrow, core, inside


def call(kernel, outs, scratch, *args, flops=1_000_000):
    vmem = pl.BlockSpec(memory_space=pltpu.VMEM)
    size = 4 * sum(a.size for a in args)
    return pl.pallas_call(
        kernel,
        out_shape=[jax.ShapeDtypeStruct(s, F32) for s in outs],
        in_specs=[vmem] * len(args),
        out_specs=[vmem] * len(outs),
        scratch_shapes=[pltpu.VMEM(s, F32) for s in scratch],
        compiler_params=pltpu.CompilerParams(vmem_limit_bytes=LIMIT),
        cost_estimate=pl.CostEstimate(flops=flops, bytes_accessed=size, transcendentals=0),
    )(*args)


def pack_zero(p, d, m, left, right, to_left, to_right):
    _, _, _, (low, high, _, _) = scalars()
    at = iota((8, 1024), 0)
    for r in range(14):
        a = r - 3
        for side, out in ((0, to_left), (1, to_right)):
            tile = slice(8 * side, 8 * side + 8)
            if a < 0:
                vp, vm = left[r, tile] * low, left[3 + r, tile] * low
                vd = left[5 + r, tile] * low if r > 0 else jnp.zeros_like(vp)
            elif a < 8:
                vp, vm, vd = p[a, tile], m[a, tile], d[a, tile]
            else:
                vp, vm = right[a - 8, tile] * high, right[a - 5, tile] * high
                vd = right[a - 2, tile] * high if a < 10 else jnp.zeros_like(vp)
            if side == 0:
                vm, vd = pltpu.roll(vm, 3, 0), pltpu.roll(vd, 6, 0)
                out[r] = jnp.where(at < 3, vp, jnp.where(at < 6, vm, vd))
            else:
                vm, vd = pltpu.roll(vm, 5, 0), pltpu.roll(vd, 2, 0)
                out[r] = jnp.where(at >= 5, vp, jnp.where(at >= 2, vm, vd))


def faces(c, rows, fa, fb, fz, w, cols, mask_b):
    lo, hi = rows
    length = c.shape[2]
    last = iota((cols, length), 1) == length - 1

    def one_face(r, carry):
        fa[r] = 0.5 * (c[r] + c[r + 1])
        return carry

    lax.fori_loop(lo - 1, hi, one_face, 0)

    def one(r, carry):
        here = c[r]
        b = 0.5 * (here + following(here, 0))
        z = jnp.where(last, 0.0, 0.5 * (here + following(here, 1)))
        fb[r], fz[r] = b, z
        diagonal = row_diagonal(here, fa[r - 1], fa[r], b, z)
        w[r] = jnp.where(here > 0.0, OMEGA / diagonal, 0.0)
        return carry

    lax.fori_loop(lo, hi, one, 0)


def sweep(source, target, s, c, fa, fb, fz, w, rows):
    def one(r, carry):
        v = source[r]
        a = row_operator(v, source[r - 1], source[r + 1], c[r], fa[r - 1], fa[r], fb[r], fz[r])
        target[r] = v + w[r] * (s[r] - a)
        return carry

    lax.fori_loop(rows[0], rows[1], one, 0)


def residual_row(v, s, c, fa, fb, fz, r):
    return s[r] - row_operator(v[r], v[r - 1], v[r + 1], c[r], fa[r - 1], fa[r], fb[r], fz[r])


def level_zero(p, d, m, left, right, nleft, nright, field, me, de, s1, c1, up, down, v, u, fa, fb, fz, w):
    _, _, _, (low, high, nlow, nhigh) = scalars()
    at = iota((8, 1024), 0)
    for r in range(14):
        a = r - 3
        if a < 0:
            v[r, 0:16], me[r, 0:16] = left[r] * low, left[3 + r] * low
            de[r, 0:16] = left[5 + r] * low if r > 0 else jnp.zeros((16, 1024), F32)
        elif a < 8:
            v[r, 0:16], me[r, 0:16], de[r, 0:16] = p[a], m[a], d[a]
        else:
            v[r, 0:16], me[r, 0:16] = right[a - 8] * high, right[a - 5] * high
            de[r, 0:16] = right[a - 2] * high if a < 10 else jnp.zeros((16, 1024), F32)
        x, y = nright[r] * nhigh, nleft[r] * nlow
        v[r, 16:24] = jnp.where(at < 3, x, jnp.where(at >= 5, y, 0.0))
        x3, y3 = pltpu.roll(x, 5, 0), pltpu.roll(y, 3, 0)
        me[r, 16:24] = jnp.where(at < 3, x3, jnp.where(at >= 5, y3, 0.0))
        x6, y6 = pltpu.roll(x, 2, 0), pltpu.roll(y, 6, 0)
        de[r, 16:24] = jnp.where(at < 2, x6, jnp.where(at >= 6, y6, 0.0))
    faces(me, (1, 13), fa, fb, fz, w, 24, None)
    u[0], u[13] = v[0], v[13]
    sweep(v, u, de, me, fa, fb, fz, w, (1, 13))
    sweep(u, v, de, me, fa, fb, fz, w, (2, 12))
    field[...] = v[3:11, 0:16]

    def coarse(i, carry):
        r = 2 * i + 3
        x = residual_row(v, de, me, fa, fb, fz, r)[0:16]
        y = residual_row(v, de, me, fa, fb, fz, r + 1)[0:16]
        s1[i] = 0.5 * coarse_sum(x, y)
        c1[i] = 0.125 * coarse_sum(me[r, 0:16], me[r + 1, 0:16])
        return carry

    lax.fori_loop(0, 4, coarse, 0)
    up[0:3], down[0:3] = s1[1:4], s1[0:3]
    up[3:7], down[3:7] = c1[...], c1[...]


def pack_one(s, c, left, right, to_left, to_right):
    _, _, _, (low, high, _, _) = scalars()
    at = iota((8, 512), 0)
    for r in range(12):
        a = r - 4
        if a < 0:
            vc = left[3 + r] * low
            vs = left[r - 1] * low if r > 0 else jnp.zeros_like(vc)
        elif a < 4:
            vs, vc = s[a], c[a]
        else:
            vc = right[a - 1] * high
            vs = right[a - 4] * high if a < 7 else jnp.zeros_like(vc)
        to_left[r] = jnp.where(at < 4, vc, pltpu.roll(vs, 4, 0))
        to_right[r] = jnp.where(at >= 4, vc, pltpu.roll(vs, 4, 0))


def level_one(s, c, left, right, nleft, nright, f0, se, ce, field, send, keep, up, down, v, u, fa, fb, fz, w):
    _, _, core, (low, high, nlow, nhigh) = scalars()
    at = iota((8, 512), 0)
    for r in range(12):
        a = r - 4
        if a < 0:
            ce[r, 0:8] = left[3 + r] * low
            se[r, 0:8] = left[r - 1] * low if r > 0 else jnp.zeros((8, 512), F32)
        elif a < 4:
            se[r, 0:8], ce[r, 0:8] = s[a], c[a]
        else:
            ce[r, 0:8] = right[a - 1] * high
            se[r, 0:8] = right[a - 4] * high if a < 7 else jnp.zeros((8, 512), F32)
        x, y = nright[r] * nhigh, nleft[r] * nlow
        ce[r, 8:16] = jnp.where(at < 4, x, y)
        se[r, 8:16] = jnp.where(at < 4, pltpu.roll(x, 4, 0), pltpu.roll(y, 4, 0))
    faces(ce, (2, 10), fa, fb, fz, w, 16, None)

    def first(r, carry):
        u[r] = w[r] * se[r]
        return carry

    lax.fori_loop(2, 10, first, 0)
    sweep(u, v, se, ce, fa, fb, fz, w, (3, 9))
    field[...] = v[4:8, 0:8]
    rows = iota((8, 256), 0)
    index = iota((8, 256), 0) % 4
    mine = rows // 4 == core
    for i in range(2):
        r = 2 * i + 4
        x = residual_row(v, se, ce, fa, fb, fz, r)[0:8]
        y = residual_row(v, se, ce, fa, fb, fz, r + 1)[0:8]
        s2 = 0.5 * coarse_sum(x, y)
        c2 = 0.125 * coarse_sum(ce[r, 0:8], ce[r + 1, 0:8])
        s2 = jnp.where(mine, take_rows(s2, index[:, :128]), 0.0)
        c2 = jnp.where(mine, take_rows(c2, index[:, :128]), 0.0)
        send[i] = jnp.where(core == 0, c2, s2)
        keep[i] = jnp.where(core == 0, s2, c2)
    for r in range(3):
        for t in range(2):
            up[2 * r + t] = f0[5 + r, 8 * t : 8 * t + 8]
            down[2 * r + t] = f0[r, 8 * t : 8 * t + 8]
    for r in range(2):
        both = jnp.concatenate([field[2 * r], field[2 * r + 1]], axis=1)
        up[6 + r] = both
        down[6 + r] = both


def pack_up(f0, f1, left, right, to_left, to_right):
    _, _, _, (low, high, _, _) = scalars()
    at = iota((8, 1024), 0)
    for r in range(14):
        for side, out in ((0, to_left), (1, to_right)):
            tile = slice(8 * side, 8 * side + 8)
            if r < 3:
                x = left[2 * r + side] * low
            elif r < 11:
                x = f0[r - 3, tile]
            else:
                x = right[2 * (r - 11) + side] * high
            if r < 2:
                y = left[6 + r] * low
            elif r < 4:
                y = jnp.concatenate([f1[2 * r - 4], f1[2 * r - 3]], axis=1)
            elif r < 6:
                y = right[2 + r] * high
            else:
                y = None
            if y is not None:
                y = pltpu.roll(y, 4, 0)
                x = jnp.where(at < 4, x, y) if side == 0 else jnp.where(at >= 4, x, y)
            out[r] = x


def level_up(me, de, w, f0, left, right, nleft, nright, se, ce, f1, e2, out, res, v, u, fa, fb, fz, v1, u1, fa1, fb1, fz1, w1):
    _, _, _, (low, high, nlow, nhigh) = scalars()
    at = iota((8, 512), 0)
    half = iota((8, 128), 0)
    for r in range(12):
        if r < 4:
            f = left[6 + r // 2][:, 512 * (r % 2) : 512 * (r % 2) + 512] * low
        elif r < 8:
            f = f1[r - 4]
        else:
            f = right[2 + r // 2][:, 512 * (r % 2) : 512 * (r % 2) + 512] * high
        x = nright[r // 2][:, 512 * (r % 2) : 512 * (r % 2) + 512] * nhigh
        y = nleft[r // 2][:, 512 * (r % 2) : 512 * (r % 2) + 512] * nlow
        g = jnp.where(at < 4, pltpu.roll(x, 4, 0), pltpu.roll(y, 4, 0))
        e = e2[r // 2]
        own = widen(take_rows(e, 2 + half // 2), 4)
        beside = widen(take_rows(e, jnp.where(half < 4, 6 + half // 2, (half - 4) // 2)), 4)
        v1[r, 0:8] = f + jnp.where(ce[r, 0:8] > 0.0, own, 0.0)
        v1[r, 8:16] = g + jnp.where(ce[r, 8:16] > 0.0, beside, 0.0)
    faces(ce, (1, 11), fa1, fb1, fz1, w1, 16, None)
    sweep(v1, u1, se, ce, fa1, fb1, fz1, w1, (1, 11))
    sweep(u1, v1, se, ce, fa1, fb1, fz1, w1, (2, 10))
    zero = iota((8, 1024), 0)
    for r in range(14):
        if r < 3:
            f = [left[2 * r] * low, left[2 * r + 1] * low]
        elif r < 11:
            f = [f0[r - 3, 0:8], f0[r - 3, 8:16]]
        else:
            f = [right[2 * (r - 11)] * high, right[2 * (r - 11) + 1] * high]
        x, y = nright[r] * nhigh, nleft[r] * nlow
        f.append(jnp.where(zero < 3, x, jnp.where(zero >= 5, y, 0.0)))
        e = v1[(r + 5) // 2]
        pieces = (
            (e[0:8], half // 2),
            (e[0:8], 4 + half // 2),
            (e[8:16], jnp.where(half < 4, half // 2, 4 + half // 2)),
        )
        for t, (part, index) in enumerate(pieces):
            fine = widen(take_rows(part, index), 8)
            tile = slice(8 * t, 8 * t + 8)
            v[r, tile] = f[t] + jnp.where(me[r, tile] > 0.0, fine, 0.0)

    def one_face(r, carry):
        fa[r] = 0.5 * (me[r] + me[r + 1])
        return carry

    lax.fori_loop(0, 13, one_face, 0)
    last = iota((24, 1024), 1) == 1023

    def one(r, carry):
        here = me[r]
        fb[r] = 0.5 * (here + following(here, 0))
        fz[r] = jnp.where(last, 0.0, 0.5 * (here + following(here, 1)))
        return carry

    lax.fori_loop(1, 13, one, 0)
    sweep(v, u, de, me, fa, fb, fz, w, (1, 13))
    sweep(u, v, de, me, fa, fb, fz, w, (2, 12))
    out[...] = v[3:11, 0:16]

    def final(r, carry):
        res[r] = residual_row(v, de, me, fa, fb, fz, r + 3)[0:16]
        return carry

    lax.fori_loop(0, 8, final, 0)


def shifted(x, step):
    zero = jnp.zeros((1,) + x.shape[1:], F32)
    return jnp.concatenate([x[1:], zero] if step > 0 else [zero, x[:-1]], axis=0)


class Whole:
    def __init__(self, c, cols, length):
        b, z = iota(c.shape, 1), iota(c.shape, 2)
        valid = (b < cols) & (z < length)
        self.fa = 0.5 * (c + shifted(c, 1))
        self.fa_below = 0.5 * (c + shifted(c, -1))
        self.fb = jnp.where(b < cols - 1, 0.5 * (c + following(c, 1)), 0.0)
        self.fz = jnp.where(z < length - 1, 0.5 * (c + following(c, 2)), 0.0)
        half = 0.5 * c
        self.ends = jnp.where(b == 0, half, 0.0) + jnp.where(b == cols - 1, half, 0.0)
        self.ends = self.ends + jnp.where(z == 0, half, 0.0) + jnp.where(z == length - 1, half, 0.0)
        diagonal = self.fa + self.fa_below + self.fb + preceding(self.fb, 1)
        diagonal = diagonal + self.fz + preceding(self.fz, 2) + self.ends
        self.w = jnp.where(valid, OMEGA / diagonal, 0.0)

    def operator(self, v):
        gb = self.fb * (following(v, 1) - v)
        gz = self.fz * (following(v, 2) - v)
        out = self.fa * (v - shifted(v, 1)) + self.fa_below * (v - shifted(v, -1)) + self.ends * v
        return out + (preceding(gb, 1) - gb) + (preceding(gz, 2) - gz)

    def sweep(self, v, s):
        return v + self.w * (s - self.operator(v))


def coarsen_whole(x):
    return jnp.stack([coarse_sum(x[a], x[a + 1]) for a in range(0, x.shape[0], 2)])


def refine_row(x, cols_tiles, blocks):
    half = iota((8, 128), 0)
    tiles = []
    for t in range(cols_tiles):
        source = x[8 * (t // 2) : 8 * (t // 2) + 8]
        tiles.append(widen(take_rows(source, half // 2 + 4 * (t % 2)), blocks))
    return tiles[0] if cols_tiles == 1 else jnp.concatenate(tiles, axis=0)


def refine_whole(x, cols_tiles):
    rows = [refine_row(x[a], cols_tiles, 1) for a in range(x.shape[0])]
    return jnp.stack([rows[a // 2] for a in range(2 * x.shape[0])])


def multiply(x, y):
    out = [[None] * 4 for _ in range(4)]
    for i in range(4):
        for j in range(4):
            for k in range(4):
                if x[i][k] is not None and y[k][j] is not None:
                    term = x[i][k] * y[k][j]
                    out[i][j] = term if out[i][j] is None else out[i][j] + term
    return out


def apply(x, y):
    out = []
    for i in range(4):
        total = None
        for k in range(4):
            if x[i][k] is not None:
                term = x[i][k] * y[k]
                total = term if total is None else total + term
        out.append(total)
    return out


def inverse(x):
    x = [[jnp.zeros((8, 128), F32) if e is None else e for e in line] for line in x]
    for k in range(4):
        pivot = 1.0 / x[k][k]
        line = [pivot if j == k else x[k][j] * pivot for j in range(4)]
        for i in range(4):
            if i != k:
                factor = x[i][k]
                x[i] = [-factor * pivot if j == k else x[i][j] - factor * line[j] for j in range(4)]
        x[k] = line
    return x


def each(x, move):
    return [[None if e is None else move(e) for e in line] for line in x]


def exact(s, c):
    length = 16
    lane = iota((8, 128), 1)
    row = iota((8, 128), 0)
    valid = lane < length

    def line(x, a, b):
        picked = jnp.take_along_axis(x[a], jnp.full((8, 128), b, jnp.int32), axis=0)
        return jnp.where(valid, picked, 0.0)

    cs = [line(c, k // 2, k % 2) for k in range(4)]
    rhs = [line(s, k // 2, k % 2) for k in range(4)]
    below = [[None] * 4 for _ in range(4)]
    above = [[None] * 4 for _ in range(4)]
    centre = [[None] * 4 for _ in range(4)]
    for k in range(4):
        here = cs[k]
        upper = 0.5 * (here + following(here, 1))
        lower = 0.5 * (here + preceding(here, 1))
        fa, fb = 0.5 * (here + cs[k ^ 2]), 0.5 * (here + cs[k ^ 1])
        diagonal = upper + lower + fa + fb + here
        centre[k][k] = jnp.where(valid, diagonal, 1.0)
        centre[k][k ^ 2], centre[k][k ^ 1] = -fa, -fb
        above[k][k] = jnp.where(lane < length - 1, -upper, 0.0)
        below[k][k] = jnp.where((lane > 0) & valid, -lower, 0.0)
    step = 1
    while step < length:
        ahead = lambda e, step=step: pltpu.roll(e, 128 - step, 1)
        behind = lambda e, step=step: pltpu.roll(e, step, 1)
        solved = inverse(centre)
        t, u, q = multiply(solved, below), multiply(solved, above), apply(solved, rhs)
        t_ahead, u_behind = each(t, ahead), each(u, behind)
        x, y = multiply(below, u_behind), multiply(above, t_ahead)
        centre = [
            [jnp.zeros((8, 128), F32) if centre[i][j] is None else centre[i][j] for j in range(4)]
            for i in range(4)
        ]
        centre = [[centre[i][j] - x[i][j] - y[i][j] for j in range(4)] for i in range(4)]
        x, y = apply(below, [behind(e) for e in q]), apply(above, [ahead(e) for e in q])
        rhs = [rhs[i] - x[i] - y[i] for i in range(4)]
        if 2 * step < length:
            below = each(multiply(below, each(t, behind)), lambda e: -e)
            above = each(multiply(above, each(u, ahead)), lambda e: -e)
        step *= 2
    solved = [jnp.where(valid, e, 0.0) for e in apply(inverse(centre), rhs)]
    return jnp.stack(
        [
            jnp.where(row == 0, solved[2 * a], jnp.where(row == 1, solved[2 * a + 1], 0.0))
            for a in range(2)
        ]
    )


def descend(s, c, cols, length):
    if c.shape[0] == 2:
        return exact(s, c)
    level = Whole(c, cols, length)
    v = level.w * s
    v = level.sweep(v, s)
    r = s - level.operator(v)
    e = descend(0.5 * coarsen_whole(r), 0.125 * coarsen_whole(c), cols // 2, length // 2)
    v = v + refine_whole(e, c.shape[1] // 8)
    v = level.sweep(v, s)
    return level.sweep(v, s)


def coarse_levels(mine, other, e2, s, c, v, u, fa, fb, fz, w, ends):
    wide, narrow, core, _ = scalars()
    devices, strips = mine.shape[0], mine.shape[0] // 16
    rows, cols, length = 2 * (devices // strips), 8 * strips, 256
    edge = jnp.zeros((cols, length), F32)
    for x in (c, v, u):
        x[0], x[rows + 1] = edge, edge

    def load(k, carry):
        for y in range(strips):
            for i in range(2):
                x, z = mine[k * strips + y, i], other[k * strips + y, i]
                s[2 * k + i + 1, 8 * y : 8 * y + 8] = jnp.where(core == 0, x, z)
                c[2 * k + i + 1, 8 * y : 8 * y + 8] = jnp.where(core == 0, z, x)
        return carry

    lax.fori_loop(0, rows // 2, load, 0)
    b, z = iota((cols, length), 0), iota((cols, length), 1)

    def one_face(r, carry):
        fa[r] = 0.5 * (c[r] + c[r + 1])
        return carry

    lax.fori_loop(0, rows + 1, one_face, 0)

    def one(r, carry):
        here = c[r]
        half = 0.5 * here
        yb = jnp.where(b == cols - 1, 0.0, 0.5 * (here + following(here, 0)))
        yz = jnp.where(z == length - 1, 0.0, 0.5 * (here + following(here, 1)))
        e = jnp.where((b == 0) | (b == cols - 1), half, 0.0) + jnp.where((z == 0) | (z == length - 1), half, 0.0)
        diagonal = fa[r - 1] + fa[r] + (yb + preceding(yb, 0)) + (yz + preceding(yz, 1)) + e
        factor = OMEGA / diagonal
        fb[r], fz[r], ends[r], w[r] = yb, yz, e, factor
        u[r] = factor * s[r]
        return carry

    lax.fori_loop(1, rows + 1, one, 0)

    def operator(x, r):
        here = x[r]
        gb = fb[r] * (following(here, 0) - here)
        gz = fz[r] * (following(here, 1) - here)
        out = fa[r] * (here - x[r + 1]) + fa[r - 1] * (here - x[r - 1]) + ends[r] * here
        return out + (preceding(gb, 0) - gb) + (preceding(gz, 1) - gz)

    def smooth(source, target, lo, hi):
        def body(r, carry):
            target[r] = source[r] + w[r] * (s[r] - operator(source, r))
            return carry

        lax.fori_loop(lo, hi, body, 0)

    smooth(u, v, 1, rows + 1)
    def coarse(i, carry):
        r = 2 * i + 1
        x, y = s[r] - operator(v, r), s[r + 1] - operator(v, r + 1)
        u[i + 1, 0 : cols // 2, 0:128] = 0.5 * coarse_sum(x, y)
        u[i + 1, 0 : cols // 2, 128:256] = 0.125 * coarse_sum(c[r], c[r + 1])
        return carry

    lax.fori_loop(0, rows // 2, coarse, 0)
    s3 = u[1 : rows // 2 + 1, 0 : cols // 2, 0:128]
    c3 = u[1 : rows // 2 + 1, 0 : cols // 2, 128:256]
    e3 = descend(s3, c3, cols // 2, 128)
    u[1 : rows // 2 + 1, 0 : cols // 2, 0:128] = e3

    def refine(i, carry):
        e = refine_row(u[i + 1, 0 : cols // 2, 0:128], cols // 8, 2)
        v[2 * i + 1] = v[2 * i + 1] + e
        v[2 * i + 2] = v[2 * i + 2] + e
        return carry

    lax.fori_loop(0, rows // 2, refine, 0)
    smooth(v, u, 1, rows + 1)
    smooth(u, v, 1, rows + 1)
    for i in range(6):
        r = lax.rem(2 * wide - 2 + i + rows, rows)
        moved = pltpu.roll(v[r + 1], lax.rem(cols + 2 - 4 * narrow, cols), 0)
        e2[i] = moved[0:8]


def moved(x, wide_step, narrow_step):
    w, y, k = [lax.axis_size(name) for name in AX]
    n = y * k
    pairs = [
        (i * n + j, ((i + wide_step) % w) * n + (j + narrow_step) % n)
        for i in range(w)
        for j in range(n)
    ]
    return lax.ppermute(x, AX, pairs)


def other_core(x):
    w, y, k = [lax.axis_size(name) for name in AX]
    return lax.ppermute(x, AX, [(i, i ^ 1) for i in range(w * y * k)])


def per_device(p, d, m):
    up = jnp.concatenate([p[5:8], m[5:8], d[6:8]], axis=0)
    down = jnp.concatenate([p[0:3], m[0:3], d[0:2]], axis=0)
    left, right = moved(up, 1, 0), moved(down, -1, 0)
    to_left, to_right = call(pack_zero, [(14, 8, 1024)] * 2, [], p, d, m, left, right)
    nleft, nright = moved(to_right, 0, 1), moved(to_left, 0, -1)
    big = (14, 24, 1024)
    f0, me, de, s1, c1, up, down, w0 = call(
        lambda *refs: level_zero(*refs[:14], *refs[15:], refs[14]),
        [(8, 16, 1024), big, big, (4, 8, 512), (4, 8, 512), (7, 8, 512), (7, 8, 512), big],
        [big] * 5,
        p, d, m, left, right, nleft, nright,
        flops=30_000_000,
    )
    left1, right1 = moved(up, 1, 0), moved(down, -1, 0)
    to_left, to_right = call(pack_one, [(12, 8, 512)] * 2, [], s1, c1, left1, right1)
    nleft1, nright1 = moved(to_right, 0, 1), moved(to_left, 0, -1)
    mid = (12, 16, 512)
    se, ce, f1, send, keep, up, down = call(
        level_one,
        [mid, mid, (4, 8, 512), (2, 8, 256), (2, 8, 256), (8, 8, 1024), (8, 8, 1024)],
        [mid] * 6,
        s1, c1, left1, right1, nleft1, nright1, f0,
        flops=10_000_000,
    )
    hleft, hright = moved(up, 1, 0), moved(down, -1, 0)
    pair = keep + other_core(send)
    chips = lax.axis_size("wide") * lax.axis_size("ny")
    mine = lax.all_to_all(jnp.broadcast_to(pair[None], (chips,) + pair.shape), ("wide", "ny"), 0, 0, tiled=True)
    other = other_core(mine)
    to_left, to_right = call(pack_up, [(14, 8, 1024)] * 2, [], f0, f1, hleft, hright)
    nhleft, nhright = moved(to_right, 0, 1), moved(to_left, 0, -1)
    whole = (34, 32, 256)
    (e2,) = call(coarse_levels, [(6, 8, 256)], [whole] * 9, mine, other, flops=60_000_000)
    return call(
        level_up,
        [(8, 16, 1024)] * 2,
        [big] * 5 + [mid] * 6,
        me, de, w0, f0, hleft, hright, nhleft, nhright, se, ce, f1, e2,
        flops=30_000_000,
    )


def solution(mesh):
    wide, narrow = mesh.axis_names
    devices = mesh.devices.reshape(mesh.shape[wide], mesh.shape[narrow] // 2, 2)
    spec = P("wide", ("ny", "core"), None)
    return jax.shard_map(
        lambda p, d, m: tuple(per_device(p, d, m)),
        mesh=Mesh(devices, AX),
        in_specs=(spec,) * 3,
        out_specs=(spec,) * 2,
        check_vma=False,
    )
```

```python
import math

import jax
import jax.numpy as jnp
from jax import lax
from jax.experimental import pallas as pl
from jax.experimental.pallas import tpu as pltpu
from jax.sharding import Mesh, PartitionSpec as P

OMEGA = 0.8
AX = ("wide", "ny", "core")
F32 = jnp.float32
SPARE = 4 * 1024 * 1024


def iota(shape, dim):
    return lax.broadcasted_iota(jnp.int32, shape, dim)


def following(x, dim):
    return pltpu.roll(x, x.shape[dim] - 1, dim)


def preceding(x, dim):
    return pltpu.roll(x, 1, dim)


def lanes(x, r, k):
    return x[r, :, 128 * k : 128 * k + 128]


def row_operator(v, r, c, fa, fb, fz):
    count = v.shape[2] // 128
    lane = iota((v.shape[1], 128), 1)
    here = lanes(v, r, 0)
    turned = pltpu.roll(here, 127, 1)
    out = []
    for k in range(count):
        if k + 1 < count:
            later = lanes(v, r, k + 1)
            later_turned = pltpu.roll(later, 127, 1)
        else:
            later, later_turned = None, 0.0
        gz = lanes(fz, r, k) * (jnp.where(lane == 127, later_turned, turned) - here)
        gz_turned = pltpu.roll(gz, 1, 1)
        if k == 0:
            gz_before = 0.5 * lanes(c, r, 0) * here
        gb = lanes(fb, r, k) * (following(here, 0) - here)
        a = lanes(fa, r, k) * (here - lanes(v, r + 1, k)) + lanes(fa, r - 1, k) * (here - lanes(v, r - 1, k))
        a = a + (preceding(gb, 0) - gb) + (jnp.where(lane == 0, gz_before, gz_turned) - gz)
        out.append(a)
        here, turned, gz_before = later, later_turned, gz_turned
    return out


def row_faces(r, c, fa, fb, fz, w):
    count = c.shape[2] // 128
    cols = c.shape[1]
    lane = iota((cols, 128), 1)
    here = lanes(c, r, 0)
    turned = pltpu.roll(here, 127, 1)
    for k in range(count):
        if k + 1 < count:
            later = lanes(c, r, k + 1)
            later_turned = pltpu.roll(later, 127, 1)
        else:
            later, later_turned = None, 0.0
        at = slice(128 * k, 128 * k + 128)
        z = 0.5 * (here + jnp.where(lane == 127, later_turned, turned))
        z_turned = pltpu.roll(z, 1, 1)
        if k == 0:
            z_before = 0.5 * here
        y = 0.5 * (here + following(here, 0))
        diagonal = 0.5 * (here + lanes(c, r - 1, k)) + 0.5 * (here + lanes(c, r + 1, k))
        diagonal = diagonal + (y + preceding(y, 0)) + (z + jnp.where(lane == 0, z_before, z_turned))
        fa[r, :, at] = 0.5 * (here + lanes(c, r + 1, k))
        fb[r, :, at], fz[r, :, at] = y, z
        w[r, :, at] = jnp.where(here > 0.0, OMEGA / diagonal, 0.0)
        here, turned, z_before = later, later_turned, z_turned


def over_rows(lo, hi, step, body):
    whole = (hi - lo) // step

    def some(i, carry):
        for j in range(step):
            body(lo + i * step + j)
        return carry

    if whole > 1:
        lax.fori_loop(0, whole, some, 0)
        lo = lo + whole * step
    for r in range(lo, hi):
        body(r)


def half_compress(low, high, dim):
    length = low.shape[dim]
    at = iota(low.shape, dim)
    index = (2 * at) % length
    first = jnp.take_along_axis(low, index, axis=dim)
    if high is None:
        return jnp.where(at < length // 2, first, 0.0)
    return jnp.where(at < length // 2, first, jnp.take_along_axis(high, index, axis=dim))


def half_columns(x):
    x = x + following(x, 0)
    tiles = x.shape[0] // 8
    part = lambda t: x[8 * t : 8 * t + 8]
    if tiles == 1:
        return half_compress(x, None, 0)
    x = [half_compress(part(2 * t), part(2 * t + 1), 0) for t in range(tiles // 2)]
    return x[0] if len(x) == 1 else jnp.concatenate(x, axis=0)


def coarse_sum(first, second, split=False):
    halves = [half_columns(x + y) for x, y in zip(first, second)]
    halves = [x + following(x, 1) for x in halves]
    if split:
        lane = iota((8, 128), 1)
        out = []
        for odd in range(2):
            index = (4 * lane + 2 * odd) % 128
            picked = jnp.take_along_axis(halves[0], index, axis=1)
            for k in range(1, 4):
                picked = jnp.where(lane >= 32 * k, jnp.take_along_axis(halves[k], index, axis=1), picked)
            out.append(picked)
        return out
    if len(halves) == 1:
        return [by_tile(halves[0], None)]
    return [by_tile(halves[k], halves[k + 1]) for k in range(0, len(halves), 2)]


def by_tile(low, high):
    tiles = [
        half_compress(low[8 * t : 8 * t + 8], None if high is None else high[8 * t : 8 * t + 8], 1)
        for t in range(low.shape[0] // 8)
    ]
    return tiles[0] if len(tiles) == 1 else jnp.concatenate(tiles, axis=0)


def blocks_of(x):
    return [x[:, 128 * k : 128 * k + 128] for k in range(x.shape[1] // 128)]


def repeat_lanes(x, block):
    source = block // 2
    index = iota((8, 128), 1) // 2 + 64 * (block % 2)
    return jnp.take_along_axis(x[:, 128 * source : 128 * source + 128], index, axis=1)


def take_rows(x, index):
    pieces = [
        jnp.take_along_axis(x[:, k : k + 128], index, axis=0) for k in range(0, x.shape[1], 128)
    ]
    return pieces[0] if len(pieces) == 1 else jnp.concatenate(pieces, axis=1)


def widen(x, blocks):
    pieces = [repeat_lanes(x, k) for k in range(blocks)]
    return pieces[0] if len(pieces) == 1 else jnp.concatenate(pieces, axis=1)


def widen_split(x):
    lane = iota((8, 128), 1)
    pieces = []
    for k in range(4):
        index = 32 * k + lane // 4
        even = jnp.take_along_axis(x[:, :128], index, axis=1)
        odd = jnp.take_along_axis(x[:, 128:], index, axis=1)
        pieces.append(jnp.where(lane // 2 % 2 == 0, even, odd))
    return jnp.concatenate(pieces, axis=1)


def scalars():
    wide, ny, core = lax.axis_index("wide"), lax.axis_index("ny"), lax.axis_index("core")
    sizes = [lax.axis_size(name) for name in AX]
    narrow = ny * sizes[2] + core
    inside = [
        jnp.where(flag, 1.0, 0.0).astype(F32)
        for flag in (wide > 0, wide < sizes[0] - 1, narrow > 0, narrow < sizes[1] * sizes[2] - 1)
    ]
    return wide, narrow, core, inside


def call(kernel, outs, scratch, *args, flops=1_000_000):
    vmem = pl.BlockSpec(memory_space=pltpu.VMEM)
    size = 4 * sum(a.size for a in args)
    held = size + 4 * sum(math.prod(s) for s in outs + scratch)
    return pl.pallas_call(
        kernel,
        out_shape=[jax.ShapeDtypeStruct(s, F32) for s in outs],
        in_specs=[vmem] * len(args),
        out_specs=[vmem] * len(outs),
        scratch_shapes=[pltpu.VMEM(s, F32) for s in scratch],
        compiler_params=pltpu.CompilerParams(vmem_limit_bytes=held + SPARE),
        cost_estimate=pl.CostEstimate(flops=flops, bytes_accessed=0 if flops == 1000 else size, transcendentals=0),
    )(*args)


def pack_zero(p, d, m, left, right, to_left, to_right):
    _, _, _, (low, high, _, _) = scalars()
    at = iota((8, 1024), 0)
    for r in range(14):
        a = r - 3
        for side, out in ((0, to_left), (1, to_right)):
            tile = slice(8 * side, 8 * side + 8)
            if a < 0:
                vp, vm = left[r, tile] * low, left[3 + r, tile] * low
                vd = left[5 + r, tile] * low if r > 0 else jnp.zeros_like(vp)
            elif a < 8:
                vp, vm, vd = p[a, tile], m[a, tile], d[a, tile]
            else:
                vp, vm = right[a - 8, tile] * high, right[a - 5, tile] * high
                vd = right[a - 2, tile] * high if a < 10 else jnp.zeros_like(vp)
            if side == 0:
                vm, vd = pltpu.roll(vm, 3, 0), pltpu.roll(vd, 6, 0)
                out[r] = jnp.where(at < 3, vp, jnp.where(at < 6, vm, vd))
            else:
                vm, vd = pltpu.roll(vm, 5, 0), pltpu.roll(vd, 2, 0)
                out[r] = jnp.where(at >= 5, vp, jnp.where(at >= 2, vm, vd))


def faces(c, rows, fa, fb, fz, w, step):
    for k in range(c.shape[2] // 128):
        at = slice(128 * k, 128 * k + 128)
        fa[rows[0] - 1, :, at] = 0.5 * (c[rows[0] - 1, :, at] + c[rows[0], :, at])
    over_rows(rows[0], rows[1], step, lambda r: row_faces(r, c, fa, fb, fz, w))


def sweep(source, target, s, c, fa, fb, fz, w, rows, step):
    def one(r):
        for k, a in enumerate(row_operator(source, r, c, fa, fb, fz)):
            at = slice(128 * k, 128 * k + 128)
            target[r, :, at] = source[r, :, at] + w[r, :, at] * (s[r, :, at] - a)

    over_rows(rows[0], rows[1], step, one)


def residual_row(v, s, c, fa, fb, fz, r, cols):
    return [
        (lanes(s, r, k) - a)[0:cols]
        for k, a in enumerate(row_operator(v, r, c, fa, fb, fz))
    ]


def level_zero(p, d, m, left, right, nleft, nright, field, s1, c1, up, down, me, de, w, fa, fb, fz, v, u):
    _, _, _, (low, high, nlow, nhigh) = scalars()
    at = iota((8, 1024), 0)
    for r in range(14):
        a = r - 3
        if a < 0:
            v[r, 0:16], me[r, 0:16] = left[r] * low, left[3 + r] * low
            de[r, 0:16] = left[5 + r] * low if r > 0 else jnp.zeros((16, 1024), F32)
        elif a < 8:
            v[r, 0:16], me[r, 0:16], de[r, 0:16] = p[a], m[a], d[a]
        else:
            v[r, 0:16], me[r, 0:16] = right[a - 8] * high, right[a - 5] * high
            de[r, 0:16] = right[a - 2] * high if a < 10 else jnp.zeros((16, 1024), F32)
        x, y = nright[r] * nhigh, nleft[r] * nlow
        v[r, 16:24] = jnp.where(at < 3, x, jnp.where(at >= 5, y, 0.0))
        x3, y3 = pltpu.roll(x, 5, 0), pltpu.roll(y, 3, 0)
        me[r, 16:24] = jnp.where(at < 3, x3, jnp.where(at >= 5, y3, 0.0))
        x6, y6 = pltpu.roll(x, 2, 0), pltpu.roll(y, 6, 0)
        de[r, 16:24] = jnp.where(at < 2, x6, jnp.where(at >= 6, y6, 0.0))
    faces(me, (1, 13), fa, fb, fz, w, 2)
    u[0], u[13] = v[0], v[13]
    sweep(v, u, de, me, fa, fb, fz, w, (1, 13), 2)
    sweep(u, v, de, me, fa, fb, fz, w, (2, 12), 2)
    field[...] = v[3:11, 0:16]

    def coarse(i, carry):
        r = 2 * i + 3
        x = residual_row(v, de, me, fa, fb, fz, r, 16)
        y = residual_row(v, de, me, fa, fb, fz, r + 1, 16)
        mx, my = blocks_of(me[r, 0:16]), blocks_of(me[r + 1, 0:16])
        for k, (a, b) in enumerate(zip(coarse_sum(x, y), coarse_sum(mx, my))):
            s1[i, :, 128 * k : 128 * k + 128] = 0.5 * a
            c1[i, :, 128 * k : 128 * k + 128] = 0.125 * b
        return carry

    lax.fori_loop(0, 4, coarse, 0)
    up[0:3], down[0:3] = s1[1:4], s1[0:3]
    up[3:7], down[3:7] = c1[...], c1[...]


def pack_one(s, c, left, right, to_left, to_right):
    _, _, _, (low, high, _, _) = scalars()
    at = iota((8, 512), 0)
    for r in range(12):
        a = r - 4
        if a < 0:
            vc = left[3 + r] * low
            vs = left[r - 1] * low if r > 0 else jnp.zeros_like(vc)
        elif a < 4:
            vs, vc = s[a], c[a]
        else:
            vc = right[a - 1] * high
            vs = right[a - 4] * high if a < 7 else jnp.zeros_like(vc)
        to_left[r] = jnp.where(at < 4, vc, pltpu.roll(vs, 4, 0))
        to_right[r] = jnp.where(at >= 4, vc, pltpu.roll(vs, 4, 0))


def level_one(s, c, left, right, nleft, nright, f0, se, ce, field, send, keep, up, down, v, u, fa, fb, fz, w):
    _, _, core, (low, high, nlow, nhigh) = scalars()
    at = iota((8, 512), 0)
    for r in range(12):
        a = r - 4
        if a < 0:
            ce[r, 0:8] = left[3 + r] * low
            se[r, 0:8] = left[r - 1] * low if r > 0 else jnp.zeros((8, 512), F32)
        elif a < 4:
            se[r, 0:8], ce[r, 0:8] = s[a], c[a]
        else:
            ce[r, 0:8] = right[a - 1] * high
            se[r, 0:8] = right[a - 4] * high if a < 7 else jnp.zeros((8, 512), F32)
        x, y = nright[r] * nhigh, nleft[r] * nlow
        ce[r, 8:16] = jnp.where(at < 4, x, y)
        se[r, 8:16] = jnp.where(at < 4, pltpu.roll(x, 4, 0), pltpu.roll(y, 4, 0))
    faces(ce, (2, 10), fa, fb, fz, w, 4)

    for r in range(2, 10):
        u[r] = w[r] * se[r]
    sweep(u, v, se, ce, fa, fb, fz, w, (3, 9), 3)
    field[...] = v[4:8, 0:8]
    rows = iota((8, 256), 0)
    index = iota((8, 256), 0) % 4
    mine = rows // 4 == core
    for i in range(2):
        r = 2 * i + 4
        x = residual_row(v, se, ce, fa, fb, fz, r, 8)
        y = residual_row(v, se, ce, fa, fb, fz, r + 1, 8)
        mx, my = blocks_of(ce[r, 0:8]), blocks_of(ce[r + 1, 0:8])
        s2 = 0.5 * jnp.concatenate(coarse_sum(x, y, True), axis=1)
        c2 = 0.125 * jnp.concatenate(coarse_sum(mx, my, True), axis=1)
        s2 = jnp.where(mine, take_rows(s2, index[:, :128]), 0.0)
        c2 = jnp.where(mine, take_rows(c2, index[:, :128]), 0.0)
        send[i] = jnp.where(core == 0, c2, s2)
        keep[i] = jnp.where(core == 0, s2, c2)
    for r in range(3):
        for t in range(2):
            up[2 * r + t] = f0[5 + r, 8 * t : 8 * t + 8]
            down[2 * r + t] = f0[r, 8 * t : 8 * t + 8]
    for r in range(2):
        both = jnp.concatenate([field[2 * r], field[2 * r + 1]], axis=1)
        up[6 + r] = both
        down[6 + r] = both


def pack_up(f0, f1, left, right, to_left, to_right):
    _, _, _, (low, high, _, _) = scalars()
    at = iota((8, 1024), 0)
    for r in range(14):
        for side, out in ((0, to_left), (1, to_right)):
            tile = slice(8 * side, 8 * side + 8)
            if r < 3:
                x = left[2 * r + side] * low
            elif r < 11:
                x = f0[r - 3, tile]
            else:
                x = right[2 * (r - 11) + side] * high
            if r < 2:
                y = left[6 + r] * low
            elif r < 4:
                y = jnp.concatenate([f1[2 * r - 4], f1[2 * r - 3]], axis=1)
            elif r < 6:
                y = right[2 + r] * high
            else:
                y = None
            if y is not None:
                y = pltpu.roll(y, 4, 0)
                x = jnp.where(at < 4, x, y) if side == 0 else jnp.where(at >= 4, x, y)
            out[r] = x


def level_up(me, de, w, fa, fb, fz, f0, left, right, nleft, nright, se, ce, f1, e2, out, res, v, u, v1, u1, fa1, fb1, fz1, w1):
    _, _, _, (low, high, nlow, nhigh) = scalars()
    at = iota((8, 512), 0)
    half = iota((8, 128), 0)
    for r in range(12):
        if r < 4:
            f = left[6 + r // 2][:, 512 * (r % 2) : 512 * (r % 2) + 512] * low
        elif r < 8:
            f = f1[r - 4]
        else:
            f = right[2 + r // 2][:, 512 * (r % 2) : 512 * (r % 2) + 512] * high
        x = nright[r // 2][:, 512 * (r % 2) : 512 * (r % 2) + 512] * nhigh
        y = nleft[r // 2][:, 512 * (r % 2) : 512 * (r % 2) + 512] * nlow
        g = jnp.where(at < 4, pltpu.roll(x, 4, 0), pltpu.roll(y, 4, 0))
        e = e2[r // 2]
        own = widen_split(take_rows(e, 2 + half // 2))
        beside = widen_split(take_rows(e, jnp.where(half < 4, 6 + half // 2, (half - 4) // 2)))
        v1[r, 0:8] = f + jnp.where(ce[r, 0:8] > 0.0, own, 0.0)
        v1[r, 8:16] = g + jnp.where(ce[r, 8:16] > 0.0, beside, 0.0)
    faces(ce, (1, 11), fa1, fb1, fz1, w1, 5)
    sweep(v1, u1, se, ce, fa1, fb1, fz1, w1, (1, 11), 5)
    sweep(u1, v1, se, ce, fa1, fb1, fz1, w1, (2, 10), 4)
    zero = iota((8, 1024), 0)
    for r in range(14):
        if r < 3:
            f = [left[2 * r] * low, left[2 * r + 1] * low]
        elif r < 11:
            f = [f0[r - 3, 0:8], f0[r - 3, 8:16]]
        else:
            f = [right[2 * (r - 11)] * high, right[2 * (r - 11) + 1] * high]
        x, y = nright[r] * nhigh, nleft[r] * nlow
        f.append(jnp.where(zero < 3, x, jnp.where(zero >= 5, y, 0.0)))
        e = v1[(r + 5) // 2]
        pieces = (
            (e[0:8], half // 2),
            (e[0:8], 4 + half // 2),
            (e[8:16], jnp.where(half < 4, half // 2, 4 + half // 2)),
        )
        for t, (part, index) in enumerate(pieces):
            fine = widen(take_rows(part, index), 8)
            tile = slice(8 * t, 8 * t + 8)
            v[r, tile] = f[t] + jnp.where(me[r, tile] > 0.0, fine, 0.0)

    sweep(v, u, de, me, fa, fb, fz, w, (1, 13), 2)
    sweep(u, v, de, me, fa, fb, fz, w, (2, 12), 2)
    out[...] = v[3:11, 0:16]

    def final(r):
        for k, x in enumerate(residual_row(v, de, me, fa, fb, fz, r, 16)):
            res[r - 3, :, 128 * k : 128 * k + 128] = x

    over_rows(3, 11, 2, final)


def shifted(x, step):
    zero = jnp.zeros((1,) + x.shape[1:], F32)
    return jnp.concatenate([x[1:], zero] if step > 0 else [zero, x[:-1]], axis=0)


class Whole:
    def __init__(self, c, cols, length):
        b, z = iota(c.shape, 1), iota(c.shape, 2)
        valid = (b < cols) & (z < length)
        self.fa = 0.5 * (c + shifted(c, 1))
        self.fa_below = 0.5 * (c + shifted(c, -1))
        self.fb = jnp.where(b < cols - 1, 0.5 * (c + following(c, 1)), 0.0)
        self.fz = jnp.where(z < length - 1, 0.5 * (c + following(c, 2)), 0.0)
        half = 0.5 * c
        self.ends = jnp.where(b == 0, half, 0.0) + jnp.where(b == cols - 1, half, 0.0)
        self.ends = self.ends + jnp.where(z == 0, half, 0.0) + jnp.where(z == length - 1, half, 0.0)
        diagonal = self.fa + self.fa_below + self.fb + preceding(self.fb, 1)
        diagonal = diagonal + self.fz + preceding(self.fz, 2) + self.ends
        self.w = jnp.where(valid, OMEGA / diagonal, 0.0)

    def operator(self, v):
        gb = self.fb * (following(v, 1) - v)
        gz = self.fz * (following(v, 2) - v)
        out = self.fa * (v - shifted(v, 1)) + self.fa_below * (v - shifted(v, -1)) + self.ends * v
        return out + (preceding(gb, 1) - gb) + (preceding(gz, 2) - gz)

    def sweep(self, v, s):
        return v + self.w * (s - self.operator(v))


def coarsen_whole(x):
    return jnp.stack([coarse_sum([x[a]], [x[a + 1]])[0] for a in range(0, x.shape[0], 2)])


def refine_row(x, cols_tiles, lanes_too):
    half = iota((8, 128), 0)
    tiles = []
    for t in range(cols_tiles):
        source = x[8 * (t // 2) : 8 * (t // 2) + 8]
        tile = take_rows(source, half // 2 + 4 * (t % 2))
        tiles.append(widen(tile, 1) if lanes_too else tile)
    return tiles[0] if cols_tiles == 1 else jnp.concatenate(tiles, axis=0)


def refine_whole(x, cols_tiles):
    rows = [refine_row(x[a], cols_tiles, True) for a in range(x.shape[0])]
    return jnp.stack([rows[a // 2] for a in range(2 * x.shape[0])])


def multiply(x, y):
    out = [[None] * 4 for _ in range(4)]
    for i in range(4):
        for j in range(4):
            for k in range(4):
                if x[i][k] is not None and y[k][j] is not None:
                    term = x[i][k] * y[k][j]
                    out[i][j] = term if out[i][j] is None else out[i][j] + term
    return out


def apply(x, y):
    out = []
    for i in range(4):
        total = None
        for k in range(4):
            if x[i][k] is not None:
                term = x[i][k] * y[k]
                total = term if total is None else total + term
        out.append(total)
    return out


def inverse(x):
    x = [[jnp.zeros((8, 128), F32) if e is None else e for e in line] for line in x]
    for k in range(4):
        pivot = 1.0 / x[k][k]
        line = [pivot if j == k else x[k][j] * pivot for j in range(4)]
        for i in range(4):
            if i != k:
                factor = x[i][k]
                x[i] = [-factor * pivot if j == k else x[i][j] - factor * line[j] for j in range(4)]
        x[k] = line
    return x


def each(x, move):
    return [[None if e is None else move(e) for e in line] for line in x]


def exact(s, c):
    length = 16
    lane = iota((8, 128), 1)
    row = iota((8, 128), 0)
    valid = lane < length

    def line(x, a, b):
        picked = jnp.take_along_axis(x[a], jnp.full((8, 128), b, jnp.int32), axis=0)
        return jnp.where(valid, picked, 0.0)

    cs = [line(c, k // 2, k % 2) for k in range(4)]
    rhs = [line(s, k // 2, k % 2) for k in range(4)]
    below = [[None] * 4 for _ in range(4)]
    above = [[None] * 4 for _ in range(4)]
    centre = [[None] * 4 for _ in range(4)]
    for k in range(4):
        here = cs[k]
        upper = 0.5 * (here + following(here, 1))
        lower = 0.5 * (here + preceding(here, 1))
        fa, fb = 0.5 * (here + cs[k ^ 2]), 0.5 * (here + cs[k ^ 1])
        diagonal = upper + lower + fa + fb + here
        centre[k][k] = jnp.where(valid, diagonal, 1.0)
        centre[k][k ^ 2], centre[k][k ^ 1] = -fa, -fb
        above[k][k] = jnp.where(lane < length - 1, -upper, 0.0)
        below[k][k] = jnp.where((lane > 0) & valid, -lower, 0.0)
    step = 1
    while step < length:
        ahead = lambda e, step=step: pltpu.roll(e, 128 - step, 1)
        behind = lambda e, step=step: pltpu.roll(e, step, 1)
        solved = inverse(centre)
        t, u, q = multiply(solved, below), multiply(solved, above), apply(solved, rhs)
        t_ahead, u_behind = each(t, ahead), each(u, behind)
        x, y = multiply(below, u_behind), multiply(above, t_ahead)
        centre = [
            [jnp.zeros((8, 128), F32) if centre[i][j] is None else centre[i][j] for j in range(4)]
            for i in range(4)
        ]
        centre = [[centre[i][j] - x[i][j] - y[i][j] for j in range(4)] for i in range(4)]
        x, y = apply(below, [behind(e) for e in q]), apply(above, [ahead(e) for e in q])
        rhs = [rhs[i] - x[i] - y[i] for i in range(4)]
        if 2 * step < length:
            below = each(multiply(below, each(t, behind)), lambda e: -e)
            above = each(multiply(above, each(u, ahead)), lambda e: -e)
        step *= 2
    solved = [jnp.where(valid, e, 0.0) for e in apply(inverse(centre), rhs)]
    return jnp.stack(
        [
            jnp.where(row == 0, solved[2 * a], jnp.where(row == 1, solved[2 * a + 1], 0.0))
            for a in range(2)
        ]
    )


def descend(s, c, cols, length):
    if c.shape[0] == 2:
        return exact(s, c)
    level = Whole(c, cols, length)
    v = level.w * s
    v = level.sweep(v, s)
    r = s - level.operator(v)
    e = descend(0.5 * coarsen_whole(r), 0.125 * coarsen_whole(c), cols // 2, length // 2)
    v = v + refine_whole(e, c.shape[1] // 8)
    v = level.sweep(v, s)
    return level.sweep(v, s)


def split_before(last, first_lane):
    lane = iota(last.shape, 1)
    return jnp.where(lane == 0, first_lane, pltpu.roll(last, 1, 1))


def split_after(first):
    lane = iota(first.shape, 1)
    return jnp.where(lane == 127, 0.0, pltpu.roll(first, 127, 1))


def split_operator(v, r, c, fa, fb, fz, ends):
    here = [lanes(v, r, k) for k in range(2)]
    after = [here[1], split_after(here[0])]
    gz = [lanes(fz, r, k) * (after[k] - here[k]) for k in range(2)]
    before = [split_before(gz[1], 0.5 * lanes(c, r, 0) * here[0]), gz[0]]
    out = []
    for k in range(2):
        gb = lanes(fb, r, k) * (following(here[k], 0) - here[k])
        a = lanes(fa, r, k) * (here[k] - lanes(v, r + 1, k)) + lanes(fa, r - 1, k) * (here[k] - lanes(v, r - 1, k))
        a = a + lanes(ends, r, k) * here[k]
        out.append(a + (preceding(gb, 0) - gb) + (before[k] - gz[k]))
    return out


def split_sweep(source, target, s, c, fa, fb, fz, ends, w, r):
    for k, a in enumerate(split_operator(source, r, c, fa, fb, fz, ends)):
        at = slice(128 * k, 128 * k + 128)
        target[r, :, at] = source[r, :, at] + w[r, :, at] * (s[r, :, at] - a)


def level_two(mine, other, s, c, v, fa, fb, fz, ends, w, s3, c3, u):
    _, _, core, _ = scalars()
    strips = mine.shape[0] // 16
    rows, cols = 32, 8 * strips
    edge = jnp.zeros((cols, 256), F32)
    for x in (c, v, u):
        x[0], x[rows + 1] = edge, edge

    def load(k):
        for y in range(strips):
            for i in range(2):
                x, z = mine[k * strips + y, i], other[k * strips + y, i]
                s[2 * k + i + 1, 8 * y : 8 * y + 8] = jnp.where(core == 0, x, z)
                c[2 * k + i + 1, 8 * y : 8 * y + 8] = jnp.where(core == 0, z, x)

    over_rows(0, rows // 2, 2, load)
    fa[0] = 0.5 * c[1]
    b = iota((cols, 128), 0)

    def one(r):
        here = [lanes(c, r, k) for k in range(2)]
        z = [0.5 * (here[0] + here[1]), 0.5 * (here[1] + split_after(here[0]))]
        before = [split_before(z[1], 0.5 * here[0]), z[0]]
        for k in range(2):
            at = slice(128 * k, 128 * k + 128)
            x, h = here[k], 0.5 * here[k]
            y = jnp.where(b == cols - 1, 0.0, 0.5 * (x + following(x, 0)))
            e = jnp.where((b == 0) | (b == cols - 1), h, 0.0)
            above = h + 0.5 * lanes(c, r + 1, k)
            diagonal = above + (h + 0.5 * lanes(c, r - 1, k)) + (y + preceding(y, 0)) + (z[k] + before[k]) + e
            factor = OMEGA / diagonal
            fa[r, :, at], fb[r, :, at], fz[r, :, at] = above, y, z[k]
            ends[r, :, at], w[r, :, at] = e, factor
            u[r, :, at] = factor * s[r, :, at]

    over_rows(1, rows + 1, 4, one)
    over_rows(1, rows + 1, 4, lambda r: split_sweep(u, v, s, c, fa, fb, fz, ends, w, r))

    def coarse(i):
        total = None
        for r in (2 * i + 1, 2 * i + 2):
            for k, a in enumerate(split_operator(v, r, c, fa, fb, fz, ends)):
                x = lanes(s, r, k) - a
                total = x if total is None else total + x
        s3[i] = 0.5 * half_columns(total)
        total = (lanes(c, 2 * i + 1, 0) + lanes(c, 2 * i + 1, 1)) + (lanes(c, 2 * i + 2, 0) + lanes(c, 2 * i + 2, 1))
        c3[i] = 0.125 * half_columns(total)

    over_rows(0, rows // 2, 2, coarse)


def coarse_levels(s3, c3, s, c, v, fa, fb, fz, ends, w, e2, e3, u, t):
    wide, narrow, _, _ = scalars()
    rows, cols = s.shape[0] - 2, s.shape[1]
    e3[...] = descend(s3[...], c3[...], cols // 2, 128)
    row = lambda step: jnp.clip(2 * wide + step, 0, rows - 1) + 1
    u[0], u[rows + 1], t[0], t[rows + 1] = v[0], v[0], v[0], v[0]
    for i in range(-2, 3):
        k = jnp.clip(wide + i, 0, rows // 2 - 1)
        e = refine_row(e3[k], cols // 8, False)
        for r in (2 * k + 1, 2 * k + 2):
            for half in range(2):
                at = slice(128 * half, 128 * half + 128)
                u[r, :, at] = v[r, :, at] + e
    for i in range(-3, 5):
        split_sweep(u, t, s, c, fa, fb, fz, ends, w, row(i))
    for i in range(-2, 4):
        split_sweep(t, u, s, c, fa, fb, fz, ends, w, row(i))
    for i in range(6):
        turned = pltpu.roll(u[row(i - 2)], lax.rem(cols + 2 - 4 * narrow, cols), 0)
        e2[i] = turned[0:8]


def moved(x, wide_step, narrow_step):
    w, y, k = [lax.axis_size(name) for name in AX]
    n = y * k
    pairs = [
        (i * n + j, ((i + wide_step) % w) * n + (j + narrow_step) % n)
        for i in range(w)
        for j in range(n)
    ]
    return lax.ppermute(x, AX, pairs)


def other_core(x):
    w, y, k = [lax.axis_size(name) for name in AX]
    return lax.ppermute(x, AX, [(i, i ^ 1) for i in range(w * y * k)])


def gathered(x):
    chips = lax.axis_size("wide") * lax.axis_size("ny")
    return lax.all_to_all(jnp.broadcast_to(x[None], (chips,) + x.shape), ("wide", "ny"), 0, 0, tiled=True)


def per_device(p, d, m):
    up = jnp.concatenate([p[5:8], m[5:8], d[6:8]], axis=0)
    down = jnp.concatenate([p[0:3], m[0:3], d[0:2]], axis=0)
    left, right = moved(up, 1, 0), moved(down, -1, 0)
    to_left, to_right = call(pack_zero, [(14, 8, 1024)] * 2, [], p, d, m, left, right)
    nleft, nright = moved(to_right, 0, 1), moved(to_left, 0, -1)
    big = (14, 24, 1024)
    f0, s1, c1, up, down, *zero = call(
        level_zero,
        [(8, 16, 1024), (4, 8, 512), (4, 8, 512), (7, 8, 512), (7, 8, 512)] + [big] * 6,
        [big] * 2,
        p, d, m, left, right, nleft, nright,
        flops=30_000_000,
    )
    left1, right1 = moved(up, 1, 0), moved(down, -1, 0)
    to_left, to_right = call(pack_one, [(12, 8, 512)] * 2, [], s1, c1, left1, right1)
    nleft1, nright1 = moved(to_right, 0, 1), moved(to_left, 0, -1)
    mid = (12, 16, 512)
    se, ce, f1, send, keep, up, down = call(
        level_one,
        [mid, mid, (4, 8, 512), (2, 8, 256), (2, 8, 256), (8, 8, 1024), (8, 8, 1024)],
        [mid] * 6,
        s1, c1, left1, right1, nleft1, nright1, f0,
        flops=10_000_000,
    )
    hleft, hright = moved(up, 1, 0), moved(down, -1, 0)
    pair = keep + other_core(send)
    mine = gathered(pair)
    other = other_core(mine)
    whole, small = (34, 32, 256), (16, 16, 128)
    *two, s3, c3 = call(level_two, [whole] * 8 + [small] * 2, [whole], mine, other, flops=1000)
    s3, hleft, hright = lax.optimization_barrier((s3, hleft, hright))
    to_left, to_right = call(pack_up, [(14, 8, 1024)] * 2, [], f0, f1, hleft, hright)
    nhleft, nhright = moved(to_right, 0, 1), moved(to_left, 0, -1)
    (e2,) = call(coarse_levels, [(6, 8, 256)], [small] + [whole] * 2, s3, c3, *two, flops=1000)
    return call(
        level_up,
        [(8, 16, 1024)] * 2,
        [big] * 2 + [mid] * 6,
        *zero, f0, hleft, hright, nhleft, nhright, se, ce, f1, e2,
        flops=30_000_000,
    )


def solution(mesh):
    wide, narrow = mesh.axis_names
    devices = mesh.devices.reshape(mesh.shape[wide], mesh.shape[narrow] // 2, 2)
    spec = P("wide", ("ny", "core"), None)
    return jax.shard_map(
        lambda p, d, m: tuple(per_device(p, d, m)),
        mesh=Mesh(devices, AX),
        in_specs=(spec,) * 3,
        out_specs=(spec,) * 2,
        check_vma=False,
    )
```

```python
import math

import jax
import jax.numpy as jnp
from jax import lax
from jax.experimental import pallas as pl
from jax.experimental.pallas import tpu as pltpu
from jax.sharding import Mesh, PartitionSpec as P

OMEGA = 0.8
AX = ("wide", "ny", "core")
F32 = jnp.float32
SPARE = 4 * 1024 * 1024


def iota(shape, dim):
    return lax.broadcasted_iota(jnp.int32, shape, dim)


def following(x, dim):
    return pltpu.roll(x, x.shape[dim] - 1, dim)


def preceding(x, dim):
    return pltpu.roll(x, 1, dim)


def lanes(x, r, k):
    return x[r, :, 128 * k : 128 * k + 128]


def row_operator(v, r, c, fa, fb, fz):
    count = v.shape[2] // 128
    lane = iota((v.shape[1], 128), 1)
    here = lanes(v, r, 0)
    turned = pltpu.roll(here, 127, 1)
    out = []
    for k in range(count):
        if k + 1 < count:
            later = lanes(v, r, k + 1)
            later_turned = pltpu.roll(later, 127, 1)
        else:
            later, later_turned = None, 0.0
        gz = lanes(fz, r, k) * (jnp.where(lane == 127, later_turned, turned) - here)
        gz_turned = pltpu.roll(gz, 1, 1)
        if k == 0:
            gz_before = 0.5 * lanes(c, r, 0) * here
        gb = lanes(fb, r, k) * (following(here, 0) - here)
        a = lanes(fa, r, k) * (here - lanes(v, r + 1, k)) + lanes(fa, r - 1, k) * (here - lanes(v, r - 1, k))
        a = a + (preceding(gb, 0) - gb) + (jnp.where(lane == 0, gz_before, gz_turned) - gz)
        out.append(a)
        here, turned, gz_before = later, later_turned, gz_turned
    return out


def row_faces(r, c, fa, fb, fz, w):
    count = c.shape[2] // 128
    cols = c.shape[1]
    lane = iota((cols, 128), 1)
    here = lanes(c, r, 0)
    turned = pltpu.roll(here, 127, 1)
    for k in range(count):
        if k + 1 < count:
            later = lanes(c, r, k + 1)
            later_turned = pltpu.roll(later, 127, 1)
        else:
            later, later_turned = None, 0.0
        at = slice(128 * k, 128 * k + 128)
        z = 0.5 * (here + jnp.where(lane == 127, later_turned, turned))
        z_turned = pltpu.roll(z, 1, 1)
        if k == 0:
            z_before = 0.5 * here
        y = 0.5 * (here + following(here, 0))
        diagonal = 0.5 * (here + lanes(c, r - 1, k)) + 0.5 * (here + lanes(c, r + 1, k))
        diagonal = diagonal + (y + preceding(y, 0)) + (z + jnp.where(lane == 0, z_before, z_turned))
        fa[r, :, at] = 0.5 * (here + lanes(c, r + 1, k))
        fb[r, :, at], fz[r, :, at] = y, z
        w[r, :, at] = jnp.where(here > 0.0, OMEGA / diagonal, 0.0)
        here, turned, z_before = later, later_turned, z_turned


def over_rows(lo, hi, step, body):
    whole = (hi - lo) // step

    def some(i, carry):
        for j in range(step):
            body(lo + i * step + j)
        return carry

    if whole > 1:
        lax.fori_loop(0, whole, some, 0)
        lo = lo + whole * step
    for r in range(lo, hi):
        body(r)


def half_compress(low, high, dim):
    length = low.shape[dim]
    at = iota(low.shape, dim)
    index = (2 * at) % length
    first = jnp.take_along_axis(low, index, axis=dim)
    if high is None:
        return jnp.where(at < length // 2, first, 0.0)
    return jnp.where(at < length // 2, first, jnp.take_along_axis(high, index, axis=dim))


def half_columns(x):
    x = x + following(x, 0)
    tiles = x.shape[0] // 8
    part = lambda t: x[8 * t : 8 * t + 8]
    if tiles == 1:
        return half_compress(x, None, 0)
    x = [half_compress(part(2 * t), part(2 * t + 1), 0) for t in range(tiles // 2)]
    return x[0] if len(x) == 1 else jnp.concatenate(x, axis=0)


def coarse_sum(first, second, split=False):
    halves = [half_columns(x + y) for x, y in zip(first, second)]
    halves = [x + following(x, 1) for x in halves]
    if split:
        lane = iota((8, 128), 1)
        out = []
        for odd in range(2):
            index = (4 * lane + 2 * odd) % 128
            picked = jnp.take_along_axis(halves[0], index, axis=1)
            for k in range(1, 4):
                picked = jnp.where(lane >= 32 * k, jnp.take_along_axis(halves[k], index, axis=1), picked)
            out.append(picked)
        return out
    if len(halves) == 1:
        return [by_tile(halves[0], None)]
    return [by_tile(halves[k], halves[k + 1]) for k in range(0, len(halves), 2)]


def by_tile(low, high):
    tiles = [
        half_compress(low[8 * t : 8 * t + 8], None if high is None else high[8 * t : 8 * t + 8], 1)
        for t in range(low.shape[0] // 8)
    ]
    return tiles[0] if len(tiles) == 1 else jnp.concatenate(tiles, axis=0)


def blocks_of(x):
    return [x[:, 128 * k : 128 * k + 128] for k in range(x.shape[1] // 128)]


def repeat_lanes(x, block):
    source = block // 2
    index = iota((8, 128), 1) // 2 + 64 * (block % 2)
    return jnp.take_along_axis(x[:, 128 * source : 128 * source + 128], index, axis=1)


def take_rows(x, index):
    pieces = [
        jnp.take_along_axis(x[:, k : k + 128], index, axis=0) for k in range(0, x.shape[1], 128)
    ]
    return pieces[0] if len(pieces) == 1 else jnp.concatenate(pieces, axis=1)


def widen(x, blocks):
    pieces = [repeat_lanes(x, k) for k in range(blocks)]
    return pieces[0] if len(pieces) == 1 else jnp.concatenate(pieces, axis=1)


def widen_split(x):
    lane = iota((8, 128), 1)
    pieces = []
    for k in range(4):
        index = 32 * k + lane // 4
        even = jnp.take_along_axis(x[:, :128], index, axis=1)
        odd = jnp.take_along_axis(x[:, 128:], index, axis=1)
        pieces.append(jnp.where(lane // 2 % 2 == 0, even, odd))
    return jnp.concatenate(pieces, axis=1)


def scalars():
    wide, ny, core = lax.axis_index("wide"), lax.axis_index("ny"), lax.axis_index("core")
    sizes = [lax.axis_size(name) for name in AX]
    narrow = ny * sizes[2] + core
    inside = [
        jnp.where(flag, 1.0, 0.0).astype(F32)
        for flag in (wide > 0, wide < sizes[0] - 1, narrow > 0, narrow < sizes[1] * sizes[2] - 1)
    ]
    return wide, narrow, core, inside


def call(kernel, outs, scratch, *args, flops=1_000_000, copies=0):
    vmem = pl.BlockSpec(memory_space=pltpu.VMEM)
    size = 4 * sum(a.size for a in args)
    held = size + 4 * sum(math.prod(s) for s in outs + scratch)
    return pl.pallas_call(
        kernel,
        out_shape=[jax.ShapeDtypeStruct(s, F32) for s in outs],
        in_specs=[vmem] * len(args),
        out_specs=[pl.BlockSpec(memory_space=pltpu.HBM) if copies else vmem] * len(outs),
        scratch_shapes=[pltpu.VMEM(s, F32) for s in scratch] + [pltpu.SemaphoreType.DMA((copies,))] * (copies > 0),
        compiler_params=pltpu.CompilerParams(vmem_limit_bytes=held + SPARE),
        cost_estimate=pl.CostEstimate(flops=flops, bytes_accessed=0 if flops == 1000 else size, transcendentals=0),
    )(*args)


def coarse_coefficients(m, c1, c2):
    for i in range(4):
        x = coarse_sum(blocks_of(m[2 * i]), blocks_of(m[2 * i + 1]))
        for k, a in enumerate(x):
            c1[i, :, 128 * k : 128 * k + 128] = 0.125 * a
    for i in range(2):
        even, odd = coarse_sum(blocks_of(c1[2 * i]), blocks_of(c1[2 * i + 1]), True)
        c2[i] = 0.125 * (even + pltpu.roll(odd, 4, 0))


def pack_zero(p, d, m, left, right, to_left, to_right):
    _, _, _, (low, high, _, _) = scalars()
    at = iota((8, 1024), 0)
    for r in range(14):
        a = r - 3
        for side, out in ((0, to_left), (1, to_right)):
            tile = slice(8 * side, 8 * side + 8)
            if a < 0:
                vp, vm = left[r, tile] * low, left[3 + r, tile] * low
                vd = left[5 + r, tile] * low if r > 0 else jnp.zeros_like(vp)
            elif a < 8:
                vp, vm, vd = p[a, tile], m[a, tile], d[a, tile]
            else:
                vp, vm = right[a - 8, tile] * high, right[a - 5, tile] * high
                vd = right[a - 2, tile] * high if a < 10 else jnp.zeros_like(vp)
            if side == 0:
                vm, vd = pltpu.roll(vm, 3, 0), pltpu.roll(vd, 6, 0)
                out[r] = jnp.where(at < 3, vp, jnp.where(at < 6, vm, vd))
            else:
                vm, vd = pltpu.roll(vm, 5, 0), pltpu.roll(vd, 2, 0)
                out[r] = jnp.where(at >= 5, vp, jnp.where(at >= 2, vm, vd))


def faces(c, rows, fa, fb, fz, w, step):
    for k in range(c.shape[2] // 128):
        at = slice(128 * k, 128 * k + 128)
        fa[rows[0] - 1, :, at] = 0.5 * (c[rows[0] - 1, :, at] + c[rows[0], :, at])
    over_rows(rows[0], rows[1], step, lambda r: row_faces(r, c, fa, fb, fz, w))


def sweep(source, target, s, c, fa, fb, fz, w, rows, step):
    def one(r):
        for k, a in enumerate(row_operator(source, r, c, fa, fb, fz)):
            at = slice(128 * k, 128 * k + 128)
            target[r, :, at] = source[r, :, at] + w[r, :, at] * (s[r, :, at] - a)

    over_rows(rows[0], rows[1], step, one)


def residual_row(v, s, c, fa, fb, fz, r, cols):
    return [
        (lanes(s, r, k) - a)[0:cols]
        for k, a in enumerate(row_operator(v, r, c, fa, fb, fz))
    ]


def level_zero(p, d, m, left, right, c1, nleft, nright, field, s1, up, down, me, de, w, fa, fb, fz, v, u):
    _, _, _, (low, high, nlow, nhigh) = scalars()
    at = iota((8, 1024), 0)
    for r in range(14):
        a = r - 3
        if a < 0:
            v[r, 0:16], me[r, 0:16] = left[r] * low, left[3 + r] * low
            de[r, 0:16] = left[5 + r] * low if r > 0 else jnp.zeros((16, 1024), F32)
        elif a < 8:
            v[r, 0:16], me[r, 0:16], de[r, 0:16] = p[a], m[a], d[a]
        else:
            v[r, 0:16], me[r, 0:16] = right[a - 8] * high, right[a - 5] * high
            de[r, 0:16] = right[a - 2] * high if a < 10 else jnp.zeros((16, 1024), F32)
        x, y = nright[r] * nhigh, nleft[r] * nlow
        v[r, 16:24] = jnp.where(at < 3, x, jnp.where(at >= 5, y, 0.0))
        x3, y3 = pltpu.roll(x, 5, 0), pltpu.roll(y, 3, 0)
        me[r, 16:24] = jnp.where(at < 3, x3, jnp.where(at >= 5, y3, 0.0))
        x6, y6 = pltpu.roll(x, 2, 0), pltpu.roll(y, 6, 0)
        de[r, 16:24] = jnp.where(at < 2, x6, jnp.where(at >= 6, y6, 0.0))
    faces(me, (1, 13), fa, fb, fz, w, 2)
    u[0], u[13] = v[0], v[13]
    sweep(v, u, de, me, fa, fb, fz, w, (1, 13), 2)
    sweep(u, v, de, me, fa, fb, fz, w, (2, 12), 2)
    field[...] = v[3:11, 0:16]

    def coarse(i, carry):
        r = 2 * i + 3
        x = residual_row(v, de, me, fa, fb, fz, r, 16)
        y = residual_row(v, de, me, fa, fb, fz, r + 1, 16)
        for k, a in enumerate(coarse_sum(x, y)):
            s1[i, :, 128 * k : 128 * k + 128] = 0.5 * a
        return carry

    lax.fori_loop(0, 4, coarse, 0)
    up[0:3], down[0:3] = s1[1:4], s1[0:3]
    up[3:7], down[3:7] = c1[...], c1[...]


def pack_one(s, c, left, right, to_left, to_right):
    _, _, _, (low, high, _, _) = scalars()
    at = iota((8, 512), 0)
    for r in range(12):
        a = r - 4
        if a < 0:
            vc = left[3 + r] * low
            vs = left[r - 1] * low if r > 0 else jnp.zeros_like(vc)
        elif a < 4:
            vs, vc = s[a], c[a]
        else:
            vc = right[a - 1] * high
            vs = right[a - 4] * high if a < 7 else jnp.zeros_like(vc)
        to_left[r] = jnp.where(at < 4, vc, pltpu.roll(vs, 4, 0))
        to_right[r] = jnp.where(at >= 4, vc, pltpu.roll(vs, 4, 0))


def level_one(s, c, left, right, nleft, nright, f0, field, s2, up, down, se, ce, fa, fb, fz, w, v, u):
    _, _, _, (low, high, nlow, nhigh) = scalars()
    at = iota((8, 512), 0)
    for r in range(12):
        a = r - 4
        if a < 0:
            ce[r, 0:8] = left[3 + r] * low
            se[r, 0:8] = left[r - 1] * low if r > 0 else jnp.zeros((8, 512), F32)
        elif a < 4:
            se[r, 0:8], ce[r, 0:8] = s[a], c[a]
        else:
            ce[r, 0:8] = right[a - 1] * high
            se[r, 0:8] = right[a - 4] * high if a < 7 else jnp.zeros((8, 512), F32)
        x, y = nright[r] * nhigh, nleft[r] * nlow
        ce[r, 8:16] = jnp.where(at < 4, x, y)
        se[r, 8:16] = jnp.where(at < 4, pltpu.roll(x, 4, 0), pltpu.roll(y, 4, 0))
    faces(ce, (1, 11), fa, fb, fz, w, 5)

    for r in range(2, 10):
        u[r] = w[r] * se[r]
    sweep(u, v, se, ce, fa, fb, fz, w, (3, 9), 3)
    field[...] = v[4:8, 0:8]
    for i in range(2):
        r = 2 * i + 4
        x = residual_row(v, se, ce, fa, fb, fz, r, 8)
        y = residual_row(v, se, ce, fa, fb, fz, r + 1, 8)
        even, odd = coarse_sum(x, y, True)
        s2[i] = 0.5 * (even + pltpu.roll(odd, 4, 0))
    for r in range(3):
        for t in range(2):
            up[2 * r + t] = f0[5 + r, 8 * t : 8 * t + 8]
            down[2 * r + t] = f0[r, 8 * t : 8 * t + 8]
    for r in range(2):
        both = jnp.concatenate([field[2 * r], field[2 * r + 1]], axis=1)
        up[6 + r] = both
        down[6 + r] = both


def pack_up(f0, f1, left, right, to_left, to_right):
    _, _, _, (low, high, _, _) = scalars()
    at = iota((8, 1024), 0)

    def fine(r, side):
        if r < 3:
            return left[2 * r + side] * low
        if r < 11:
            return f0[r - 3, 8 * side : 8 * side + 8]
        return right[2 * (r - 11) + side] * high

    def pair(r):
        if r < 2:
            return left[6 + r] * low
        if r < 4:
            return jnp.concatenate([f1[2 * r - 4], f1[2 * r - 3]], axis=1)
        return right[2 + r] * high

    for t in range(7):
        to_left[t] = jnp.where(at < 4, fine(2 * t, 0), pltpu.roll(fine(2 * t + 1, 0), 4, 0))
        to_right[t] = jnp.where(at >= 4, fine(2 * t, 1), pltpu.roll(fine(2 * t + 1, 1), 4, 0))
    for t in range(3):
        to_left[7 + t] = jnp.where(at < 4, pair(2 * t), pltpu.roll(pair(2 * t + 1), 4, 0))
        to_right[7 + t] = jnp.where(at >= 4, pair(2 * t), pltpu.roll(pair(2 * t + 1), 4, 0))


def level_up(
    me, de, w, fa, fb, fz, se, ce, fa1, fb1, fz1, w1, f0, f1, left, right, nleft, nright, e2,
    out, res, v, u, v1, u1, kept, sent,
):
    _, _, _, (low, high, nlow, nhigh) = scalars()
    at = iota((8, 512), 0)
    half = iota((8, 128), 0)
    for r in range(12):
        if r < 4:
            f = left[6 + r // 2][:, 512 * (r % 2) : 512 * (r % 2) + 512] * low
        elif r < 8:
            f = f1[r - 4]
        else:
            f = right[2 + r // 2][:, 512 * (r % 2) : 512 * (r % 2) + 512] * high
        x = nright[7 + r // 4][:, 512 * (r % 2) : 512 * (r % 2) + 512] * nhigh
        y = nleft[7 + r // 4][:, 512 * (r % 2) : 512 * (r % 2) + 512] * nlow
        if r % 4 > 1:
            x, y = pltpu.roll(x, 4, 0), pltpu.roll(y, 4, 0)
        g = jnp.where(at < 4, x, y)
        e = e2[r // 2]
        own = widen_split(take_rows(e, 2 + half // 2))
        beside = widen_split(take_rows(e, jnp.where(half < 4, 6 + half // 2, (half - 4) // 2)))
        v1[r, 0:8] = f + jnp.where(ce[r, 0:8] > 0.0, own, 0.0)
        v1[r, 8:16] = g + jnp.where(ce[r, 8:16] > 0.0, beside, 0.0)
    sweep(v1, u1, se, ce, fa1, fb1, fz1, w1, (1, 11), 5)
    sweep(u1, v1, se, ce, fa1, fb1, fz1, w1, (2, 10), 4)
    zero = iota((8, 1024), 0)
    for r in range(14):
        if r < 3:
            f = [left[2 * r] * low, left[2 * r + 1] * low]
        elif r < 11:
            f = [f0[r - 3, 0:8], f0[r - 3, 8:16]]
        else:
            f = [right[2 * (r - 11)] * high, right[2 * (r - 11) + 1] * high]
        x, y = nright[r // 2] * nhigh, nleft[r // 2] * nlow
        if r % 2 > 0:
            x, y = pltpu.roll(x, 4, 0), pltpu.roll(y, 4, 0)
        f.append(jnp.where(zero < 3, x, jnp.where(zero >= 5, y, 0.0)))
        e = v1[(r + 5) // 2]
        pieces = (
            (e[0:8], half // 2),
            (e[0:8], 4 + half // 2),
            (e[8:16], jnp.where(half < 4, half // 2, 4 + half // 2)),
        )
        for t, (part, index) in enumerate(pieces):
            fine = widen(take_rows(part, index), 8)
            tile = slice(8 * t, 8 * t + 8)
            v[r, tile] = f[t] + jnp.where(me[r, tile] > 0.0, fine, 0.0)

    sweep(v, u, de, me, fa, fb, fz, w, (1, 13), 2)
    sweep(u, v, de, me, fa, fb, fz, w, (2, 12), 2)
    first = pltpu.make_async_copy(v.at[3:11, 0:16], out, sent.at[0])
    first.start()

    def final(r):
        for k, x in enumerate(residual_row(v, de, me, fa, fb, fz, r, 16)):
            kept[r - 3, :, 128 * k : 128 * k + 128] = x

    over_rows(3, 7, 2, final)
    second = pltpu.make_async_copy(kept.at[0:4], res.at[0:4], sent.at[1])
    second.start()
    over_rows(7, 11, 2, final)
    third = pltpu.make_async_copy(kept.at[4:8], res.at[4:8], sent.at[2])
    third.start()
    for copy in (first, second, third):
        copy.wait()


def shifted(x, step):
    zero = jnp.zeros((1,) + x.shape[1:], F32)
    return jnp.concatenate([x[1:], zero] if step > 0 else [zero, x[:-1]], axis=0)


class Whole:
    def __init__(self, c, cols, length):
        b, z = iota(c.shape, 1), iota(c.shape, 2)
        valid = (b < cols) & (z < length)
        self.fa = 0.5 * (c + shifted(c, 1))
        self.fa_below = 0.5 * (c + shifted(c, -1))
        self.fb = jnp.where(b < cols - 1, 0.5 * (c + following(c, 1)), 0.0)
        self.fz = jnp.where(z < length - 1, 0.5 * (c + following(c, 2)), 0.0)
        half = 0.5 * c
        self.ends = jnp.where(b == 0, half, 0.0) + jnp.where(b == cols - 1, half, 0.0)
        self.ends = self.ends + jnp.where(z == 0, half, 0.0) + jnp.where(z == length - 1, half, 0.0)
        diagonal = self.fa + self.fa_below + self.fb + preceding(self.fb, 1)
        diagonal = diagonal + self.fz + preceding(self.fz, 2) + self.ends
        self.w = jnp.where(valid, OMEGA / diagonal, 0.0)

    def operator(self, v):
        gb = self.fb * (following(v, 1) - v)
        gz = self.fz * (following(v, 2) - v)
        out = self.fa * (v - shifted(v, 1)) + self.fa_below * (v - shifted(v, -1)) + self.ends * v
        return out + (preceding(gb, 1) - gb) + (preceding(gz, 2) - gz)

    def sweep(self, v, s):
        return v + self.w * (s - self.operator(v))


def coarsen_whole(x):
    return jnp.stack([coarse_sum([x[a]], [x[a + 1]])[0] for a in range(0, x.shape[0], 2)])


def refine_row(x, cols_tiles, lanes_too):
    half = iota((8, 128), 0)
    tiles = []
    for t in range(cols_tiles):
        source = x[8 * (t // 2) : 8 * (t // 2) + 8]
        tile = take_rows(source, half // 2 + 4 * (t % 2))
        tiles.append(widen(tile, 1) if lanes_too else tile)
    return tiles[0] if cols_tiles == 1 else jnp.concatenate(tiles, axis=0)


def refine_whole(x, cols_tiles):
    rows = [refine_row(x[a], cols_tiles, True) for a in range(x.shape[0])]
    return jnp.stack([rows[a // 2] for a in range(2 * x.shape[0])])


def multiply(x, y):
    out = [[None] * 4 for _ in range(4)]
    for i in range(4):
        for j in range(4):
            for k in range(4):
                if x[i][k] is not None and y[k][j] is not None:
                    term = x[i][k] * y[k][j]
                    out[i][j] = term if out[i][j] is None else out[i][j] + term
    return out


def apply(x, y):
    out = []
    for i in range(4):
        total = None
        for k in range(4):
            if x[i][k] is not None:
                term = x[i][k] * y[k]
                total = term if total is None else total + term
        out.append(total)
    return out


def inverse(x):
    x = [[jnp.zeros((8, 128), F32) if e is None else e for e in line] for line in x]
    for k in range(4):
        pivot = 1.0 / x[k][k]
        line = [pivot if j == k else x[k][j] * pivot for j in range(4)]
        for i in range(4):
            if i != k:
                factor = x[i][k]
                x[i] = [-factor * pivot if j == k else x[i][j] - factor * line[j] for j in range(4)]
        x[k] = line
    return x


def each(x, move):
    return [[None if e is None else move(e) for e in line] for line in x]


def exact(s, c):
    length = 16
    lane = iota((8, 128), 1)
    row = iota((8, 128), 0)
    valid = lane < length

    def line(x, a, b):
        picked = jnp.take_along_axis(x[a], jnp.full((8, 128), b, jnp.int32), axis=0)
        return jnp.where(valid, picked, 0.0)

    cs = [line(c, k // 2, k % 2) for k in range(4)]
    rhs = [line(s, k // 2, k % 2) for k in range(4)]
    below = [[None] * 4 for _ in range(4)]
    above = [[None] * 4 for _ in range(4)]
    centre = [[None] * 4 for _ in range(4)]
    for k in range(4):
        here = cs[k]
        upper = 0.5 * (here + following(here, 1))
        lower = 0.5 * (here + preceding(here, 1))
        fa, fb = 0.5 * (here + cs[k ^ 2]), 0.5 * (here + cs[k ^ 1])
        diagonal = upper + lower + fa + fb + here
        centre[k][k] = jnp.where(valid, diagonal, 1.0)
        centre[k][k ^ 2], centre[k][k ^ 1] = -fa, -fb
        above[k][k] = jnp.where(lane < length - 1, -upper, 0.0)
        below[k][k] = jnp.where((lane > 0) & valid, -lower, 0.0)
    step = 1
    while step < length:
        ahead = lambda e, step=step: pltpu.roll(e, 128 - step, 1)
        behind = lambda e, step=step: pltpu.roll(e, step, 1)
        solved = inverse(centre)
        t, u, q = multiply(solved, below), multiply(solved, above), apply(solved, rhs)
        t_ahead, u_behind = each(t, ahead), each(u, behind)
        x, y = multiply(below, u_behind), multiply(above, t_ahead)
        centre = [
            [jnp.zeros((8, 128), F32) if centre[i][j] is None else centre[i][j] for j in range(4)]
            for i in range(4)
        ]
        centre = [[centre[i][j] - x[i][j] - y[i][j] for j in range(4)] for i in range(4)]
        x, y = apply(below, [behind(e) for e in q]), apply(above, [ahead(e) for e in q])
        rhs = [rhs[i] - x[i] - y[i] for i in range(4)]
        if 2 * step < length:
            below = each(multiply(below, each(t, behind)), lambda e: -e)
            above = each(multiply(above, each(u, ahead)), lambda e: -e)
        step *= 2
    solved = [jnp.where(valid, e, 0.0) for e in apply(inverse(centre), rhs)]
    return jnp.stack(
        [
            jnp.where(row == 0, solved[2 * a], jnp.where(row == 1, solved[2 * a + 1], 0.0))
            for a in range(2)
        ]
    )


def descend(s, c, cols, length):
    if c.shape[0] == 2:
        return exact(s, c)
    level = Whole(c, cols, length)
    v = level.w * s
    v = level.sweep(v, s)
    r = s - level.operator(v)
    e = descend(0.5 * coarsen_whole(r), 0.125 * coarsen_whole(c), cols // 2, length // 2)
    v = v + refine_whole(e, c.shape[1] // 8)
    v = level.sweep(v, s)
    return level.sweep(v, s)


def split_before(last, first_lane):
    lane = iota(last.shape, 1)
    return jnp.where(lane == 0, first_lane, pltpu.roll(last, 1, 1))


def split_after(first):
    lane = iota(first.shape, 1)
    return jnp.where(lane == 127, 0.0, pltpu.roll(first, 127, 1))


def split_operator(v, r, c, fa, fb, fz, ends):
    here = [lanes(v, r, k) for k in range(2)]
    after = [here[1], split_after(here[0])]
    gz = [lanes(fz, r, k) * (after[k] - here[k]) for k in range(2)]
    before = [split_before(gz[1], 0.5 * lanes(c, r, 0) * here[0]), gz[0]]
    out = []
    for k in range(2):
        gb = lanes(fb, r, k) * (following(here[k], 0) - here[k])
        a = lanes(fa, r, k) * (here[k] - lanes(v, r + 1, k)) + lanes(fa, r - 1, k) * (here[k] - lanes(v, r - 1, k))
        a = a + lanes(ends, r, k) * here[k]
        out.append(a + (preceding(gb, 0) - gb) + (before[k] - gz[k]))
    return out


def split_sweep(source, target, s, c, fa, fb, fz, ends, w, r):
    for k, a in enumerate(split_operator(source, r, c, fa, fb, fz, ends)):
        at = slice(128 * k, 128 * k + 128)
        target[r, :, at] = source[r, :, at] + w[r, :, at] * (s[r, :, at] - a)


def level_two(mine, other, s, c, v, fa, fb, fz, ends, w, s3, c3, u):
    _, _, core, _ = scalars()
    strips = mine.shape[0] // 32
    rows, cols = 32, 8 * strips
    first = iota((8, 128), 0) < 4
    edge = jnp.zeros((cols, 256), F32)
    for x in (c, v, u):
        x[0], x[rows + 1] = edge, edge

    def place(target, r, y, near, far):
        target[r, 8 * y : 8 * y + 8, 0:128] = jnp.where(first, near, pltpu.roll(far, 4, 0))
        target[r, 8 * y : 8 * y + 8, 128:256] = jnp.where(first, pltpu.roll(near, 4, 0), far)

    def load(k):
        for y in range(strips):
            at = 2 * (k * strips + y)
            for i in range(2):
                r = 2 * k + i + 1
                x, z = (mine[at, i], mine[at + 1, i]), (other[at, i], other[at + 1, i])
                place(s, r, y, *(jnp.where(core == 0, a, b) for a, b in zip(x, z)))
                place(c, r, y, *(jnp.where(core == 0, b, a) for a, b in zip(x, z)))

    over_rows(0, rows // 2, 2, load)
    fa[0] = 0.5 * c[1]
    b = iota((cols, 128), 0)

    def one(r):
        here = [lanes(c, r, k) for k in range(2)]
        z = [0.5 * (here[0] + here[1]), 0.5 * (here[1] + split_after(here[0]))]
        before = [split_before(z[1], 0.5 * here[0]), z[0]]
        for k in range(2):
            at = slice(128 * k, 128 * k + 128)
            x, h = here[k], 0.5 * here[k]
            y = jnp.where(b == cols - 1, 0.0, 0.5 * (x + following(x, 0)))
            e = jnp.where((b == 0) | (b == cols - 1), h, 0.0)
            above = h + 0.5 * lanes(c, r + 1, k)
            diagonal = above + (h + 0.5 * lanes(c, r - 1, k)) + (y + preceding(y, 0)) + (z[k] + before[k]) + e
            factor = OMEGA / diagonal
            fa[r, :, at], fb[r, :, at], fz[r, :, at] = above, y, z[k]
            ends[r, :, at], w[r, :, at] = e, factor
            u[r, :, at] = factor * s[r, :, at]

    over_rows(1, rows + 1, 4, one)
    over_rows(1, rows + 1, 4, lambda r: split_sweep(u, v, s, c, fa, fb, fz, ends, w, r))

    def coarse(i):
        total = None
        for r in (2 * i + 1, 2 * i + 2):
            for k, a in enumerate(split_operator(v, r, c, fa, fb, fz, ends)):
                x = lanes(s, r, k) - a
                total = x if total is None else total + x
        s3[i] = 0.5 * half_columns(total)
        total = (lanes(c, 2 * i + 1, 0) + lanes(c, 2 * i + 1, 1)) + (lanes(c, 2 * i + 2, 0) + lanes(c, 2 * i + 2, 1))
        c3[i] = 0.125 * half_columns(total)

    over_rows(0, rows // 2, 2, coarse)


def coarse_levels(s3, c3, s, c, v, fa, fb, fz, ends, w, e2, e3, u, t):
    wide, narrow, _, _ = scalars()
    rows, cols = s.shape[0] - 2, s.shape[1]
    e3[...] = descend(s3[...], c3[...], cols // 2, 128)
    row = lambda step: jnp.clip(2 * wide + step, 0, rows - 1) + 1
    u[0], u[rows + 1], t[0], t[rows + 1] = v[0], v[0], v[0], v[0]
    for i in range(-2, 3):
        k = jnp.clip(wide + i, 0, rows // 2 - 1)
        e = refine_row(e3[k], cols // 8, False)
        for r in (2 * k + 1, 2 * k + 2):
            for half in range(2):
                at = slice(128 * half, 128 * half + 128)
                u[r, :, at] = v[r, :, at] + e
    for i in range(-3, 5):
        split_sweep(u, t, s, c, fa, fb, fz, ends, w, row(i))
    for i in range(-2, 4):
        split_sweep(t, u, s, c, fa, fb, fz, ends, w, row(i))
    for i in range(6):
        turned = pltpu.roll(u[row(i - 2)], lax.rem(cols + 2 - 4 * narrow, cols), 0)
        e2[i] = turned[0:8]


def moved(x, wide_step, narrow_step):
    w, y, k = [lax.axis_size(name) for name in AX]
    n = y * k
    pairs = [
        (i * n + j, ((i + wide_step) % w) * n + (j + narrow_step) % n)
        for i in range(w)
        for j in range(n)
    ]
    return lax.ppermute(x, AX, pairs)


def other_core(x):
    w, y, k = [lax.axis_size(name) for name in AX]
    return lax.ppermute(x, AX, [(i, i ^ 1) for i in range(w * y * k)])


def gathered(s2, c2):
    chips = lax.axis_size("wide") * lax.axis_size("ny")
    both = jnp.stack([s2, c2])
    sent = jnp.broadcast_to(both[None], (chips,) + both.shape).reshape((-1,) + s2.shape)
    return lax.all_to_all(sent, AX, 0, 0, tiled=True)


def per_device(p, d, m):
    up = jnp.concatenate([p[5:8], m[5:8], d[6:8]], axis=0)
    down = jnp.concatenate([p[0:3], m[0:3], d[0:2]], axis=0)
    left, right = moved(up, 1, 0), moved(down, -1, 0)
    c1, c2 = call(coarse_coefficients, [(4, 8, 512), (2, 8, 128)], [], m)
    to_left, to_right = call(pack_zero, [(14, 8, 1024)] * 2, [], p, d, m, left, right)
    nleft, nright = moved(to_right, 0, 1), moved(to_left, 0, -1)
    big = (14, 24, 1024)
    f0, s1, up, down, *zero = call(
        level_zero,
        [(8, 16, 1024), (4, 8, 512)] + [(7, 8, 512)] * 2 + [big] * 6,
        [big] * 2,
        p, d, m, left, right, c1, nleft, nright,
        flops=30_000_000,
    )
    left1, right1 = moved(up, 1, 0), moved(down, -1, 0)
    to_left, to_right = call(pack_one, [(12, 8, 512)] * 2, [], s1, c1, left1, right1)
    nleft1, nright1 = moved(to_right, 0, 1), moved(to_left, 0, -1)
    mid = (12, 16, 512)
    f1, s2, up, down, *one = call(
        level_one,
        [(4, 8, 512), (2, 8, 128)] + [(8, 8, 1024)] * 2 + [mid] * 6,
        [mid] * 2,
        s1, c1, left1, right1, nleft1, nright1, f0,
        flops=10_000_000,
    )
    hleft, hright = moved(up, 1, 0), moved(down, -1, 0)
    mine = gathered(s2, c2)
    other = other_core(mine)
    whole, small = (34, 32, 256), (16, 16, 128)
    *two, s3, c3 = call(level_two, [whole] * 8 + [small] * 2, [whole], mine, other, flops=1000)
    s3, hleft, hright = lax.optimization_barrier((s3, hleft, hright))
    to_left, to_right = call(pack_up, [(10, 8, 1024)] * 2, [], f0, f1, hleft, hright)
    nhleft, nhright = moved(to_right, 0, 1), moved(to_left, 0, -1)
    (e2,) = call(coarse_levels, [(6, 8, 256)], [small] + [whole] * 2, s3, c3, *two, flops=1000)
    return call(
        level_up,
        [(8, 16, 1024)] * 2,
        [big] * 2 + [mid] * 2 + [(8, 16, 1024)],
        *zero, *one, f0, f1, hleft, hright, nhleft, nhright, e2,
        flops=30_000_000,
        copies=3,
    )


def solution(mesh):
    wide, narrow = mesh.axis_names
    devices = mesh.devices.reshape(mesh.shape[wide], mesh.shape[narrow] // 2, 2)
    spec = P("wide", ("ny", "core"), None)
    return jax.shard_map(
        lambda p, d, m: tuple(per_device(p, d, m)),
        mesh=Mesh(devices, AX),
        in_specs=(spec,) * 3,
        out_specs=(spec,) * 2,
        check_vma=False,
    )
```

```python
import math

import jax
import jax.numpy as jnp
from jax import lax
from jax.experimental import pallas as pl
from jax.experimental.pallas import tpu as pltpu
from jax.sharding import Mesh, PartitionSpec as P

OMEGA = 0.8
AX = ("wide", "ny", "core")
F32 = jnp.float32
SPARE = 4 * 1024 * 1024


def iota(shape, dim):
    return lax.broadcasted_iota(jnp.int32, shape, dim)


def following(x, dim):
    return pltpu.roll(x, x.shape[dim] - 1, dim)


def preceding(x, dim):
    return pltpu.roll(x, 1, dim)


def lanes(x, r, k):
    if isinstance(x, tuple):
        return jnp.concatenate([lanes(part, r, k) for part in x], axis=0)
    return x[r, :, 128 * k : 128 * k + 128]


def row_operator(v, r, c, fa, fb, fz):
    count = v.shape[2] // 128
    lane = iota((v.shape[1], 128), 1)
    here = lanes(v, r, 0)
    turned = pltpu.roll(here, 127, 1)
    out = []
    for k in range(count):
        if k + 1 < count:
            later = lanes(v, r, k + 1)
            later_turned = pltpu.roll(later, 127, 1)
        else:
            later, later_turned = None, 0.0
        gz = lanes(fz, r, k) * (jnp.where(lane == 127, later_turned, turned) - here)
        gz_turned = pltpu.roll(gz, 1, 1)
        if k == 0:
            gz_before = 0.5 * lanes(c, r, 0) * here
        gb = lanes(fb, r, k) * (following(here, 0) - here)
        a = lanes(fa, r, k) * (here - lanes(v, r + 1, k)) + lanes(fa, r - 1, k) * (here - lanes(v, r - 1, k))
        a = a + (preceding(gb, 0) - gb) + (jnp.where(lane == 0, gz_before, gz_turned) - gz)
        out.append(a)
        here, turned, gz_before = later, later_turned, gz_turned
    return out


def row_faces(r, c, fa, fb, fz, w):
    count = c.shape[2] // 128
    cols = c.shape[1]
    lane = iota((cols, 128), 1)
    here = lanes(c, r, 0)
    turned = pltpu.roll(here, 127, 1)
    for k in range(count):
        if k + 1 < count:
            later = lanes(c, r, k + 1)
            later_turned = pltpu.roll(later, 127, 1)
        else:
            later, later_turned = None, 0.0
        at = slice(128 * k, 128 * k + 128)
        z = 0.5 * (here + jnp.where(lane == 127, later_turned, turned))
        z_turned = pltpu.roll(z, 1, 1)
        if k == 0:
            z_before = 0.5 * here
        y = 0.5 * (here + following(here, 0))
        diagonal = 0.5 * (here + lanes(c, r - 1, k)) + 0.5 * (here + lanes(c, r + 1, k))
        diagonal = diagonal + (y + preceding(y, 0)) + (z + jnp.where(lane == 0, z_before, z_turned))
        fa[r, :, at] = 0.5 * (here + lanes(c, r + 1, k))
        fb[r, :, at], fz[r, :, at] = y, z
        w[r, :, at] = jnp.where(here > 0.0, OMEGA / diagonal, 0.0)
        here, turned, z_before = later, later_turned, z_turned


def over_rows(lo, hi, step, body):
    whole = (hi - lo) // step

    def some(i, carry):
        for j in range(step):
            body(lo + i * step + j)
        return carry

    if whole > 1:
        lax.fori_loop(0, whole, some, 0)
        lo = lo + whole * step
    for r in range(lo, hi):
        body(r)


def half_compress(low, high, dim):
    length = low.shape[dim]
    at = iota(low.shape, dim)
    index = (2 * at) % length
    first = jnp.take_along_axis(low, index, axis=dim)
    if high is None:
        return jnp.where(at < length // 2, first, 0.0)
    return jnp.where(at < length // 2, first, jnp.take_along_axis(high, index, axis=dim))


def half_columns(x):
    x = x + following(x, 0)
    tiles = x.shape[0] // 8
    part = lambda t: x[8 * t : 8 * t + 8]
    if tiles == 1:
        return half_compress(x, None, 0)
    x = [half_compress(part(2 * t), part(2 * t + 1), 0) for t in range(tiles // 2)]
    return x[0] if len(x) == 1 else jnp.concatenate(x, axis=0)


def coarse_sum(first, second, split=False):
    halves = [half_columns(x + y) for x, y in zip(first, second)]
    halves = [x + following(x, 1) for x in halves]
    if split:
        lane = iota((8, 128), 1)
        out = []
        for odd in range(2):
            index = (4 * lane + 2 * odd) % 128
            picked = jnp.take_along_axis(halves[0], index, axis=1)
            for k in range(1, 4):
                picked = jnp.where(lane >= 32 * k, jnp.take_along_axis(halves[k], index, axis=1), picked)
            out.append(picked)
        return out
    if len(halves) == 1:
        return [by_tile(halves[0], None)]
    return [by_tile(halves[k], halves[k + 1]) for k in range(0, len(halves), 2)]


def by_tile(low, high):
    tiles = [
        half_compress(low[8 * t : 8 * t + 8], None if high is None else high[8 * t : 8 * t + 8], 1)
        for t in range(low.shape[0] // 8)
    ]
    return tiles[0] if len(tiles) == 1 else jnp.concatenate(tiles, axis=0)


def blocks_of(x):
    return [x[:, 128 * k : 128 * k + 128] for k in range(x.shape[1] // 128)]


def repeat_lanes(x, block):
    source = block // 2
    index = iota((8, 128), 1) // 2 + 64 * (block % 2)
    return jnp.take_along_axis(x[:, 128 * source : 128 * source + 128], index, axis=1)


def take_rows(x, index):
    pieces = [
        jnp.take_along_axis(x[:, k : k + 128], index, axis=0) for k in range(0, x.shape[1], 128)
    ]
    return pieces[0] if len(pieces) == 1 else jnp.concatenate(pieces, axis=1)


def widen(x, blocks):
    pieces = [repeat_lanes(x, k) for k in range(blocks)]
    return pieces[0] if len(pieces) == 1 else jnp.concatenate(pieces, axis=1)


def widen_split(x):
    lane = iota((8, 128), 1)
    pieces = []
    for k in range(4):
        index = 32 * k + lane // 4
        even = jnp.take_along_axis(x[:, :128], index, axis=1)
        odd = jnp.take_along_axis(x[:, 128:], index, axis=1)
        pieces.append(jnp.where(lane // 2 % 2 == 0, even, odd))
    return jnp.concatenate(pieces, axis=1)


def scalars():
    wide, ny, core = lax.axis_index("wide"), lax.axis_index("ny"), lax.axis_index("core")
    sizes = [lax.axis_size(name) for name in AX]
    narrow = ny * sizes[2] + core
    inside = [
        jnp.where(flag, 1.0, 0.0).astype(F32)
        for flag in (wide > 0, wide < sizes[0] - 1, narrow > 0, narrow < sizes[1] * sizes[2] - 1)
    ]
    return wide, narrow, core, inside


def call(kernel, outs, scratch, *args, flops=1_000_000, copies=0):
    vmem = pl.BlockSpec(memory_space=pltpu.VMEM)
    size = 4 * sum(a.size for a in args)
    held = size + 4 * sum(math.prod(s) for s in outs + scratch)
    return pl.pallas_call(
        kernel,
        out_shape=[jax.ShapeDtypeStruct(s, F32) for s in outs],
        in_specs=[vmem] * len(args),
        out_specs=[pl.BlockSpec(memory_space=pltpu.HBM) if copies else vmem] * len(outs),
        scratch_shapes=[pltpu.VMEM(s, F32) for s in scratch] + [pltpu.SemaphoreType.DMA((copies,))] * (copies > 0),
        compiler_params=pltpu.CompilerParams(vmem_limit_bytes=held + SPARE),
        cost_estimate=pl.CostEstimate(flops=flops, bytes_accessed=0 if flops == 1000 else size, transcendentals=0),
    )(*args)


def coarse_coefficients(m, c1, c2):
    for i in range(4):
        x = coarse_sum(blocks_of(m[2 * i]), blocks_of(m[2 * i + 1]))
        for k, a in enumerate(x):
            c1[i, :, 128 * k : 128 * k + 128] = 0.125 * a
    for i in range(2):
        even, odd = coarse_sum(blocks_of(c1[2 * i]), blocks_of(c1[2 * i + 1]), True)
        c2[i] = 0.125 * (even + pltpu.roll(odd, 4, 0))


def pack_zero(p, d, m, left, right, to_left, to_right):
    _, _, _, (low, high, _, _) = scalars()
    at = iota((8, 1024), 0)
    for r in range(1, 13):
        a = r - 3
        for side, out in ((0, to_left), (1, to_right)):
            tile = slice(8 * side, 8 * side + 8)
            if a < 0:
                vp, vm = left[r, tile] * low, left[3 + r, tile] * low
                vd = left[5 + r, tile] * low if r > 0 else jnp.zeros_like(vp)
            elif a < 8:
                vp, vm, vd = p[a, tile], m[a, tile], d[a, tile]
            else:
                vp, vm = right[a - 8, tile] * high, right[a - 5, tile] * high
                vd = right[a - 2, tile] * high if a < 10 else jnp.zeros_like(vp)
            if side == 0:
                vm, vd = pltpu.roll(vm, 3, 0), pltpu.roll(vd, 6, 0)
                out[r - 1] = jnp.where(at < 3, vp, jnp.where(at < 6, vm, vd))
            else:
                vm, vd = pltpu.roll(vm, 5, 0), pltpu.roll(vd, 2, 0)
                out[r - 1] = jnp.where(at >= 5, vp, jnp.where(at >= 2, vm, vd))


def faces(c, rows, fa, fb, fz, w, step):
    for k in range(c.shape[2] // 128):
        at = slice(128 * k, 128 * k + 128)
        fa[rows[0] - 1, :, at] = 0.5 * (c[rows[0] - 1, :, at] + c[rows[0], :, at])
    over_rows(rows[0], rows[1], step, lambda r: row_faces(r, c, fa, fb, fz, w))


def sweep(source, target, s, c, fa, fb, fz, w, rows, step):
    def one(r):
        for k, a in enumerate(row_operator(source, r, c, fa, fb, fz)):
            at = slice(128 * k, 128 * k + 128)
            target[r, :, at] = source[r, :, at] + w[r, :, at] * (lanes(s, r, k) - a)

    over_rows(rows[0], rows[1], step, one)


def residual_row(v, s, c, fa, fb, fz, r, cols):
    return [
        (lanes(s, r, k) - a)[0:cols]
        for k, a in enumerate(row_operator(v, r, c, fa, fb, fz))
    ]


def across(r, v, c, s, fa, fz, diagonal, left_over):
    lane = iota((c.shape[1], 128), 1)
    count = c.shape[2] // 128
    turn = lambda x, k: pltpu.roll(lanes(x, r, k), 127, 1) if k < count else 0.0
    here, there, c_next, v_next = lanes(c, r, 0), lanes(v, r, 0), turn(c, 0), turn(v, 0)
    for k in range(count):
        at = slice(128 * k, 128 * k + 128)
        c_later, v_later = turn(c, k + 1), turn(v, k + 1)
        z = 0.5 * (here + jnp.where(lane == 127, c_later, c_next))
        flux = z * (jnp.where(lane == 127, v_later, v_next) - there)
        z_turned, flux_turned = pltpu.roll(z, 1, 1), pltpu.roll(flux, 1, 1)
        if k == 0:
            z_before, flux_before = 0.5 * here, 0.5 * here * there
        above, below = 0.5 * (here + lanes(c, r + 1, k)), 0.5 * (here + lanes(c, r - 1, k))
        fa[r, :, at], fz[r, :, at] = above, z
        diagonal[r, :, at] = above + below + (z + jnp.where(lane == 0, z_before, z_turned))
        a = above * (there - lanes(v, r + 1, k)) + below * (there - lanes(v, r - 1, k))
        a = a + (jnp.where(lane == 0, flux_before, flux_turned) - flux)
        left_over[r, :, at] = s[r, :, at] - a
        if k + 1 < count:
            here, there = lanes(c, r, k + 1), lanes(v, r, k + 1)
        c_next, v_next, z_before, flux_before = c_later, v_later, z_turned, flux_turned


def first_face(c, fa):
    fa[0] = 0.5 * (c[0] + c[1])


def level_zero_own(p, d, m, left, right, v, me, de, fa, fz, diagonal, left_over):
    _, _, _, (low, high, _, _) = scalars()
    for r in range(14):
        a = r - 3
        if a < 0:
            v[r], me[r] = left[r] * low, left[3 + r] * low
            de[r] = left[5 + r] * low if r > 0 else jnp.zeros((16, 1024), F32)
        elif a < 8:
            v[r], me[r], de[r] = p[a], m[a], d[a]
        else:
            v[r], me[r] = right[a - 8] * high, right[a - 5] * high
            de[r] = right[a - 2] * high if a < 10 else jnp.zeros((16, 1024), F32)
    first_face(me, fa)
    over_rows(1, 13, 2, lambda r: across(r, v, me, de, fa, fz, diagonal, left_over))


def level_zero(
    own_v, own_me, own_de, own_fa, own_fz, own_diagonal, own_left_over, c1, nleft, nright,
    field, s1, up, down, me, de, fa, fz, fb, w, v, u, beside, diagonal, left_over,
):
    _, _, _, (_, _, nlow, nhigh) = scalars()
    at = iota((8, 1024), 0)
    for r in (0, 13):
        beside[r] = me[r] = de[r] = jnp.zeros((8, 1024), F32)
    for r in range(1, 13):
        x, y = nright[r - 1] * nhigh, nleft[r - 1] * nlow
        beside[r] = jnp.where(at < 3, x, jnp.where(at >= 5, y, 0.0))
        x3, y3 = pltpu.roll(x, 5, 0), pltpu.roll(y, 3, 0)
        me[r] = jnp.where(at < 3, x3, jnp.where(at >= 5, y3, 0.0))
        x6, y6 = pltpu.roll(x, 2, 0), pltpu.roll(y, 6, 0)
        de[r] = jnp.where(at < 2, x6, jnp.where(at >= 6, y6, 0.0))
    first_face(me, fa)
    pairs = [(own_v, beside), (own_me, me), (own_diagonal, diagonal), (own_left_over, left_over)]

    def one(r):
        across(r, beside, me, de, fa, fz, diagonal, left_over)
        for k in range(8):
            lane = slice(128 * k, 128 * k + 128)
            there, here, total, rest = [lanes(x, r, k) for x in pairs]
            y = 0.5 * (here + following(here, 0))
            flux = y * (following(there, 0) - there)
            total = total + (y + preceding(y, 0))
            factor = jnp.where(here > 0.0, OMEGA / total, 0.0)
            fb[r, :, lane], w[r, :, lane] = y, factor
            u[r, :, lane] = there + factor * (rest - (preceding(flux, 0) - flux))

    over_rows(1, 13, 2, one)
    me, de, fa, fz = (own_me, me), (own_de, de), (own_fa, fa), (own_fz, fz)
    sweep(u, v, de, me, fa, fb, fz, w, (2, 12), 3)
    field[...] = v[3:11, 0:16]

    def coarse(i, carry):
        r = 2 * i + 3
        x = residual_row(v, de, me, fa, fb, fz, r, 16)
        y = residual_row(v, de, me, fa, fb, fz, r + 1, 16)
        for k, a in enumerate(coarse_sum(x, y)):
            s1[i, :, 128 * k : 128 * k + 128] = 0.5 * a
        return carry

    lax.fori_loop(0, 4, coarse, 0)
    up[0:3], down[0:3] = s1[1:4], s1[0:3]
    up[3:7], down[3:7] = c1[...], c1[...]


def pack_one(s, c, left, right, to_left, to_right):
    _, _, _, (low, high, _, _) = scalars()
    at = iota((8, 512), 0)
    for r in range(1, 11):
        a = r - 4
        if a < 0:
            vc = left[3 + r] * low
            vs = left[r - 1] * low if r > 0 else jnp.zeros_like(vc)
        elif a < 4:
            vs, vc = s[a], c[a]
        else:
            vc = right[a - 1] * high
            vs = right[a - 4] * high if a < 7 else jnp.zeros_like(vc)
        to_left[r - 1] = jnp.where(at < 4, vc, pltpu.roll(vs, 4, 0))
        to_right[r - 1] = jnp.where(at >= 4, vc, pltpu.roll(vs, 4, 0))


def level_one(s, c, left, right, nleft, nright, f0, field, s2, up, down, se, ce, fa, fb, fz, w, v, u):
    _, _, _, (low, high, nlow, nhigh) = scalars()
    at = iota((8, 512), 0)
    for r in range(12):
        a = r - 4
        if a < 0:
            ce[r, 0:8] = left[3 + r] * low
            se[r, 0:8] = left[r - 1] * low if r > 0 else jnp.zeros((8, 512), F32)
        elif a < 4:
            se[r, 0:8], ce[r, 0:8] = s[a], c[a]
        else:
            ce[r, 0:8] = right[a - 1] * high
            se[r, 0:8] = right[a - 4] * high if a < 7 else jnp.zeros((8, 512), F32)
        if r in (0, 11):
            ce[r, 8:16] = se[r, 8:16] = jnp.zeros((8, 512), F32)
            continue
        x, y = nright[r - 1] * nhigh, nleft[r - 1] * nlow
        ce[r, 8:16] = jnp.where(at < 4, x, y)
        se[r, 8:16] = jnp.where(at < 4, pltpu.roll(x, 4, 0), pltpu.roll(y, 4, 0))
    faces(ce, (1, 11), fa, fb, fz, w, 5)

    for r in range(2, 10):
        u[r] = w[r] * se[r]
    sweep(u, v, se, ce, fa, fb, fz, w, (3, 9), 3)
    field[...] = v[4:8, 0:8]
    for i in range(2):
        r = 2 * i + 4
        x = residual_row(v, se, ce, fa, fb, fz, r, 8)
        y = residual_row(v, se, ce, fa, fb, fz, r + 1, 8)
        even, odd = coarse_sum(x, y, True)
        s2[i] = 0.5 * (even + pltpu.roll(odd, 4, 0))
    for r in range(3):
        for t in range(2):
            up[2 * r + t] = f0[5 + r, 8 * t : 8 * t + 8]
            down[2 * r + t] = f0[r, 8 * t : 8 * t + 8]
    for r in range(2):
        both = jnp.concatenate([field[2 * r], field[2 * r + 1]], axis=1)
        up[6 + r] = both
        down[6 + r] = both


def pack_up(f0, f1, left, right, to_left, to_right):
    _, _, _, (low, high, _, _) = scalars()
    at = iota((8, 1024), 0)

    def fine(r, side):
        if r < 3:
            return left[2 * r + side] * low
        if r < 11:
            return f0[r - 3, 8 * side : 8 * side + 8]
        return right[2 * (r - 11) + side] * high

    def pair(r):
        if r < 2:
            return left[6 + r] * low
        if r < 4:
            return jnp.concatenate([f1[2 * r - 4], f1[2 * r - 3]], axis=1)
        return right[2 + r] * high

    for t in range(6):
        to_left[t] = jnp.where(at < 4, fine(2 * t + 1, 0), pltpu.roll(fine(2 * t + 2, 0), 4, 0))
        to_right[t] = jnp.where(at >= 4, fine(2 * t + 1, 1), pltpu.roll(fine(2 * t + 2, 1), 4, 0))
    for t in range(3):
        to_left[6 + t] = jnp.where(at < 4, pair(2 * t), pltpu.roll(pair(2 * t + 1), 4, 0))
        to_right[6 + t] = jnp.where(at >= 4, pair(2 * t), pltpu.roll(pair(2 * t + 1), 4, 0))


def level_up(
    own_me, own_de, own_fa, own_fz, me, de, fa, fz, fb, w, se, ce, fa1, fb1, fz1, w1,
    f0, f1, left, right, nleft, nright, e2,
    out, res, v, u, v1, u1, kept, sent,
):
    _, _, _, (low, high, nlow, nhigh) = scalars()
    at = iota((8, 512), 0)
    half = iota((8, 128), 0)
    for r in range(12):
        if r < 4:
            f = left[6 + r // 2][:, 512 * (r % 2) : 512 * (r % 2) + 512] * low
        elif r < 8:
            f = f1[r - 4]
        else:
            f = right[2 + r // 2][:, 512 * (r % 2) : 512 * (r % 2) + 512] * high
        x = nright[6 + r // 4][:, 512 * (r % 2) : 512 * (r % 2) + 512] * nhigh
        y = nleft[6 + r // 4][:, 512 * (r % 2) : 512 * (r % 2) + 512] * nlow
        if r % 4 > 1:
            x, y = pltpu.roll(x, 4, 0), pltpu.roll(y, 4, 0)
        g = jnp.where(at < 4, x, y)
        e = e2[r // 2]
        own = widen_split(take_rows(e, 2 + half // 2))
        beside = widen_split(take_rows(e, jnp.where(half < 4, 6 + half // 2, (half - 4) // 2)))
        v1[r, 0:8] = f + jnp.where(ce[r, 0:8] > 0.0, own, 0.0)
        v1[r, 8:16] = g + jnp.where(ce[r, 8:16] > 0.0, beside, 0.0)
    sweep(v1, u1, se, ce, fa1, fb1, fz1, w1, (1, 11), 5)
    sweep(u1, v1, se, ce, fa1, fb1, fz1, w1, (2, 10), 4)
    zero = iota((8, 1024), 0)
    for r in range(14):
        if r < 3:
            f = [left[2 * r] * low, left[2 * r + 1] * low]
        elif r < 11:
            f = [f0[r - 3, 0:8], f0[r - 3, 8:16]]
        else:
            f = [right[2 * (r - 11)] * high, right[2 * (r - 11) + 1] * high]
        if r in (0, 13):
            f.append(jnp.zeros((8, 1024), F32))
        else:
            x, y = nright[(r - 1) // 2] * nhigh, nleft[(r - 1) // 2] * nlow
            if r % 2 == 0:
                x, y = pltpu.roll(x, 4, 0), pltpu.roll(y, 4, 0)
            f.append(jnp.where(zero < 3, x, jnp.where(zero >= 5, y, 0.0)))
        e = v1[(r + 5) // 2]
        pieces = (
            (e[0:8], half // 2),
            (e[0:8], 4 + half // 2),
            (e[8:16], jnp.where(half < 4, half // 2, 4 + half // 2)),
        )
        for t, (part, index) in enumerate(pieces):
            fine = widen(take_rows(part, index), 8)
            tile = slice(8 * t, 8 * t + 8)
            inside = own_me[r, tile] if t < 2 else me[r]
            v[r, tile] = f[t] + jnp.where(inside > 0.0, fine, 0.0)

    me, de, fa, fz = (own_me, me), (own_de, de), (own_fa, fa), (own_fz, fz)
    sweep(v, u, de, me, fa, fb, fz, w, (1, 13), 3)
    sweep(u, v, de, me, fa, fb, fz, w, (2, 12), 3)
    first = pltpu.make_async_copy(v.at[3:11, 0:16], out, sent.at[0])
    first.start()

    def final(r):
        for k, x in enumerate(residual_row(v, de, me, fa, fb, fz, r, 16)):
            kept[r - 3, :, 128 * k : 128 * k + 128] = x

    over_rows(3, 7, 2, final)
    second = pltpu.make_async_copy(kept.at[0:4], res.at[0:4], sent.at[1])
    second.start()
    over_rows(7, 11, 2, final)
    third = pltpu.make_async_copy(kept.at[4:8], res.at[4:8], sent.at[2])
    third.start()
    for copy in (first, second, third):
        copy.wait()


def shifted(x, step):
    zero = jnp.zeros((1,) + x.shape[1:], F32)
    return jnp.concatenate([x[1:], zero] if step > 0 else [zero, x[:-1]], axis=0)


class Whole:
    def __init__(self, c, cols, length):
        b, z = iota(c.shape, 1), iota(c.shape, 2)
        valid = (b < cols) & (z < length)
        self.fa = 0.5 * (c + shifted(c, 1))
        self.fa_below = 0.5 * (c + shifted(c, -1))
        self.fb = jnp.where(b < cols - 1, 0.5 * (c + following(c, 1)), 0.0)
        self.fz = jnp.where(z < length - 1, 0.5 * (c + following(c, 2)), 0.0)
        half = 0.5 * c
        self.ends = jnp.where(b == 0, half, 0.0) + jnp.where(b == cols - 1, half, 0.0)
        self.ends = self.ends + jnp.where(z == 0, half, 0.0) + jnp.where(z == length - 1, half, 0.0)
        diagonal = self.fa + self.fa_below + self.fb + preceding(self.fb, 1)
        diagonal = diagonal + self.fz + preceding(self.fz, 2) + self.ends
        self.w = jnp.where(valid, OMEGA / diagonal, 0.0)

    def operator(self, v):
        gb = self.fb * (following(v, 1) - v)
        gz = self.fz * (following(v, 2) - v)
        out = self.fa * (v - shifted(v, 1)) + self.fa_below * (v - shifted(v, -1)) + self.ends * v
        return out + (preceding(gb, 1) - gb) + (preceding(gz, 2) - gz)

    def sweep(self, v, s):
        return v + self.w * (s - self.operator(v))


def coarsen_whole(x):
    return jnp.stack([coarse_sum([x[a]], [x[a + 1]])[0] for a in range(0, x.shape[0], 2)])


def refine_row(x, cols_tiles, lanes_too):
    half = iota((8, 128), 0)
    tiles = []
    for t in range(cols_tiles):
        source = x[8 * (t // 2) : 8 * (t // 2) + 8]
        tile = take_rows(source, half // 2 + 4 * (t % 2))
        tiles.append(widen(tile, 1) if lanes_too else tile)
    return tiles[0] if cols_tiles == 1 else jnp.concatenate(tiles, axis=0)


def refine_whole(x, cols_tiles):
    rows = [refine_row(x[a], cols_tiles, True) for a in range(x.shape[0])]
    return jnp.stack([rows[a // 2] for a in range(2 * x.shape[0])])


def multiply(x, y):
    out = [[None] * 4 for _ in range(4)]
    for i in range(4):
        for j in range(4):
            for k in range(4):
                if x[i][k] is not None and y[k][j] is not None:
                    term = x[i][k] * y[k][j]
                    out[i][j] = term if out[i][j] is None else out[i][j] + term
    return out


def apply(x, y):
    out = []
    for i in range(4):
        total = None
        for k in range(4):
            if x[i][k] is not None:
                term = x[i][k] * y[k]
                total = term if total is None else total + term
        out.append(total)
    return out


def inverse(x):
    x = [[jnp.zeros((8, 128), F32) if e is None else e for e in line] for line in x]
    for k in range(4):
        pivot = 1.0 / x[k][k]
        line = [pivot if j == k else x[k][j] * pivot for j in range(4)]
        for i in range(4):
            if i != k:
                factor = x[i][k]
                x[i] = [-factor * pivot if j == k else x[i][j] - factor * line[j] for j in range(4)]
        x[k] = line
    return x


def each(x, move):
    return [[None if e is None else move(e) for e in line] for line in x]


def exact(s, c):
    length = 16
    lane = iota((8, 128), 1)
    row = iota((8, 128), 0)
    valid = lane < length

    def line(x, a, b):
        picked = jnp.take_along_axis(x[a], jnp.full((8, 128), b, jnp.int32), axis=0)
        return jnp.where(valid, picked, 0.0)

    cs = [line(c, k // 2, k % 2) for k in range(4)]
    rhs = [line(s, k // 2, k % 2) for k in range(4)]
    below = [[None] * 4 for _ in range(4)]
    above = [[None] * 4 for _ in range(4)]
    centre = [[None] * 4 for _ in range(4)]
    for k in range(4):
        here = cs[k]
        upper = 0.5 * (here + following(here, 1))
        lower = 0.5 * (here + preceding(here, 1))
        fa, fb = 0.5 * (here + cs[k ^ 2]), 0.5 * (here + cs[k ^ 1])
        diagonal = upper + lower + fa + fb + here
        centre[k][k] = jnp.where(valid, diagonal, 1.0)
        centre[k][k ^ 2], centre[k][k ^ 1] = -fa, -fb
        above[k][k] = jnp.where(lane < length - 1, -upper, 0.0)
        below[k][k] = jnp.where((lane > 0) & valid, -lower, 0.0)
    step = 1
    while step < length:
        ahead = lambda e, step=step: pltpu.roll(e, 128 - step, 1)
        behind = lambda e, step=step: pltpu.roll(e, step, 1)
        solved = inverse(centre)
        t, u, q = multiply(solved, below), multiply(solved, above), apply(solved, rhs)
        t_ahead, u_behind = each(t, ahead), each(u, behind)
        x, y = multiply(below, u_behind), multiply(above, t_ahead)
        centre = [
            [jnp.zeros((8, 128), F32) if centre[i][j] is None else centre[i][j] for j in range(4)]
            for i in range(4)
        ]
        centre = [[centre[i][j] - x[i][j] - y[i][j] for j in range(4)] for i in range(4)]
        x, y = apply(below, [behind(e) for e in q]), apply(above, [ahead(e) for e in q])
        rhs = [rhs[i] - x[i] - y[i] for i in range(4)]
        if 2 * step < length:
            below = each(multiply(below, each(t, behind)), lambda e: -e)
            above = each(multiply(above, each(u, ahead)), lambda e: -e)
        step *= 2
    solved = [jnp.where(valid, e, 0.0) for e in apply(inverse(centre), rhs)]
    return jnp.stack(
        [
            jnp.where(row == 0, solved[2 * a], jnp.where(row == 1, solved[2 * a + 1], 0.0))
            for a in range(2)
        ]
    )


def descend(s, c, cols, length):
    if c.shape[0] == 2:
        return exact(s, c)
    level = Whole(c, cols, length)
    v = level.w * s
    v = level.sweep(v, s)
    r = s - level.operator(v)
    e = descend(0.5 * coarsen_whole(r), 0.125 * coarsen_whole(c), cols // 2, length // 2)
    v = v + refine_whole(e, c.shape[1] // 8)
    v = level.sweep(v, s)
    return level.sweep(v, s)


def split_before(last, first_lane):
    lane = iota(last.shape, 1)
    return jnp.where(lane == 0, first_lane, pltpu.roll(last, 1, 1))


def split_after(first):
    lane = iota(first.shape, 1)
    return jnp.where(lane == 127, 0.0, pltpu.roll(first, 127, 1))


def split_operator(v, r, c, fa, fb, fz, ends):
    here = [lanes(v, r, k) for k in range(2)]
    after = [here[1], split_after(here[0])]
    gz = [lanes(fz, r, k) * (after[k] - here[k]) for k in range(2)]
    before = [split_before(gz[1], 0.5 * lanes(c, r, 0) * here[0]), gz[0]]
    out = []
    for k in range(2):
        gb = lanes(fb, r, k) * (following(here[k], 0) - here[k])
        a = lanes(fa, r, k) * (here[k] - lanes(v, r + 1, k)) + lanes(fa, r - 1, k) * (here[k] - lanes(v, r - 1, k))
        a = a + lanes(ends, r, k) * here[k]
        out.append(a + (preceding(gb, 0) - gb) + (before[k] - gz[k]))
    return out


def split_sweep(source, target, s, c, fa, fb, fz, ends, w, r):
    for k, a in enumerate(split_operator(source, r, c, fa, fb, fz, ends)):
        at = slice(128 * k, 128 * k + 128)
        target[r, :, at] = source[r, :, at] + w[r, :, at] * (s[r, :, at] - a)


def level_two(mine, other, s, c, v, fa, fb, fz, ends, w, s3, c3, u):
    _, _, core, _ = scalars()
    strips = mine.shape[0] // 16
    rows, cols = 32, 8 * strips
    first = iota((8, 128), 0) < 4
    edge = jnp.zeros((cols, 256), F32)
    for x in (c, v, u):
        x[0], x[rows + 1] = edge, edge

    def place(target, r, y, near, far):
        target[r, 8 * y : 8 * y + 8, 0:128] = jnp.where(first, near, pltpu.roll(far, 4, 0))
        target[r, 8 * y : 8 * y + 8, 128:256] = jnp.where(first, pltpu.roll(near, 4, 0), far)

    def load(k):
        for y in range(strips):
            at = k * strips + y
            for i in range(2):
                r = 2 * k + i + 1
                for n, target in enumerate((s, c)):
                    x, z = mine[at, n, i], other[at, n, i]
                    place(target, r, y, jnp.where(core == 0, x, z), jnp.where(core == 0, z, x))

    over_rows(0, rows // 2, 2, load)
    fa[0] = 0.5 * c[1]
    b = iota((cols, 128), 0)

    def one(r):
        here = [lanes(c, r, k) for k in range(2)]
        z = [0.5 * (here[0] + here[1]), 0.5 * (here[1] + split_after(here[0]))]
        before = [split_before(z[1], 0.5 * here[0]), z[0]]
        for k in range(2):
            at = slice(128 * k, 128 * k + 128)
            x, h = here[k], 0.5 * here[k]
            y = jnp.where(b == cols - 1, 0.0, 0.5 * (x + following(x, 0)))
            e = jnp.where((b == 0) | (b == cols - 1), h, 0.0)
            above = h + 0.5 * lanes(c, r + 1, k)
            diagonal = above + (h + 0.5 * lanes(c, r - 1, k)) + (y + preceding(y, 0)) + (z[k] + before[k]) + e
            factor = OMEGA / diagonal
            fa[r, :, at], fb[r, :, at], fz[r, :, at] = above, y, z[k]
            ends[r, :, at], w[r, :, at] = e, factor
            u[r, :, at] = factor * s[r, :, at]

    over_rows(1, rows + 1, 8, one)
    over_rows(1, rows + 1, 16, lambda r: split_sweep(u, v, s, c, fa, fb, fz, ends, w, r))

    def coarse(i):
        total = None
        for r in (2 * i + 1, 2 * i + 2):
            for k, a in enumerate(split_operator(v, r, c, fa, fb, fz, ends)):
                x = lanes(s, r, k) - a
                total = x if total is None else total + x
        s3[i] = 0.5 * half_columns(total)
        total = (lanes(c, 2 * i + 1, 0) + lanes(c, 2 * i + 1, 1)) + (lanes(c, 2 * i + 2, 0) + lanes(c, 2 * i + 2, 1))
        c3[i] = 0.125 * half_columns(total)

    over_rows(0, rows // 2, 4, coarse)


def coarse_levels(s3, c3, s, c, v, fa, fb, fz, ends, w, e2, e3, u, t):
    wide, narrow, _, _ = scalars()
    rows, cols = s.shape[0] - 2, s.shape[1]
    e3[...] = descend(s3[...], c3[...], cols // 2, 128)
    row = lambda step: jnp.clip(2 * wide + step, 0, rows - 1) + 1
    u[0], u[rows + 1], t[0], t[rows + 1] = v[0], v[0], v[0], v[0]
    for i in range(-2, 3):
        k = jnp.clip(wide + i, 0, rows // 2 - 1)
        e = refine_row(e3[k], cols // 8, False)
        for r in (2 * k + 1, 2 * k + 2):
            for half in range(2):
                at = slice(128 * half, 128 * half + 128)
                u[r, :, at] = v[r, :, at] + e
    for i in range(-3, 5):
        split_sweep(u, t, s, c, fa, fb, fz, ends, w, row(i))
    for i in range(-2, 4):
        split_sweep(t, u, s, c, fa, fb, fz, ends, w, row(i))
    for i in range(6):
        turned = pltpu.roll(u[row(i - 2)], lax.rem(cols + 2 - 4 * narrow, cols), 0)
        e2[i] = turned[0:8]


def moved(x, wide_step, narrow_step):
    w, y, k = [lax.axis_size(name) for name in AX]
    n = y * k
    pairs = [
        (i * n + j, ((i + wide_step) % w) * n + (j + narrow_step) % n)
        for i in range(w)
        for j in range(n)
    ]
    return lax.ppermute(x, AX, pairs)


def other_core(x):
    w, y, k = [lax.axis_size(name) for name in AX]
    return lax.ppermute(x, AX, [(i, i ^ 1) for i in range(w * y * k)])


def gathered(s2, c2):
    both = jnp.stack([s2, c2])
    chips = lax.axis_size("wide") * lax.axis_size("ny")
    return lax.all_to_all(jnp.broadcast_to(both[None], (chips,) + both.shape), ("wide", "ny"), 0, 0, tiled=True)


def per_device(p, d, m):
    up = jnp.concatenate([p[5:8], m[5:8], d[6:8]], axis=0)
    down = jnp.concatenate([p[0:3], m[0:3], d[0:2]], axis=0)
    left, right = moved(up, 1, 0), moved(down, -1, 0)
    c1, c2 = call(coarse_coefficients, [(4, 8, 512), (2, 8, 128)], [], m)
    to_left, to_right = call(pack_zero, [(12, 8, 1024)] * 2, [], p, d, m, left, right)
    nleft, nright = moved(to_right, 0, 1), moved(to_left, 0, -1)
    big, own, halo = (14, 24, 1024), (14, 16, 1024), (14, 8, 1024)
    alone = call(level_zero_own, [own] * 7, [], p, d, m, left, right, flops=20_000_000)
    f0, s1, up, down, *zero = call(
        level_zero,
        [(8, 16, 1024), (4, 8, 512)] + [(7, 8, 512)] * 2 + [halo] * 4 + [big] * 2,
        [big] * 2 + [halo] * 3,
        *alone, c1, nleft, nright,
        flops=30_000_000,
    )
    zero = [*alone[1:5], *zero]
    left1, right1 = moved(up, 1, 0), moved(down, -1, 0)
    to_left, to_right = call(pack_one, [(10, 8, 512)] * 2, [], s1, c1, left1, right1)
    nleft1, nright1 = moved(to_right, 0, 1), moved(to_left, 0, -1)
    mid = (12, 16, 512)
    f1, s2, up, down, *one = call(
        level_one,
        [(4, 8, 512), (2, 8, 128)] + [(8, 8, 1024)] * 2 + [mid] * 6,
        [mid] * 2,
        s1, c1, left1, right1, nleft1, nright1, f0,
        flops=10_000_000,
    )
    hleft, hright = moved(up, 1, 0), moved(down, -1, 0)
    mine = gathered(s2, c2)
    other = other_core(mine)
    whole, small = (34, 32, 256), (16, 16, 128)
    *two, s3, c3 = call(level_two, [whole] * 8 + [small] * 2, [whole], mine, other, flops=1000)
    s3, hleft, hright = lax.optimization_barrier((s3, hleft, hright))
    to_left, to_right = call(pack_up, [(9, 8, 1024)] * 2, [], f0, f1, hleft, hright)
    nhleft, nhright = moved(to_right, 0, 1), moved(to_left, 0, -1)
    (e2,) = call(coarse_levels, [(6, 8, 256)], [small] + [whole] * 2, s3, c3, *two, flops=1000)
    return call(
        level_up,
        [(8, 16, 1024)] * 2,
        [big] * 2 + [mid] * 2 + [(8, 16, 1024)],
        *zero, *one, f0, f1, hleft, hright, nhleft, nhright, e2,
        flops=30_000_000,
        copies=3,
    )


def solution(mesh):
    wide, narrow = mesh.axis_names
    devices = mesh.devices.reshape(mesh.shape[wide], mesh.shape[narrow] // 2, 2)
    spec = P("wide", ("ny", "core"), None)
    return jax.shard_map(
        lambda p, d, m: tuple(per_device(p, d, m)),
        mesh=Mesh(devices, AX),
        in_specs=(spec,) * 3,
        out_specs=(spec,) * 2,
        check_vma=False,
    )
```

```python
import math

import jax
import jax.numpy as jnp
from jax import lax
from jax.experimental import pallas as pl
from jax.experimental.pallas import tpu as pltpu
from jax.sharding import Mesh, PartitionSpec as P

OMEGA = 0.8
AX = ("wide", "ny", "core")
F32 = jnp.float32
SPARE = 4 * 1024 * 1024


def iota(shape, dim):
    return lax.broadcasted_iota(jnp.int32, shape, dim)


def following(x, dim):
    return pltpu.roll(x, x.shape[dim] - 1, dim)


def preceding(x, dim):
    return pltpu.roll(x, 1, dim)


def lanes(x, r, k):
    if isinstance(x, tuple):
        return jnp.concatenate([lanes(part, r, k) for part in x], axis=0)
    return x[r, :, 128 * k : 128 * k + 128]


def row_operator(v, r, c, fa, fb, fz):
    count = v.shape[2] // 128
    lane = iota((v.shape[1], 128), 1)
    here = lanes(v, r, 0)
    turned = pltpu.roll(here, 127, 1)
    out = []
    for k in range(count):
        if k + 1 < count:
            later = lanes(v, r, k + 1)
            later_turned = pltpu.roll(later, 127, 1)
        else:
            later, later_turned = None, 0.0
        gz = lanes(fz, r, k) * (jnp.where(lane == 127, later_turned, turned) - here)
        gz_turned = pltpu.roll(gz, 1, 1)
        if k == 0:
            gz_before = 0.5 * lanes(c, r, 0) * here
        gb = lanes(fb, r, k) * (following(here, 0) - here)
        a = lanes(fa, r, k) * (here - lanes(v, r + 1, k)) + lanes(fa, r - 1, k) * (here - lanes(v, r - 1, k))
        a = a + (preceding(gb, 0) - gb) + (jnp.where(lane == 0, gz_before, gz_turned) - gz)
        out.append(a)
        here, turned, gz_before = later, later_turned, gz_turned
    return out


def row_faces(r, c, fa, fb, fz, w):
    count = c.shape[2] // 128
    cols = c.shape[1]
    lane = iota((cols, 128), 1)
    here = lanes(c, r, 0)
    turned = pltpu.roll(here, 127, 1)
    for k in range(count):
        if k + 1 < count:
            later = lanes(c, r, k + 1)
            later_turned = pltpu.roll(later, 127, 1)
        else:
            later, later_turned = None, 0.0
        at = slice(128 * k, 128 * k + 128)
        z = 0.5 * (here + jnp.where(lane == 127, later_turned, turned))
        z_turned = pltpu.roll(z, 1, 1)
        if k == 0:
            z_before = 0.5 * here
        y = 0.5 * (here + following(here, 0))
        diagonal = 0.5 * (here + lanes(c, r - 1, k)) + 0.5 * (here + lanes(c, r + 1, k))
        diagonal = diagonal + (y + preceding(y, 0)) + (z + jnp.where(lane == 0, z_before, z_turned))
        fa[r, :, at] = 0.5 * (here + lanes(c, r + 1, k))
        fb[r, :, at], fz[r, :, at] = y, z
        w[r, :, at] = jnp.where(here > 0.0, OMEGA / diagonal, 0.0)
        here, turned, z_before = later, later_turned, z_turned


def over_rows(lo, hi, step, body):
    whole = (hi - lo) // step

    def some(i, carry):
        for j in range(step):
            body(lo + i * step + j)
        return carry

    if whole > 1:
        lax.fori_loop(0, whole, some, 0)
        lo = lo + whole * step
    for r in range(lo, hi):
        body(r)


def half_compress(low, high, dim):
    length = low.shape[dim]
    at = iota(low.shape, dim)
    index = (2 * at) % length
    first = jnp.take_along_axis(low, index, axis=dim)
    if high is None:
        return jnp.where(at < length // 2, first, 0.0)
    return jnp.where(at < length // 2, first, jnp.take_along_axis(high, index, axis=dim))


def half_columns(x):
    x = x + following(x, 0)
    tiles = x.shape[0] // 8
    part = lambda t: x[8 * t : 8 * t + 8]
    if tiles == 1:
        return half_compress(x, None, 0)
    x = [half_compress(part(2 * t), part(2 * t + 1), 0) for t in range(tiles // 2)]
    return x[0] if len(x) == 1 else jnp.concatenate(x, axis=0)


def coarse_sum(first, second, split=False):
    halves = [half_columns(x + y) for x, y in zip(first, second)]
    halves = [x + following(x, 1) for x in halves]
    if split:
        lane = iota((8, 128), 1)
        out = []
        for odd in range(2):
            index = (4 * lane + 2 * odd) % 128
            picked = jnp.take_along_axis(halves[0], index, axis=1)
            for k in range(1, 4):
                picked = jnp.where(lane >= 32 * k, jnp.take_along_axis(halves[k], index, axis=1), picked)
            out.append(picked)
        return out
    if len(halves) == 1:
        return [by_tile(halves[0], None)]
    return [by_tile(halves[k], halves[k + 1]) for k in range(0, len(halves), 2)]


def by_tile(low, high):
    tiles = [
        half_compress(low[8 * t : 8 * t + 8], None if high is None else high[8 * t : 8 * t + 8], 1)
        for t in range(low.shape[0] // 8)
    ]
    return tiles[0] if len(tiles) == 1 else jnp.concatenate(tiles, axis=0)


def blocks_of(x):
    return [x[:, 128 * k : 128 * k + 128] for k in range(x.shape[1] // 128)]


def repeat_lanes(x, block):
    source = block // 2
    index = iota((8, 128), 1) // 2 + 64 * (block % 2)
    return jnp.take_along_axis(x[:, 128 * source : 128 * source + 128], index, axis=1)


def take_rows(x, index):
    pieces = [
        jnp.take_along_axis(x[:, k : k + 128], index, axis=0) for k in range(0, x.shape[1], 128)
    ]
    return pieces[0] if len(pieces) == 1 else jnp.concatenate(pieces, axis=1)


def widen(x, blocks):
    pieces = [repeat_lanes(x, k) for k in range(blocks)]
    return pieces[0] if len(pieces) == 1 else jnp.concatenate(pieces, axis=1)


def widen_split(x):
    lane = iota((8, 128), 1)
    pieces = []
    for k in range(4):
        index = 32 * k + lane // 4
        even = jnp.take_along_axis(x[:, :128], index, axis=1)
        odd = jnp.take_along_axis(x[:, 128:], index, axis=1)
        pieces.append(jnp.where(lane // 2 % 2 == 0, even, odd))
    return jnp.concatenate(pieces, axis=1)


def scalars():
    wide, ny, core = lax.axis_index("wide"), lax.axis_index("ny"), lax.axis_index("core")
    sizes = [lax.axis_size(name) for name in AX]
    narrow = ny * sizes[2] + core
    inside = [
        jnp.where(flag, 1.0, 0.0).astype(F32)
        for flag in (wide > 0, wide < sizes[0] - 1, narrow > 0, narrow < sizes[1] * sizes[2] - 1)
    ]
    return wide, narrow, core, inside


def call(kernel, outs, scratch, *args, flops=1_000_000, copies=0):
    vmem = pl.BlockSpec(memory_space=pltpu.VMEM)
    size = 4 * sum(a.size for a in args)
    held = size + 4 * sum(math.prod(s) for s in outs + scratch)
    return pl.pallas_call(
        kernel,
        out_shape=[jax.ShapeDtypeStruct(s, F32) for s in outs],
        in_specs=[vmem] * len(args),
        out_specs=[pl.BlockSpec(memory_space=pltpu.HBM) if copies else vmem] * len(outs),
        scratch_shapes=[pltpu.VMEM(s, F32) for s in scratch] + [pltpu.SemaphoreType.DMA((copies,))] * (copies > 0),
        compiler_params=pltpu.CompilerParams(vmem_limit_bytes=held + SPARE),
        cost_estimate=pl.CostEstimate(flops=flops, bytes_accessed=0 if flops == 1000 else size, transcendentals=0),
    )(*args)


def coarse_coefficients(m, c1, c2):
    for i in range(4):
        x = coarse_sum(blocks_of(m[2 * i]), blocks_of(m[2 * i + 1]))
        for k, a in enumerate(x):
            c1[i, :, 128 * k : 128 * k + 128] = 0.125 * a
    for i in range(2):
        even, odd = coarse_sum(blocks_of(c1[2 * i]), blocks_of(c1[2 * i + 1]), True)
        c2[i] = 0.125 * (even + pltpu.roll(odd, 4, 0))


def columns_zero(vp, vm, vd, side):
    at = iota((8, 1024), 0)
    if side == 0:
        vm, vd = pltpu.roll(vm, 3, 0), pltpu.roll(vd, 6, 0)
        return jnp.where(at < 3, vp, jnp.where(at < 6, vm, vd))
    vm, vd = pltpu.roll(vm, 5, 0), pltpu.roll(vd, 2, 0)
    return jnp.where(at >= 5, vp, jnp.where(at >= 2, vm, vd))


def pack_zero_own(p, d, m, to_left, to_right):
    for a in range(8):
        for side, out in ((0, to_left), (1, to_right)):
            tile = slice(8 * side, 8 * side + 8)
            out[a] = columns_zero(p[a, tile], m[a, tile], d[a, tile], side)


def pack_zero_edge(left, right, to_left, to_right):
    _, _, _, (low, high, _, _) = scalars()
    for side, out in ((0, to_left), (1, to_right)):
        tile = slice(8 * side, 8 * side + 8)
        for i in range(2):
            out[i] = columns_zero(left[1 + i, tile], left[4 + i, tile], left[6 + i, tile], side) * low
            out[2 + i] = columns_zero(right[i, tile], right[3 + i, tile], right[6 + i, tile], side) * high


def faces(c, rows, fa, fb, fz, w, step):
    for k in range(c.shape[2] // 128):
        at = slice(128 * k, 128 * k + 128)
        fa[rows[0] - 1, :, at] = 0.5 * (c[rows[0] - 1, :, at] + c[rows[0], :, at])
    over_rows(rows[0], rows[1], step, lambda r: row_faces(r, c, fa, fb, fz, w))


def sweep(source, target, s, c, fa, fb, fz, w, rows, step):
    def one(r):
        for k, a in enumerate(row_operator(source, r, c, fa, fb, fz)):
            at = slice(128 * k, 128 * k + 128)
            target[r, :, at] = source[r, :, at] + w[r, :, at] * (lanes(s, r, k) - a)

    over_rows(rows[0], rows[1], step, one)


def residual_row(v, s, c, fa, fb, fz, r, cols):
    return [
        (lanes(s, r, k) - a)[0:cols]
        for k, a in enumerate(row_operator(v, r, c, fa, fb, fz))
    ]


def across(r, v, c, s, fa, fz, diagonal, left_over):
    lane = iota((c.shape[1], 128), 1)
    count = c.shape[2] // 128
    turn = lambda x, k: pltpu.roll(lanes(x, r, k), 127, 1) if k < count else 0.0
    here, there, c_next, v_next = lanes(c, r, 0), lanes(v, r, 0), turn(c, 0), turn(v, 0)
    for k in range(count):
        at = slice(128 * k, 128 * k + 128)
        c_later, v_later = turn(c, k + 1), turn(v, k + 1)
        z = 0.5 * (here + jnp.where(lane == 127, c_later, c_next))
        flux = z * (jnp.where(lane == 127, v_later, v_next) - there)
        z_turned, flux_turned = pltpu.roll(z, 1, 1), pltpu.roll(flux, 1, 1)
        if k == 0:
            z_before, flux_before = 0.5 * here, 0.5 * here * there
        above, below = 0.5 * (here + lanes(c, r + 1, k)), 0.5 * (here + lanes(c, r - 1, k))
        fa[r, :, at], fz[r, :, at] = above, z
        diagonal[r, :, at] = above + below + (z + jnp.where(lane == 0, z_before, z_turned))
        a = above * (there - lanes(v, r + 1, k)) + below * (there - lanes(v, r - 1, k))
        a = a + (jnp.where(lane == 0, flux_before, flux_turned) - flux)
        left_over[r, :, at] = s[r, :, at] - a
        if k + 1 < count:
            here, there = lanes(c, r, k + 1), lanes(v, r, k + 1)
        c_next, v_next, z_before, flux_before = c_later, v_later, z_turned, flux_turned


def first_face(c, fa):
    fa[0] = 0.5 * (c[0] + c[1])


def level_zero_own(p, d, m, left, right, v, me, de, fa, fz, diagonal, left_over):
    _, _, _, (low, high, _, _) = scalars()
    for r in range(14):
        a = r - 3
        if a < 0:
            v[r], me[r] = left[r] * low, left[3 + r] * low
            de[r] = left[5 + r] * low if r > 0 else jnp.zeros((16, 1024), F32)
        elif a < 8:
            v[r], me[r], de[r] = p[a], m[a], d[a]
        else:
            v[r], me[r] = right[a - 8] * high, right[a - 5] * high
            de[r] = right[a - 2] * high if a < 10 else jnp.zeros((16, 1024), F32)
    first_face(me, fa)
    over_rows(1, 13, 2, lambda r: across(r, v, me, de, fa, fz, diagonal, left_over))


def level_zero(
    own_v, own_me, own_de, own_fa, own_fz, own_diagonal, own_left_over, c1, nleft, nright, nleft_edge, nright_edge,
    field, s1, up, down, me, de, fa, fz, fb, w, v, u, beside, diagonal, left_over,
):
    _, _, _, (_, _, nlow, nhigh) = scalars()
    at = iota((8, 1024), 0)
    for r in (0, 13):
        beside[r] = me[r] = de[r] = jnp.zeros((8, 1024), F32)
    for r in range(1, 13):
        if 3 <= r < 11:
            x, y = nright[r - 3] * nhigh, nleft[r - 3] * nlow
        else:
            e = r - 1 if r < 3 else r - 9
            x, y = nright_edge[e] * nhigh, nleft_edge[e] * nlow
        beside[r] = jnp.where(at < 3, x, jnp.where(at >= 5, y, 0.0))
        x3, y3 = pltpu.roll(x, 5, 0), pltpu.roll(y, 3, 0)
        me[r] = jnp.where(at < 3, x3, jnp.where(at >= 5, y3, 0.0))
        x6, y6 = pltpu.roll(x, 2, 0), pltpu.roll(y, 6, 0)
        de[r] = jnp.where(at < 2, x6, jnp.where(at >= 6, y6, 0.0))
    first_face(me, fa)
    pairs = [(own_v, beside), (own_me, me), (own_diagonal, diagonal), (own_left_over, left_over)]

    def one(r):
        across(r, beside, me, de, fa, fz, diagonal, left_over)
        for k in range(8):
            lane = slice(128 * k, 128 * k + 128)
            there, here, total, rest = [lanes(x, r, k) for x in pairs]
            y = 0.5 * (here + following(here, 0))
            flux = y * (following(there, 0) - there)
            total = total + (y + preceding(y, 0))
            factor = jnp.where(here > 0.0, OMEGA / total, 0.0)
            fb[r, :, lane], w[r, :, lane] = y, factor
            u[r, :, lane] = there + factor * (rest - (preceding(flux, 0) - flux))

    over_rows(1, 13, 2, one)
    me, de, fa, fz = (own_me, me), (own_de, de), (own_fa, fa), (own_fz, fz)
    sweep(u, v, de, me, fa, fb, fz, w, (2, 12), 3)
    field[...] = v[3:11, 0:16]

    def coarse(i, carry):
        r = 2 * i + 3
        x = residual_row(v, de, me, fa, fb, fz, r, 16)
        y = residual_row(v, de, me, fa, fb, fz, r + 1, 16)
        for k, a in enumerate(coarse_sum(x, y)):
            s1[i, :, 128 * k : 128 * k + 128] = 0.5 * a
        return carry

    lax.fori_loop(0, 4, coarse, 0)
    up[0:3], down[0:3] = s1[1:4], s1[0:3]
    up[3:7], down[3:7] = c1[...], c1[...]


def pack_one(s, c, left, right, to_left, to_right):
    _, _, _, (low, high, _, _) = scalars()
    at = iota((8, 512), 0)
    for r in range(1, 11):
        a = r - 4
        if a < 0:
            vc = left[3 + r] * low
            vs = left[r - 1] * low if r > 0 else jnp.zeros_like(vc)
        elif a < 4:
            vs, vc = s[a], c[a]
        else:
            vc = right[a - 1] * high
            vs = right[a - 4] * high if a < 7 else jnp.zeros_like(vc)
        to_left[r - 1] = jnp.where(at < 4, vc, pltpu.roll(vs, 4, 0))
        to_right[r - 1] = jnp.where(at >= 4, vc, pltpu.roll(vs, 4, 0))


def level_one(s, c, left, right, nleft, nright, f0, field, s2, up, down, se, ce, fa, fb, fz, w, v, u):
    _, _, _, (low, high, nlow, nhigh) = scalars()
    at = iota((8, 512), 0)
    for r in range(12):
        a = r - 4
        if a < 0:
            ce[r, 0:8] = left[3 + r] * low
            se[r, 0:8] = left[r - 1] * low if r > 0 else jnp.zeros((8, 512), F32)
        elif a < 4:
            se[r, 0:8], ce[r, 0:8] = s[a], c[a]
        else:
            ce[r, 0:8] = right[a - 1] * high
            se[r, 0:8] = right[a - 4] * high if a < 7 else jnp.zeros((8, 512), F32)
        if r in (0, 11):
            ce[r, 8:16] = se[r, 8:16] = jnp.zeros((8, 512), F32)
            continue
        x, y = nright[r - 1] * nhigh, nleft[r - 1] * nlow
        ce[r, 8:16] = jnp.where(at < 4, x, y)
        se[r, 8:16] = jnp.where(at < 4, pltpu.roll(x, 4, 0), pltpu.roll(y, 4, 0))
    faces(ce, (1, 11), fa, fb, fz, w, 5)

    for r in range(2, 10):
        u[r] = w[r] * se[r]
    sweep(u, v, se, ce, fa, fb, fz, w, (3, 9), 3)
    field[...] = v[4:8, 0:8]
    for i in range(2):
        r = 2 * i + 4
        x = residual_row(v, se, ce, fa, fb, fz, r, 8)
        y = residual_row(v, se, ce, fa, fb, fz, r + 1, 8)
        even, odd = coarse_sum(x, y, True)
        s2[i] = 0.5 * (even + pltpu.roll(odd, 4, 0))
    for r in range(3):
        for t in range(2):
            up[2 * r + t] = f0[5 + r, 8 * t : 8 * t + 8]
            down[2 * r + t] = f0[r, 8 * t : 8 * t + 8]
    for r in range(2):
        both = jnp.concatenate([field[2 * r], field[2 * r + 1]], axis=1)
        up[6 + r] = both
        down[6 + r] = both


def two_rows(x, y, side):
    at = iota((8, 1024), 0)
    return jnp.where(at < 4 if side == 0 else at >= 4, x, pltpu.roll(y, 4, 0))


def pack_up_own(f0, f1, to_left, to_right):
    for side, out in ((0, to_left), (1, to_right)):
        tile = slice(8 * side, 8 * side + 8)
        for t in range(4):
            out[t] = two_rows(f0[2 * t, tile], f0[2 * t + 1, tile], side)
        pair = [jnp.concatenate([f1[2 * k], f1[2 * k + 1]], axis=1) for k in range(2)]
        out[4] = two_rows(pair[0], pair[1], side)


def pack_up_edge(left, right, to_left, to_right):
    _, _, _, (low, high, _, _) = scalars()
    for side, out in ((0, to_left), (1, to_right)):
        out[0] = two_rows(left[2 + side], left[4 + side], side) * low
        out[1] = two_rows(right[side], right[2 + side], side) * high
        out[2] = two_rows(left[6], left[7], side) * low
        out[3] = two_rows(right[6], right[7], side) * high


def tile_up(own, edge, t):
    if t in (0, 5, 6, 8):
        return edge[(0, 5, 6, 8).index(t)]
    return own[4 if t == 7 else t - 1]


def level_up(
    own_me, own_de, own_fa, own_fz, me, de, fa, fz, fb, w, se, ce, fa1, fb1, fz1, w1,
    f0, f1, left, right, nleft, nright, nleft_edge, nright_edge, e2,
    out, res, v, u, v1, u1, kept, sent,
):
    _, _, _, (low, high, nlow, nhigh) = scalars()
    at = iota((8, 512), 0)
    half = iota((8, 128), 0)
    for r in range(12):
        if r < 4:
            f = left[6 + r // 2][:, 512 * (r % 2) : 512 * (r % 2) + 512] * low
        elif r < 8:
            f = f1[r - 4]
        else:
            f = right[2 + r // 2][:, 512 * (r % 2) : 512 * (r % 2) + 512] * high
        half_tile = slice(512 * (r % 2), 512 * (r % 2) + 512)
        x = tile_up(nright, nright_edge, 6 + r // 4)[:, half_tile] * nhigh
        y = tile_up(nleft, nleft_edge, 6 + r // 4)[:, half_tile] * nlow
        if r % 4 > 1:
            x, y = pltpu.roll(x, 4, 0), pltpu.roll(y, 4, 0)
        g = jnp.where(at < 4, x, y)
        e = e2[r // 2]
        own = widen_split(take_rows(e, 2 + half // 2))
        beside = widen_split(take_rows(e, jnp.where(half < 4, 6 + half // 2, (half - 4) // 2)))
        v1[r, 0:8] = f + jnp.where(ce[r, 0:8] > 0.0, own, 0.0)
        v1[r, 8:16] = g + jnp.where(ce[r, 8:16] > 0.0, beside, 0.0)
    sweep(v1, u1, se, ce, fa1, fb1, fz1, w1, (1, 11), 5)
    sweep(u1, v1, se, ce, fa1, fb1, fz1, w1, (2, 10), 4)
    zero = iota((8, 1024), 0)
    for r in range(14):
        if r < 3:
            f = [left[2 * r] * low, left[2 * r + 1] * low]
        elif r < 11:
            f = [f0[r - 3, 0:8], f0[r - 3, 8:16]]
        else:
            f = [right[2 * (r - 11)] * high, right[2 * (r - 11) + 1] * high]
        if r in (0, 13):
            f.append(jnp.zeros((8, 1024), F32))
        else:
            t = (r - 1) // 2
            x, y = tile_up(nright, nright_edge, t) * nhigh, tile_up(nleft, nleft_edge, t) * nlow
            if r % 2 == 0:
                x, y = pltpu.roll(x, 4, 0), pltpu.roll(y, 4, 0)
            f.append(jnp.where(zero < 3, x, jnp.where(zero >= 5, y, 0.0)))
        e = v1[(r + 5) // 2]
        pieces = (
            (e[0:8], half // 2),
            (e[0:8], 4 + half // 2),
            (e[8:16], jnp.where(half < 4, half // 2, 4 + half // 2)),
        )
        for t, (part, index) in enumerate(pieces):
            fine = widen(take_rows(part, index), 8)
            tile = slice(8 * t, 8 * t + 8)
            inside = own_me[r, tile] if t < 2 else me[r]
            v[r, tile] = f[t] + jnp.where(inside > 0.0, fine, 0.0)

    me, de, fa, fz = (own_me, me), (own_de, de), (own_fa, fa), (own_fz, fz)
    sweep(v, u, de, me, fa, fb, fz, w, (1, 13), 3)
    sweep(u, v, de, me, fa, fb, fz, w, (2, 12), 3)
    first = pltpu.make_async_copy(v.at[3:11, 0:16], out, sent.at[0])
    first.start()

    def final(r):
        for k, x in enumerate(residual_row(v, de, me, fa, fb, fz, r, 16)):
            kept[r - 3, :, 128 * k : 128 * k + 128] = x

    over_rows(3, 7, 2, final)
    second = pltpu.make_async_copy(kept.at[0:4], res.at[0:4], sent.at[1])
    second.start()
    over_rows(7, 11, 2, final)
    third = pltpu.make_async_copy(kept.at[4:8], res.at[4:8], sent.at[2])
    third.start()
    for copy in (first, second, third):
        copy.wait()


def shifted(x, step):
    zero = jnp.zeros((1,) + x.shape[1:], F32)
    return jnp.concatenate([x[1:], zero] if step > 0 else [zero, x[:-1]], axis=0)


class Whole:
    def __init__(self, c, cols, length):
        b, z = iota(c.shape, 1), iota(c.shape, 2)
        valid = (b < cols) & (z < length)
        self.fa = 0.5 * (c + shifted(c, 1))
        self.fa_below = 0.5 * (c + shifted(c, -1))
        self.fb = jnp.where(b < cols - 1, 0.5 * (c + following(c, 1)), 0.0)
        self.fz = jnp.where(z < length - 1, 0.5 * (c + following(c, 2)), 0.0)
        half = 0.5 * c
        self.ends = jnp.where(b == 0, half, 0.0) + jnp.where(b == cols - 1, half, 0.0)
        self.ends = self.ends + jnp.where(z == 0, half, 0.0) + jnp.where(z == length - 1, half, 0.0)
        diagonal = self.fa + self.fa_below + self.fb + preceding(self.fb, 1)
        diagonal = diagonal + self.fz + preceding(self.fz, 2) + self.ends
        self.w = jnp.where(valid, OMEGA / diagonal, 0.0)

    def operator(self, v):
        gb = self.fb * (following(v, 1) - v)
        gz = self.fz * (following(v, 2) - v)
        out = self.fa * (v - shifted(v, 1)) + self.fa_below * (v - shifted(v, -1)) + self.ends * v
        return out + (preceding(gb, 1) - gb) + (preceding(gz, 2) - gz)

    def sweep(self, v, s):
        return v + self.w * (s - self.operator(v))


def coarsen_whole(x):
    return jnp.stack([coarse_sum([x[a]], [x[a + 1]])[0] for a in range(0, x.shape[0], 2)])


def refine_row(x, cols_tiles, lanes_too):
    half = iota((8, 128), 0)
    tiles = []
    for t in range(cols_tiles):
        source = x[8 * (t // 2) : 8 * (t // 2) + 8]
        tile = take_rows(source, half // 2 + 4 * (t % 2))
        tiles.append(widen(tile, 1) if lanes_too else tile)
    return tiles[0] if cols_tiles == 1 else jnp.concatenate(tiles, axis=0)


def refine_whole(x, cols_tiles):
    rows = [refine_row(x[a], cols_tiles, True) for a in range(x.shape[0])]
    return jnp.stack([rows[a // 2] for a in range(2 * x.shape[0])])


def multiply(x, y):
    out = [[None] * 4 for _ in range(4)]
    for i in range(4):
        for j in range(4):
            for k in range(4):
                if x[i][k] is not None and y[k][j] is not None:
                    term = x[i][k] * y[k][j]
                    out[i][j] = term if out[i][j] is None else out[i][j] + term
    return out


def apply(x, y):
    out = []
    for i in range(4):
        total = None
        for k in range(4):
            if x[i][k] is not None:
                term = x[i][k] * y[k]
                total = term if total is None else total + term
        out.append(total)
    return out


def inverse(x):
    x = [[jnp.zeros((8, 128), F32) if e is None else e for e in line] for line in x]
    for k in range(4):
        pivot = 1.0 / x[k][k]
        line = [pivot if j == k else x[k][j] * pivot for j in range(4)]
        for i in range(4):
            if i != k:
                factor = x[i][k]
                x[i] = [-factor * pivot if j == k else x[i][j] - factor * line[j] for j in range(4)]
        x[k] = line
    return x


def each(x, move):
    return [[None if e is None else move(e) for e in line] for line in x]


def exact(s, c):
    length = 16
    lane = iota((8, 128), 1)
    row = iota((8, 128), 0)
    valid = lane < length

    def line(x, a, b):
        picked = jnp.take_along_axis(x[a], jnp.full((8, 128), b, jnp.int32), axis=0)
        return jnp.where(valid, picked, 0.0)

    cs = [line(c, k // 2, k % 2) for k in range(4)]
    rhs = [line(s, k // 2, k % 2) for k in range(4)]
    below = [[None] * 4 for _ in range(4)]
    above = [[None] * 4 for _ in range(4)]
    centre = [[None] * 4 for _ in range(4)]
    for k in range(4):
        here = cs[k]
        upper = 0.5 * (here + following(here, 1))
        lower = 0.5 * (here + preceding(here, 1))
        fa, fb = 0.5 * (here + cs[k ^ 2]), 0.5 * (here + cs[k ^ 1])
        diagonal = upper + lower + fa + fb + here
        centre[k][k] = jnp.where(valid, diagonal, 1.0)
        centre[k][k ^ 2], centre[k][k ^ 1] = -fa, -fb
        above[k][k] = jnp.where(lane < length - 1, -upper, 0.0)
        below[k][k] = jnp.where((lane > 0) & valid, -lower, 0.0)
    step = 1
    while step < length:
        ahead = lambda e, step=step: pltpu.roll(e, 128 - step, 1)
        behind = lambda e, step=step: pltpu.roll(e, step, 1)
        solved = inverse(centre)
        t, u, q = multiply(solved, below), multiply(solved, above), apply(solved, rhs)
        t_ahead, u_behind = each(t, ahead), each(u, behind)
        x, y = multiply(below, u_behind), multiply(above, t_ahead)
        centre = [
            [jnp.zeros((8, 128), F32) if centre[i][j] is None else centre[i][j] for j in range(4)]
            for i in range(4)
        ]
        centre = [[centre[i][j] - x[i][j] - y[i][j] for j in range(4)] for i in range(4)]
        x, y = apply(below, [behind(e) for e in q]), apply(above, [ahead(e) for e in q])
        rhs = [rhs[i] - x[i] - y[i] for i in range(4)]
        if 2 * step < length:
            below = each(multiply(below, each(t, behind)), lambda e: -e)
            above = each(multiply(above, each(u, ahead)), lambda e: -e)
        step *= 2
    solved = [jnp.where(valid, e, 0.0) for e in apply(inverse(centre), rhs)]
    return jnp.stack(
        [
            jnp.where(row == 0, solved[2 * a], jnp.where(row == 1, solved[2 * a + 1], 0.0))
            for a in range(2)
        ]
    )


def descend(s, c, cols, length):
    if c.shape[0] == 2:
        return exact(s, c)
    level = Whole(c, cols, length)
    v = level.w * s
    v = level.sweep(v, s)
    r = s - level.operator(v)
    e = descend(0.5 * coarsen_whole(r), 0.125 * coarsen_whole(c), cols // 2, length // 2)
    v = v + refine_whole(e, c.shape[1] // 8)
    v = level.sweep(v, s)
    return level.sweep(v, s)


def split_before(last, first_lane):
    lane = iota(last.shape, 1)
    return jnp.where(lane == 0, first_lane, pltpu.roll(last, 1, 1))


def split_after(first):
    lane = iota(first.shape, 1)
    return jnp.where(lane == 127, 0.0, pltpu.roll(first, 127, 1))


def split_operator(v, r, c, fa, fb, fz, ends):
    here = [lanes(v, r, k) for k in range(2)]
    after = [here[1], split_after(here[0])]
    gz = [lanes(fz, r, k) * (after[k] - here[k]) for k in range(2)]
    before = [split_before(gz[1], 0.5 * lanes(c, r, 0) * here[0]), gz[0]]
    out = []
    for k in range(2):
        gb = lanes(fb, r, k) * (following(here[k], 0) - here[k])
        a = lanes(fa, r, k) * (here[k] - lanes(v, r + 1, k)) + lanes(fa, r - 1, k) * (here[k] - lanes(v, r - 1, k))
        a = a + lanes(ends, r, k) * here[k]
        out.append(a + (preceding(gb, 0) - gb) + (before[k] - gz[k]))
    return out


def split_sweep(source, target, s, c, fa, fb, fz, ends, w, r):
    for k, a in enumerate(split_operator(source, r, c, fa, fb, fz, ends)):
        at = slice(128 * k, 128 * k + 128)
        target[r, :, at] = source[r, :, at] + w[r, :, at] * (s[r, :, at] - a)


def level_two(mine, other, s, c, v, fa, fb, fz, ends, w, s3, c3, u):
    _, _, core, _ = scalars()
    strips = mine.shape[0] // 16
    rows, cols = 32, 8 * strips
    first = iota((8, 128), 0) < 4
    edge = jnp.zeros((cols, 256), F32)
    for x in (c, v, u):
        x[0], x[rows + 1] = edge, edge

    def place(target, r, y, near, far):
        target[r, 8 * y : 8 * y + 8, 0:128] = jnp.where(first, near, pltpu.roll(far, 4, 0))
        target[r, 8 * y : 8 * y + 8, 128:256] = jnp.where(first, pltpu.roll(near, 4, 0), far)

    def load(k):
        for y in range(strips):
            at = k * strips + y
            for i in range(2):
                r = 2 * k + i + 1
                for n, target in enumerate((s, c)):
                    x, z = mine[at, n, i], other[at, n, i]
                    place(target, r, y, jnp.where(core == 0, x, z), jnp.where(core == 0, z, x))

    over_rows(0, rows // 2, 2, load)
    fa[0] = 0.5 * c[1]
    b = iota((cols, 128), 0)

    def one(r):
        here = [lanes(c, r, k) for k in range(2)]
        z = [0.5 * (here[0] + here[1]), 0.5 * (here[1] + split_after(here[0]))]
        before = [split_before(z[1], 0.5 * here[0]), z[0]]
        for k in range(2):
            at = slice(128 * k, 128 * k + 128)
            x, h = here[k], 0.5 * here[k]
            y = jnp.where(b == cols - 1, 0.0, 0.5 * (x + following(x, 0)))
            e = jnp.where((b == 0) | (b == cols - 1), h, 0.0)
            above = h + 0.5 * lanes(c, r + 1, k)
            diagonal = above + (h + 0.5 * lanes(c, r - 1, k)) + (y + preceding(y, 0)) + (z[k] + before[k]) + e
            factor = OMEGA / diagonal
            fa[r, :, at], fb[r, :, at], fz[r, :, at] = above, y, z[k]
            ends[r, :, at], w[r, :, at] = e, factor
            u[r, :, at] = factor * s[r, :, at]

    over_rows(1, rows + 1, 8, one)
    over_rows(1, rows + 1, 16, lambda r: split_sweep(u, v, s, c, fa, fb, fz, ends, w, r))

    def coarse(i):
        total = None
        for r in (2 * i + 1, 2 * i + 2):
            for k, a in enumerate(split_operator(v, r, c, fa, fb, fz, ends)):
                x = lanes(s, r, k) - a
                total = x if total is None else total + x
        s3[i] = 0.5 * half_columns(total)
        total = (lanes(c, 2 * i + 1, 0) + lanes(c, 2 * i + 1, 1)) + (lanes(c, 2 * i + 2, 0) + lanes(c, 2 * i + 2, 1))
        c3[i] = 0.125 * half_columns(total)

    over_rows(0, rows // 2, 4, coarse)


def coarse_levels(s3, c3, s, c, v, fa, fb, fz, ends, w, e2, e3, u, t):
    wide, narrow, _, _ = scalars()
    rows, cols = s.shape[0] - 2, s.shape[1]
    e3[...] = descend(s3[...], c3[...], cols // 2, 128)
    row = lambda step: jnp.clip(2 * wide + step, 0, rows - 1) + 1
    u[0], u[rows + 1], t[0], t[rows + 1] = v[0], v[0], v[0], v[0]
    for i in range(-2, 3):
        k = jnp.clip(wide + i, 0, rows // 2 - 1)
        e = refine_row(e3[k], cols // 8, False)
        for r in (2 * k + 1, 2 * k + 2):
            for half in range(2):
                at = slice(128 * half, 128 * half + 128)
                u[r, :, at] = v[r, :, at] + e
    for i in range(-3, 5):
        split_sweep(u, t, s, c, fa, fb, fz, ends, w, row(i))
    for i in range(-2, 4):
        split_sweep(t, u, s, c, fa, fb, fz, ends, w, row(i))
    for i in range(6):
        turned = pltpu.roll(u[row(i - 2)], lax.rem(cols + 2 - 4 * narrow, cols), 0)
        e2[i] = turned[0:8]


def moved(x, wide_step, narrow_step):
    w, y, k = [lax.axis_size(name) for name in AX]
    n = y * k
    pairs = [
        (i * n + j, ((i + wide_step) % w) * n + (j + narrow_step) % n)
        for i in range(w)
        for j in range(n)
    ]
    return lax.ppermute(x, AX, pairs)


def other_core(x):
    w, y, k = [lax.axis_size(name) for name in AX]
    return lax.ppermute(x, AX, [(i, i ^ 1) for i in range(w * y * k)])


def gathered(s2, c2):
    both = jnp.stack([s2, c2])
    chips = lax.axis_size("wide") * lax.axis_size("ny")
    return lax.all_to_all(jnp.broadcast_to(both[None], (chips,) + both.shape), ("wide", "ny"), 0, 0, tiled=True)


def per_device(p, d, m):
    up = jnp.concatenate([p[5:8], m[5:8], d[6:8]], axis=0)
    down = jnp.concatenate([p[0:3], m[0:3], d[0:2]], axis=0)
    left, right = moved(up, 1, 0), moved(down, -1, 0)
    c1, c2 = call(coarse_coefficients, [(4, 8, 512), (2, 8, 128)], [], m)
    to_left, to_right = call(pack_zero_own, [(8, 8, 1024)] * 2, [], p, d, m)
    nleft, nright = moved(to_right, 0, 1), moved(to_left, 0, -1)
    left, right, nleft, nright = lax.optimization_barrier((left, right, nleft, nright))
    to_left, to_right = call(pack_zero_edge, [(4, 8, 1024)] * 2, [], left, right)
    nleft_edge, nright_edge = moved(to_right, 0, 1), moved(to_left, 0, -1)
    big, own, halo = (14, 24, 1024), (14, 16, 1024), (14, 8, 1024)
    alone = call(level_zero_own, [own] * 7, [], p, d, m, left, right, flops=20_000_000)
    f0, s1, up, down, *zero = call(
        level_zero,
        [(8, 16, 1024), (4, 8, 512)] + [(7, 8, 512)] * 2 + [halo] * 4 + [big] * 2,
        [big] * 2 + [halo] * 3,
        *alone, c1, nleft, nright, nleft_edge, nright_edge,
        flops=30_000_000,
    )
    zero = [*alone[1:5], *zero]
    left1, right1 = moved(up, 1, 0), moved(down, -1, 0)
    to_left, to_right = call(pack_one, [(10, 8, 512)] * 2, [], s1, c1, left1, right1)
    nleft1, nright1 = moved(to_right, 0, 1), moved(to_left, 0, -1)
    mid = (12, 16, 512)
    f1, s2, up, down, *one = call(
        level_one,
        [(4, 8, 512), (2, 8, 128)] + [(8, 8, 1024)] * 2 + [mid] * 6,
        [mid] * 2,
        s1, c1, left1, right1, nleft1, nright1, f0,
        flops=10_000_000,
    )
    hleft, hright = moved(up, 1, 0), moved(down, -1, 0)
    mine = gathered(s2, c2)
    other = other_core(mine)
    whole, small = (34, 32, 256), (16, 16, 128)
    *two, s3, c3 = call(level_two, [whole] * 8 + [small] * 2, [whole], mine, other, flops=1000)
    to_left, to_right = call(pack_up_own, [(5, 8, 1024)] * 2, [], f0, f1)
    nhleft, nhright = moved(to_right, 0, 1), moved(to_left, 0, -1)
    s3, hleft, hright, nhleft, nhright = lax.optimization_barrier((s3, hleft, hright, nhleft, nhright))
    to_left, to_right = call(pack_up_edge, [(4, 8, 1024)] * 2, [], hleft, hright)
    edges = [moved(to_right, 0, 1), moved(to_left, 0, -1)]
    (e2,) = call(coarse_levels, [(6, 8, 256)], [small] + [whole] * 2, s3, c3, *two, flops=1000)
    return call(
        level_up,
        [(8, 16, 1024)] * 2,
        [big] * 2 + [mid] * 2 + [(8, 16, 1024)],
        *zero, *one, f0, f1, hleft, hright, nhleft, nhright, *edges, e2,
        flops=30_000_000,
        copies=3,
    )


def solution(mesh):
    wide, narrow = mesh.axis_names
    devices = mesh.devices.reshape(mesh.shape[wide], mesh.shape[narrow] // 2, 2)
    spec = P("wide", ("ny", "core"), None)
    return jax.shard_map(
        lambda p, d, m: tuple(per_device(p, d, m)),
        mesh=Mesh(devices, AX),
        in_specs=(spec,) * 3,
        out_specs=(spec,) * 2,
        check_vma=False,
    )
```

```python
import math

import jax
import jax.numpy as jnp
from jax import lax
from jax.experimental import pallas as pl
from jax.experimental.pallas import tpu as pltpu
from jax.sharding import Mesh, PartitionSpec as P

OMEGA = 0.8
AX = ("wide", "ny", "core")
F32 = jnp.float32
SPARE = 4 * 1024 * 1024


def iota(shape, dim):
    return lax.broadcasted_iota(jnp.int32, shape, dim)


def following(x, dim):
    return pltpu.roll(x, x.shape[dim] - 1, dim)


def preceding(x, dim):
    return pltpu.roll(x, 1, dim)


def lanes(x, r, k):
    if callable(x):
        return x(r, k)
    if isinstance(x, tuple):
        return jnp.concatenate([lanes(part, r, k) for part in x], axis=0)
    return x[r, :, 128 * k : 128 * k + 128]


def row_operator(v, r, c, fa, fb, fz):
    count = v.shape[2] // 128
    lane = iota((v.shape[1], 128), 1)
    here = lanes(v, r, 0)
    turned = pltpu.roll(here, 127, 1)
    out = []
    for k in range(count):
        if k + 1 < count:
            later = lanes(v, r, k + 1)
            later_turned = pltpu.roll(later, 127, 1)
        else:
            later, later_turned = None, 0.0
        gz = lanes(fz, r, k) * (jnp.where(lane == 127, later_turned, turned) - here)
        gz_turned = pltpu.roll(gz, 1, 1)
        if k == 0:
            gz_before = 0.5 * lanes(c, r, 0) * here
        gb = lanes(fb, r, k) * (following(here, 0) - here)
        a = lanes(fa, r, k) * (here - lanes(v, r + 1, k)) + lanes(fa, r - 1, k) * (here - lanes(v, r - 1, k))
        a = a + (preceding(gb, 0) - gb) + (jnp.where(lane == 0, gz_before, gz_turned) - gz)
        out.append(a)
        here, turned, gz_before = later, later_turned, gz_turned
    return out


def row_faces(r, c, fa, fb, fz, w):
    count = c.shape[2] // 128
    cols = c.shape[1]
    lane = iota((cols, 128), 1)
    here = lanes(c, r, 0)
    turned = pltpu.roll(here, 127, 1)
    for k in range(count):
        if k + 1 < count:
            later = lanes(c, r, k + 1)
            later_turned = pltpu.roll(later, 127, 1)
        else:
            later, later_turned = None, 0.0
        at = slice(128 * k, 128 * k + 128)
        z = 0.5 * (here + jnp.where(lane == 127, later_turned, turned))
        z_turned = pltpu.roll(z, 1, 1)
        if k == 0:
            z_before = 0.5 * here
        y = 0.5 * (here + following(here, 0))
        diagonal = 0.5 * (here + lanes(c, r - 1, k)) + 0.5 * (here + lanes(c, r + 1, k))
        diagonal = diagonal + (y + preceding(y, 0)) + (z + jnp.where(lane == 0, z_before, z_turned))
        fa[r, :, at] = 0.5 * (here + lanes(c, r + 1, k))
        fb[r, :, at], fz[r, :, at] = y, z
        w[r, :, at] = jnp.where(here > 0.0, OMEGA / diagonal, 0.0)
        here, turned, z_before = later, later_turned, z_turned


def over_rows(lo, hi, step, body):
    whole = (hi - lo) // step

    def some(i, carry):
        for j in range(step):
            body(lo + i * step + j)
        return carry

    if whole > 1:
        lax.fori_loop(0, whole, some, 0)
        lo = lo + whole * step
    for r in range(lo, hi):
        body(r)


def half_compress(low, high, dim):
    length = low.shape[dim]
    at = iota(low.shape, dim)
    index = (2 * at) % length
    first = jnp.take_along_axis(low, index, axis=dim)
    if high is None:
        return jnp.where(at < length // 2, first, 0.0)
    return jnp.where(at < length // 2, first, jnp.take_along_axis(high, index, axis=dim))


def half_columns(x):
    x = x + following(x, 0)
    tiles = x.shape[0] // 8
    part = lambda t: x[8 * t : 8 * t + 8]
    if tiles == 1:
        return half_compress(x, None, 0)
    x = [half_compress(part(2 * t), part(2 * t + 1), 0) for t in range(tiles // 2)]
    return x[0] if len(x) == 1 else jnp.concatenate(x, axis=0)


def level_one_row(x, r):
    return x[6 + r // 2][:, 512 * (r % 2) : 512 * (r % 2) + 512]


def coarse_sum(first, second, split=False):
    halves = [half_columns(x + y) for x, y in zip(first, second)]
    halves = [x + following(x, 1) for x in halves]
    if split:
        lane = iota((8, 128), 1)
        out = []
        for odd in range(2):
            index = (4 * lane + 2 * odd) % 128
            picked = jnp.take_along_axis(halves[0], index, axis=1)
            for k in range(1, 4):
                picked = jnp.where(lane >= 32 * k, jnp.take_along_axis(halves[k], index, axis=1), picked)
            out.append(picked)
        return out
    if len(halves) == 1:
        return [by_tile(halves[0], None)]
    return [by_tile(halves[k], halves[k + 1]) for k in range(0, len(halves), 2)]


def by_tile(low, high):
    tiles = [
        half_compress(low[8 * t : 8 * t + 8], None if high is None else high[8 * t : 8 * t + 8], 1)
        for t in range(low.shape[0] // 8)
    ]
    return tiles[0] if len(tiles) == 1 else jnp.concatenate(tiles, axis=0)


def blocks_of(x):
    return [x[:, 128 * k : 128 * k + 128] for k in range(x.shape[1] // 128)]


def repeat_lanes(x, block):
    source = block // 2
    index = iota((8, 128), 1) // 2 + 64 * (block % 2)
    return jnp.take_along_axis(x[:, 128 * source : 128 * source + 128], index, axis=1)


def take_rows(x, index):
    pieces = [
        jnp.take_along_axis(x[:, k : k + 128], index, axis=0) for k in range(0, x.shape[1], 128)
    ]
    return pieces[0] if len(pieces) == 1 else jnp.concatenate(pieces, axis=1)


def widen(x, blocks):
    pieces = [repeat_lanes(x, k) for k in range(blocks)]
    return pieces[0] if len(pieces) == 1 else jnp.concatenate(pieces, axis=1)


def widen_split(x):
    lane = iota((8, 128), 1)
    pieces = []
    for k in range(4):
        index = 32 * k + lane // 4
        even = jnp.take_along_axis(x[:, :128], index, axis=1)
        odd = jnp.take_along_axis(x[:, 128:], index, axis=1)
        pieces.append(jnp.where(lane // 2 % 2 == 0, even, odd))
    return jnp.concatenate(pieces, axis=1)


def scalars():
    wide, ny, core = lax.axis_index("wide"), lax.axis_index("ny"), lax.axis_index("core")
    sizes = [lax.axis_size(name) for name in AX]
    narrow = ny * sizes[2] + core
    inside = [
        jnp.where(flag, 1.0, 0.0).astype(F32)
        for flag in (wide > 0, wide < sizes[0] - 1, narrow > 0, narrow < sizes[1] * sizes[2] - 1)
    ]
    return wide, narrow, core, inside


def call(kernel, outs, scratch, *args, flops=1_000_000, copies=0):
    vmem = pl.BlockSpec(memory_space=pltpu.VMEM)
    size = 4 * sum(a.size for a in args)
    held = size + 4 * sum(math.prod(s) for s in outs + scratch)
    return pl.pallas_call(
        kernel,
        out_shape=[jax.ShapeDtypeStruct(s, F32) for s in outs],
        in_specs=[vmem] * len(args),
        out_specs=[pl.BlockSpec(memory_space=pltpu.HBM) if copies else vmem] * len(outs),
        scratch_shapes=[pltpu.VMEM(s, F32) for s in scratch] + [pltpu.SemaphoreType.DMA((copies,))] * (copies > 0),
        compiler_params=pltpu.CompilerParams(vmem_limit_bytes=held + SPARE),
        cost_estimate=pl.CostEstimate(flops=flops, bytes_accessed=0 if flops == 1000 else size, transcendentals=0),
    )(*args)


def coarse_coefficients(p, d, m, c1, c2, up, down):
    for n, (x, last, first) in enumerate(((p, 5, 2), (m, 5, 2), (d, 6, 1))):
        for t in range(2):
            up[2 * n + t], down[2 * n + t] = x[last, 8 * t : 8 * t + 8], x[first, 8 * t : 8 * t + 8]
    for i in range(4):
        x = coarse_sum(blocks_of(m[2 * i]), blocks_of(m[2 * i + 1]))
        for k, a in enumerate(x):
            c1[i, :, 128 * k : 128 * k + 128] = 0.125 * a
    for i in range(2):
        even, odd = coarse_sum(blocks_of(c1[2 * i]), blocks_of(c1[2 * i + 1]), True)
        c2[i] = 0.125 * (even + pltpu.roll(odd, 4, 0))
        both = jnp.concatenate([c1[2 * i], c1[2 * i + 1]], axis=1)
        up[6 + i], down[6 + i] = both, both


def columns_zero(vp, vm, vd, side):
    at = iota((8, 1024), 0)
    if side == 0:
        vm, vd = pltpu.roll(vm, 3, 0), pltpu.roll(vd, 6, 0)
        return jnp.where(at < 3, vp, jnp.where(at < 6, vm, vd))
    vm, vd = pltpu.roll(vm, 5, 0), pltpu.roll(vd, 2, 0)
    return jnp.where(at >= 5, vp, jnp.where(at >= 2, vm, vd))


def pack_zero_own(p, d, m, to_left, to_right):
    for a in range(8):
        for side, out in ((0, to_left), (1, to_right)):
            tile = slice(8 * side, 8 * side + 8)
            out[a] = columns_zero(p[a, tile], m[a, tile], d[a, tile], side)


def pack_zero_edge(left, right, to_left, to_right):
    _, _, _, (low, high, _, _) = scalars()
    for side, out in ((0, to_left), (1, to_right)):
        tile = slice(8 * side, 8 * side + 8)
        for i in range(2):
            nothing = jnp.zeros((8, 1024), F32)
            vd = (left[4, tile] if i == 1 else nothing), (right[4, tile] if i == 0 else nothing)
            out[i] = columns_zero(left[i, tile], left[2 + i, tile], vd[0], side) * low
            out[2 + i] = columns_zero(right[i, tile], right[2 + i, tile], vd[1], side) * high


def faces(c, rows, fa, fb, fz, w, step):
    for k in range(c.shape[2] // 128):
        at = slice(128 * k, 128 * k + 128)
        fa[rows[0] - 1, :, at] = 0.5 * (c[rows[0] - 1, :, at] + c[rows[0], :, at])
    over_rows(rows[0], rows[1], step, lambda r: row_faces(r, c, fa, fb, fz, w))


def sweep(source, target, s, c, fa, fb, fz, w, rows, step):
    def one(r):
        for k, a in enumerate(row_operator(source, r, c, fa, fb, fz)):
            at = slice(128 * k, 128 * k + 128)
            target[r, :, at] = source[r, :, at] + w[r, :, at] * (lanes(s, r, k) - a)

    over_rows(rows[0], rows[1], step, one)


def residual_row(v, s, c, fa, fb, fz, r, cols):
    return [
        (lanes(s, r, k) - a)[0:cols]
        for k, a in enumerate(row_operator(v, r, c, fa, fb, fz))
    ]


def across(r, v, c, s, fa, fz, diagonal, left_over, cols=slice(None)):
    lane = iota(lanes(c, r, 0).shape, 1)
    count = fa.shape[2] // 128
    turn = lambda x, k: pltpu.roll(lanes(x, r, k), 127, 1) if k < count else 0.0
    here, there, c_next, v_next = lanes(c, r, 0), lanes(v, r, 0), turn(c, 0), turn(v, 0)
    for k in range(count):
        at = slice(128 * k, 128 * k + 128)
        c_later, v_later = turn(c, k + 1), turn(v, k + 1)
        z = 0.5 * (here + jnp.where(lane == 127, c_later, c_next))
        flux = z * (jnp.where(lane == 127, v_later, v_next) - there)
        z_turned, flux_turned = pltpu.roll(z, 1, 1), pltpu.roll(flux, 1, 1)
        if k == 0:
            z_before, flux_before = 0.5 * here, 0.5 * here * there
        above, below = 0.5 * (here + lanes(c, r + 1, k)), 0.5 * (here + lanes(c, r - 1, k))
        fa[r, cols, at], fz[r, cols, at] = above, z
        diagonal[r, cols, at] = above + below + (z + jnp.where(lane == 0, z_before, z_turned))
        a = above * (there - lanes(v, r + 1, k)) + below * (there - lanes(v, r - 1, k))
        a = a + (jnp.where(lane == 0, flux_before, flux_turned) - flux)
        left_over[r, cols, at] = lanes(s, r, k) - a
        if k + 1 < count:
            here, there = lanes(c, r, k + 1), lanes(v, r, k + 1)
        c_next, v_next, z_before, flux_before = c_later, v_later, z_turned, flux_turned


def level_zero_own(p, d, m, left, right, v, me, de, fa, fz, diagonal, left_over):
    _, _, _, (low, high, _, _) = scalars()
    for r in range(1, 13):
        a = r - 3
        if a < 0:
            v[r], me[r] = left[r - 1] * low, left[r + 1] * low
        elif a < 8:
            v[r], me[r], de[r] = p[a], m[a], d[a]
        else:
            v[r], me[r] = right[a - 8] * high, right[a - 6] * high
    de[2], de[11] = left[4] * low, right[4] * high
    fa[1] = 0.5 * (me[1] + me[2])
    over_rows(2, 12, 2, lambda r: across(r, v, me, de, fa, fz, diagonal, left_over))


def level_zero(
    own_v, own_me, own_de, own_fa, own_fz, own_diagonal, own_left_over, left, right, nleft, nright,
    nleft_edge, nright_edge,
    field, s1, up, down, me, de, fa, fz, fb, w, v, u, beside, diagonal, left_over,
):
    _, _, _, (low, high, nlow, nhigh) = scalars()
    at = iota((8, 1024), 0)
    own, halo = slice(0, 16), slice(16, 24)
    nothing = jnp.zeros((8, 1024), F32)
    for r in range(14):
        if r in (0, 13):
            beside[r], me[r], de[r, halo] = nothing, nothing, nothing
            continue
        if 3 <= r < 11:
            x, y = nright[r - 3] * nhigh, nleft[r - 3] * nlow
        else:
            e = r - 1 if r < 3 else r - 9
            x, y = nright_edge[e] * nhigh, nleft_edge[e] * nlow
        beside[r] = jnp.where(at < 3, x, jnp.where(at >= 5, y, 0.0))
        x3, y3 = pltpu.roll(x, 5, 0), pltpu.roll(y, 3, 0)
        me[r] = jnp.where(at < 3, x3, jnp.where(at >= 5, y3, 0.0))
        x6, y6 = pltpu.roll(x, 2, 0), pltpu.roll(y, 6, 0)
        de[r, halo] = jnp.where(at < 2, x6, jnp.where(at >= 6, y6, 0.0))

    def late(first):
        rows = (own_v, own_me)[first // 2]

        def row(r, k):
            if r not in (0, 13):
                return lanes(rows, r, k)
            parts = [(left if r == 0 else right)[first + t, :, 128 * k : 128 * k + 128] for t in range(2)]
            return jnp.concatenate(parts, axis=0) * (low if r == 0 else high)

        return row

    edge_v, edge_c = late(0), late(2)
    for t in range(2):
        de[1, 8 * t : 8 * t + 8], de[12, 8 * t : 8 * t + 8] = left[4 + t] * low, right[4 + t] * high
    for k in range(8):
        lane = slice(128 * k, 128 * k + 128)
        fa[0, own, lane] = 0.5 * (edge_c(0, k) + edge_c(1, k))
    fa[0, halo] = 0.5 * me[1]
    de_own = lambda r, k: de[r, own, 128 * k : 128 * k + 128]
    de_halo = lambda r, k: de[r, halo, 128 * k : 128 * k + 128]
    for r in (1, 12):
        across(r, edge_v, edge_c, de_own, fa, fz, diagonal, left_over, own)

    def one(r, edge=False):
        across(r, beside, me, de_halo, fa, fz, diagonal, left_over, halo)
        if not edge:
            de[r, own], fa[r, own], fz[r, own] = own_de[r], own_fa[r], own_fz[r]
        for k in range(8):
            lane = slice(128 * k, 128 * k + 128)
            there, here = lanes((own_v, beside), r, k), lanes((own_me, me), r, k)
            total, rest = [
                x[r, :, lane] if edge else jnp.concatenate([y[r, :, lane], x[r, halo, lane]], axis=0)
                for x, y in ((diagonal, own_diagonal), (left_over, own_left_over))
            ]
            y = 0.5 * (here + following(here, 0))
            flux = y * (following(there, 0) - there)
            total = total + (y + preceding(y, 0))
            factor = jnp.where(here > 0.0, OMEGA / total, 0.0)
            fb[r, :, lane], w[r, :, lane] = y, factor
            u[r, :, lane] = there + factor * (rest - (preceding(flux, 0) - flux))

    one(1, True)
    over_rows(2, 12, 2, one)
    one(12, True)
    me = (own_me, me)
    sweep(u, v, de, me, fa, fb, fz, w, (2, 12), 3)
    field[...] = v[3:11, 0:16]

    def coarse(i, carry):
        r = 2 * i + 3
        x = residual_row(v, de, me, fa, fb, fz, r, 16)
        y = residual_row(v, de, me, fa, fb, fz, r + 1, 16)
        for k, a in enumerate(coarse_sum(x, y)):
            s1[i, :, 128 * k : 128 * k + 128] = 0.5 * a
        return carry

    lax.fori_loop(0, 4, coarse, 0)
    up[...], down[...] = s1[1:4], s1[0:3]


def pack_one(s, c, left, right, c_left, c_right, to_left, to_right):
    _, _, _, (low, high, _, _) = scalars()
    at = iota((8, 512), 0)
    for r in range(1, 11):
        a = r - 4
        if a < 0:
            vc = level_one_row(c_left, r) * low
            vs = left[r - 1] * low if r > 0 else jnp.zeros_like(vc)
        elif a < 4:
            vs, vc = s[a], c[a]
        else:
            vc = level_one_row(c_right, a - 4) * high
            vs = right[a - 4] * high if a < 7 else jnp.zeros_like(vc)
        to_left[r - 1] = jnp.where(at < 4, vc, pltpu.roll(vs, 4, 0))
        to_right[r - 1] = jnp.where(at >= 4, vc, pltpu.roll(vs, 4, 0))


def level_one(s, c, left, right, c_left, c_right, nleft, nright, f0, field, s2, up, down, se, ce, fa, fb, fz, w, v, u):
    _, _, _, (low, high, nlow, nhigh) = scalars()
    at = iota((8, 512), 0)
    for r in range(12):
        a = r - 4
        if a < 0:
            ce[r, 0:8] = level_one_row(c_left, r) * low
            se[r, 0:8] = left[r - 1] * low if r > 0 else jnp.zeros((8, 512), F32)
        elif a < 4:
            se[r, 0:8], ce[r, 0:8] = s[a], c[a]
        else:
            ce[r, 0:8] = level_one_row(c_right, a - 4) * high
            se[r, 0:8] = right[a - 4] * high if a < 7 else jnp.zeros((8, 512), F32)
        if r in (0, 11):
            ce[r, 8:16] = se[r, 8:16] = jnp.zeros((8, 512), F32)
            continue
        x, y = nright[r - 1] * nhigh, nleft[r - 1] * nlow
        ce[r, 8:16] = jnp.where(at < 4, x, y)
        se[r, 8:16] = jnp.where(at < 4, pltpu.roll(x, 4, 0), pltpu.roll(y, 4, 0))
    faces(ce, (1, 11), fa, fb, fz, w, 5)

    for r in range(2, 10):
        u[r] = w[r] * se[r]
    sweep(u, v, se, ce, fa, fb, fz, w, (3, 9), 3)
    field[...] = v[4:8, 0:8]
    for i in range(2):
        r = 2 * i + 4
        x = residual_row(v, se, ce, fa, fb, fz, r, 8)
        y = residual_row(v, se, ce, fa, fb, fz, r + 1, 8)
        even, odd = coarse_sum(x, y, True)
        s2[i] = 0.5 * (even + pltpu.roll(odd, 4, 0))
    for r in range(3):
        for t in range(2):
            up[2 * r + t] = f0[5 + r, 8 * t : 8 * t + 8]
            down[2 * r + t] = f0[r, 8 * t : 8 * t + 8]
    for r in range(2):
        both = jnp.concatenate([field[2 * r], field[2 * r + 1]], axis=1)
        up[6 + r] = both
        down[6 + r] = both


def two_rows(x, y, side):
    at = iota((8, 1024), 0)
    return jnp.where(at < 4 if side == 0 else at >= 4, x, pltpu.roll(y, 4, 0))


def pack_up_own(f0, f1, to_left, to_right):
    for side, out in ((0, to_left), (1, to_right)):
        tile = slice(8 * side, 8 * side + 8)
        for t in range(4):
            out[t] = two_rows(f0[2 * t, tile], f0[2 * t + 1, tile], side)
        pair = [jnp.concatenate([f1[2 * k], f1[2 * k + 1]], axis=1) for k in range(2)]
        out[4] = two_rows(pair[0], pair[1], side)


def pack_up_edge(left, right, to_left, to_right):
    _, _, _, (low, high, _, _) = scalars()
    for side, out in ((0, to_left), (1, to_right)):
        out[0] = two_rows(left[2 + side], left[4 + side], side) * low
        out[1] = two_rows(right[side], right[2 + side], side) * high
        out[2] = two_rows(left[6], left[7], side) * low
        out[3] = two_rows(right[6], right[7], side) * high


def tile_up(own, edge, t):
    if t in (0, 5, 6, 8):
        return edge[(0, 5, 6, 8).index(t)]
    return own[4 if t == 7 else t - 1]


def level_up(
    own_me, me, de, fa, fz, fb, w, se, ce, fa1, fb1, fz1, w1,
    f0, f1, left, right, nleft, nright, nleft_edge, nright_edge, e2,
    out, res, v, u, v1, u1, kept, sent,
):
    _, _, _, (low, high, nlow, nhigh) = scalars()
    at = iota((8, 512), 0)
    half = iota((8, 128), 0)
    for r in range(12):
        if r < 4:
            f = left[6 + r // 2][:, 512 * (r % 2) : 512 * (r % 2) + 512] * low
        elif r < 8:
            f = f1[r - 4]
        else:
            f = right[2 + r // 2][:, 512 * (r % 2) : 512 * (r % 2) + 512] * high
        half_tile = slice(512 * (r % 2), 512 * (r % 2) + 512)
        x = tile_up(nright, nright_edge, 6 + r // 4)[:, half_tile] * nhigh
        y = tile_up(nleft, nleft_edge, 6 + r // 4)[:, half_tile] * nlow
        if r % 4 > 1:
            x, y = pltpu.roll(x, 4, 0), pltpu.roll(y, 4, 0)
        g = jnp.where(at < 4, x, y)
        e = e2[r // 2]
        own = widen_split(take_rows(e, 2 + half // 2))
        beside = widen_split(take_rows(e, jnp.where(half < 4, 6 + half // 2, (half - 4) // 2)))
        v1[r, 0:8] = f + jnp.where(ce[r, 0:8] > 0.0, own, 0.0)
        v1[r, 8:16] = g + jnp.where(ce[r, 8:16] > 0.0, beside, 0.0)
    sweep(v1, u1, se, ce, fa1, fb1, fz1, w1, (1, 11), 5)
    sweep(u1, v1, se, ce, fa1, fb1, fz1, w1, (2, 10), 4)
    zero = iota((8, 1024), 0)
    for r in range(14):
        if r < 3:
            f = [left[2 * r] * low, left[2 * r + 1] * low]
        elif r < 11:
            f = [f0[r - 3, 0:8], f0[r - 3, 8:16]]
        else:
            f = [right[2 * (r - 11)] * high, right[2 * (r - 11) + 1] * high]
        if r in (0, 13):
            f.append(jnp.zeros((8, 1024), F32))
        else:
            t = (r - 1) // 2
            x, y = tile_up(nright, nright_edge, t) * nhigh, tile_up(nleft, nleft_edge, t) * nlow
            if r % 2 == 0:
                x, y = pltpu.roll(x, 4, 0), pltpu.roll(y, 4, 0)
            f.append(jnp.where(zero < 3, x, jnp.where(zero >= 5, y, 0.0)))
        e = v1[(r + 5) // 2]
        pieces = (
            (e[0:8], half // 2),
            (e[0:8], 4 + half // 2),
            (e[8:16], jnp.where(half < 4, half // 2, 4 + half // 2)),
        )
        for t, (part, index) in enumerate(pieces):
            fine = widen(take_rows(part, index), 8)
            tile = slice(8 * t, 8 * t + 8)
            inside = own_me[min(max(r, 1), 12), tile] if t < 2 else me[r]
            v[r, tile] = f[t] + jnp.where(inside > 0.0, fine, 0.0)

    me = (own_me, me)
    sweep(v, u, de, me, fa, fb, fz, w, (1, 13), 3)
    sweep(u, v, de, me, fa, fb, fz, w, (2, 12), 3)
    first = pltpu.make_async_copy(v.at[3:11, 0:16], out, sent.at[0])
    first.start()

    def final(r):
        for k, x in enumerate(residual_row(v, de, me, fa, fb, fz, r, 16)):
            kept[r - 3, :, 128 * k : 128 * k + 128] = x

    over_rows(3, 7, 2, final)
    second = pltpu.make_async_copy(kept.at[0:4], res.at[0:4], sent.at[1])
    second.start()
    over_rows(7, 11, 2, final)
    third = pltpu.make_async_copy(kept.at[4:8], res.at[4:8], sent.at[2])
    third.start()
    for copy in (first, second, third):
        copy.wait()


def shifted(x, step):
    zero = jnp.zeros((1,) + x.shape[1:], F32)
    return jnp.concatenate([x[1:], zero] if step > 0 else [zero, x[:-1]], axis=0)


class Whole:
    def __init__(self, c, cols, length):
        b, z = iota(c.shape, 1), iota(c.shape, 2)
        valid = (b < cols) & (z < length)
        self.fa = 0.5 * (c + shifted(c, 1))
        self.fa_below = 0.5 * (c + shifted(c, -1))
        self.fb = jnp.where(b < cols - 1, 0.5 * (c + following(c, 1)), 0.0)
        self.fz = jnp.where(z < length - 1, 0.5 * (c + following(c, 2)), 0.0)
        half = 0.5 * c
        self.ends = jnp.where(b == 0, half, 0.0) + jnp.where(b == cols - 1, half, 0.0)
        self.ends = self.ends + jnp.where(z == 0, half, 0.0) + jnp.where(z == length - 1, half, 0.0)
        diagonal = self.fa + self.fa_below + self.fb + preceding(self.fb, 1)
        diagonal = diagonal + self.fz + preceding(self.fz, 2) + self.ends
        self.w = jnp.where(valid, OMEGA / diagonal, 0.0)

    def operator(self, v):
        gb = self.fb * (following(v, 1) - v)
        gz = self.fz * (following(v, 2) - v)
        out = self.fa * (v - shifted(v, 1)) + self.fa_below * (v - shifted(v, -1)) + self.ends * v
        return out + (preceding(gb, 1) - gb) + (preceding(gz, 2) - gz)

    def sweep(self, v, s):
        return v + self.w * (s - self.operator(v))


def coarsen_whole(x):
    return jnp.stack([coarse_sum([x[a]], [x[a + 1]])[0] for a in range(0, x.shape[0], 2)])


def refine_row(x, cols_tiles, lanes_too):
    half = iota((8, 128), 0)
    tiles = []
    for t in range(cols_tiles):
        source = x[8 * (t // 2) : 8 * (t // 2) + 8]
        tile = take_rows(source, half // 2 + 4 * (t % 2))
        tiles.append(widen(tile, 1) if lanes_too else tile)
    return tiles[0] if cols_tiles == 1 else jnp.concatenate(tiles, axis=0)


def refine_whole(x, cols_tiles):
    rows = [refine_row(x[a], cols_tiles, True) for a in range(x.shape[0])]
    return jnp.stack([rows[a // 2] for a in range(2 * x.shape[0])])


def multiply(x, y):
    out = [[None] * 4 for _ in range(4)]
    for i in range(4):
        for j in range(4):
            for k in range(4):
                if x[i][k] is not None and y[k][j] is not None:
                    term = x[i][k] * y[k][j]
                    out[i][j] = term if out[i][j] is None else out[i][j] + term
    return out


def apply(x, y):
    out = []
    for i in range(4):
        total = None
        for k in range(4):
            if x[i][k] is not None:
                term = x[i][k] * y[k]
                total = term if total is None else total + term
        out.append(total)
    return out


def inverse(x):
    x = [[jnp.zeros((8, 128), F32) if e is None else e for e in line] for line in x]
    for k in range(4):
        pivot = 1.0 / x[k][k]
        line = [pivot if j == k else x[k][j] * pivot for j in range(4)]
        for i in range(4):
            if i != k:
                factor = x[i][k]
                x[i] = [-factor * pivot if j == k else x[i][j] - factor * line[j] for j in range(4)]
        x[k] = line
    return x


def each(x, move):
    return [[None if e is None else move(e) for e in line] for line in x]


def exact(s, c):
    length = 16
    lane = iota((8, 128), 1)
    row = iota((8, 128), 0)
    valid = lane < length

    def line(x, a, b):
        picked = jnp.take_along_axis(x[a], jnp.full((8, 128), b, jnp.int32), axis=0)
        return jnp.where(valid, picked, 0.0)

    cs = [line(c, k // 2, k % 2) for k in range(4)]
    rhs = [line(s, k // 2, k % 2) for k in range(4)]
    below = [[None] * 4 for _ in range(4)]
    above = [[None] * 4 for _ in range(4)]
    centre = [[None] * 4 for _ in range(4)]
    for k in range(4):
        here = cs[k]
        upper = 0.5 * (here + following(here, 1))
        lower = 0.5 * (here + preceding(here, 1))
        fa, fb = 0.5 * (here + cs[k ^ 2]), 0.5 * (here + cs[k ^ 1])
        diagonal = upper + lower + fa + fb + here
        centre[k][k] = jnp.where(valid, diagonal, 1.0)
        centre[k][k ^ 2], centre[k][k ^ 1] = -fa, -fb
        above[k][k] = jnp.where(lane < length - 1, -upper, 0.0)
        below[k][k] = jnp.where((lane > 0) & valid, -lower, 0.0)
    step = 1
    while step < length:
        ahead = lambda e, step=step: pltpu.roll(e, 128 - step, 1)
        behind = lambda e, step=step: pltpu.roll(e, step, 1)
        solved = inverse(centre)
        t, u, q = multiply(solved, below), multiply(solved, above), apply(solved, rhs)
        t_ahead, u_behind = each(t, ahead), each(u, behind)
        x, y = multiply(below, u_behind), multiply(above, t_ahead)
        centre = [
            [jnp.zeros((8, 128), F32) if centre[i][j] is None else centre[i][j] for j in range(4)]
            for i in range(4)
        ]
        centre = [[centre[i][j] - x[i][j] - y[i][j] for j in range(4)] for i in range(4)]
        x, y = apply(below, [behind(e) for e in q]), apply(above, [ahead(e) for e in q])
        rhs = [rhs[i] - x[i] - y[i] for i in range(4)]
        if 2 * step < length:
            below = each(multiply(below, each(t, behind)), lambda e: -e)
            above = each(multiply(above, each(u, ahead)), lambda e: -e)
        step *= 2
    solved = [jnp.where(valid, e, 0.0) for e in apply(inverse(centre), rhs)]
    return jnp.stack(
        [
            jnp.where(row == 0, solved[2 * a], jnp.where(row == 1, solved[2 * a + 1], 0.0))
            for a in range(2)
        ]
    )


def descend(s, c, cols, length):
    if c.shape[0] == 2:
        return exact(s, c)
    level = Whole(c, cols, length)
    v = level.w * s
    v = level.sweep(v, s)
    r = s - level.operator(v)
    e = descend(0.5 * coarsen_whole(r), 0.125 * coarsen_whole(c), cols // 2, length // 2)
    v = v + refine_whole(e, c.shape[1] // 8)
    v = level.sweep(v, s)
    return level.sweep(v, s)


def split_before(last, first_lane):
    lane = iota(last.shape, 1)
    return jnp.where(lane == 0, first_lane, pltpu.roll(last, 1, 1))


def split_after(first):
    lane = iota(first.shape, 1)
    return jnp.where(lane == 127, 0.0, pltpu.roll(first, 127, 1))


def split_operator(v, r, c, fa, fb, fz, ends):
    here = [lanes(v, r, k) for k in range(2)]
    after = [here[1], split_after(here[0])]
    gz = [lanes(fz, r, k) * (after[k] - here[k]) for k in range(2)]
    before = [split_before(gz[1], 0.5 * lanes(c, r, 0) * here[0]), gz[0]]
    out = []
    for k in range(2):
        gb = lanes(fb, r, k) * (following(here[k], 0) - here[k])
        a = lanes(fa, r, k) * (here[k] - lanes(v, r + 1, k)) + lanes(fa, r - 1, k) * (here[k] - lanes(v, r - 1, k))
        a = a + lanes(ends, r, k) * here[k]
        out.append(a + (preceding(gb, 0) - gb) + (before[k] - gz[k]))
    return out


def split_sweep(source, target, s, c, fa, fb, fz, ends, w, r):
    for k, a in enumerate(split_operator(source, r, c, fa, fb, fz, ends)):
        at = slice(128 * k, 128 * k + 128)
        target[r, :, at] = source[r, :, at] + w[r, :, at] * (s[r, :, at] - a)


def level_two(mine, other, s, c, v, fa, fb, fz, ends, w, s3, c3, u):
    _, _, core, _ = scalars()
    strips = mine.shape[0] // 16
    rows, cols = 32, 8 * strips
    first = iota((8, 128), 0) < 4
    edge = jnp.zeros((cols, 256), F32)
    for x in (c, v, u):
        x[0], x[rows + 1] = edge, edge

    def place(target, r, y, near, far):
        target[r, 8 * y : 8 * y + 8, 0:128] = jnp.where(first, near, pltpu.roll(far, 4, 0))
        target[r, 8 * y : 8 * y + 8, 128:256] = jnp.where(first, pltpu.roll(near, 4, 0), far)

    def load(k):
        for y in range(strips):
            at = k * strips + y
            for i in range(2):
                r = 2 * k + i + 1
                for n, target in enumerate((s, c)):
                    x, z = mine[at, n, i], other[at, n, i]
                    place(target, r, y, jnp.where(core == 0, x, z), jnp.where(core == 0, z, x))

    over_rows(0, rows // 2, 2, load)
    fa[0] = 0.5 * c[1]
    b = iota((cols, 128), 0)

    def one(r):
        here = [lanes(c, r, k) for k in range(2)]
        z = [0.5 * (here[0] + here[1]), 0.5 * (here[1] + split_after(here[0]))]
        before = [split_before(z[1], 0.5 * here[0]), z[0]]
        for k in range(2):
            at = slice(128 * k, 128 * k + 128)
            x, h = here[k], 0.5 * here[k]
            y = jnp.where(b == cols - 1, 0.0, 0.5 * (x + following(x, 0)))
            e = jnp.where((b == 0) | (b == cols - 1), h, 0.0)
            above = h + 0.5 * lanes(c, r + 1, k)
            diagonal = above + (h + 0.5 * lanes(c, r - 1, k)) + (y + preceding(y, 0)) + (z[k] + before[k]) + e
            factor = OMEGA / diagonal
            fa[r, :, at], fb[r, :, at], fz[r, :, at] = above, y, z[k]
            ends[r, :, at], w[r, :, at] = e, factor
            u[r, :, at] = factor * s[r, :, at]

    over_rows(1, rows + 1, 8, one)
    over_rows(1, rows + 1, 16, lambda r: split_sweep(u, v, s, c, fa, fb, fz, ends, w, r))

    def coarse(i):
        total = None
        for r in (2 * i + 1, 2 * i + 2):
            for k, a in enumerate(split_operator(v, r, c, fa, fb, fz, ends)):
                x = lanes(s, r, k) - a
                total = x if total is None else total + x
        s3[i] = 0.5 * half_columns(total)
        total = (lanes(c, 2 * i + 1, 0) + lanes(c, 2 * i + 1, 1)) + (lanes(c, 2 * i + 2, 0) + lanes(c, 2 * i + 2, 1))
        c3[i] = 0.125 * half_columns(total)

    over_rows(0, rows // 2, 4, coarse)


def coarse_levels(s3, c3, s, c, v, fa, fb, fz, ends, w, e2, e3, u, t):
    wide, narrow, _, _ = scalars()
    rows, cols = s.shape[0] - 2, s.shape[1]
    e3[...] = descend(s3[...], c3[...], cols // 2, 128)
    row = lambda step: jnp.clip(2 * wide + step, 0, rows - 1) + 1
    u[0], u[rows + 1], t[0], t[rows + 1] = v[0], v[0], v[0], v[0]
    for i in range(-2, 3):
        k = jnp.clip(wide + i, 0, rows // 2 - 1)
        e = refine_row(e3[k], cols // 8, False)
        for r in (2 * k + 1, 2 * k + 2):
            for half in range(2):
                at = slice(128 * half, 128 * half + 128)
                u[r, :, at] = v[r, :, at] + e
    for i in range(-3, 5):
        split_sweep(u, t, s, c, fa, fb, fz, ends, w, row(i))
    for i in range(-2, 4):
        split_sweep(t, u, s, c, fa, fb, fz, ends, w, row(i))
    for i in range(6):
        turned = pltpu.roll(u[row(i - 2)], lax.rem(cols + 2 - 4 * narrow, cols), 0)
        e2[i] = turned[0:8]


def moved(x, wide_step, narrow_step):
    w, y, k = [lax.axis_size(name) for name in AX]
    n = y * k
    pairs = [
        (i * n + j, ((i + wide_step) % w) * n + (j + narrow_step) % n)
        for i in range(w)
        for j in range(n)
    ]
    return lax.ppermute(x, AX, pairs)


def other_core(x):
    w, y, k = [lax.axis_size(name) for name in AX]
    return lax.ppermute(x, AX, [(i, i ^ 1) for i in range(w * y * k)])


def gathered(s2, c2):
    both = jnp.stack([s2, c2])
    chips = lax.axis_size("wide") * lax.axis_size("ny")
    return lax.all_to_all(jnp.broadcast_to(both[None], (chips,) + both.shape), ("wide", "ny"), 0, 0, tiled=True)


def per_device(p, d, m):
    up = jnp.concatenate([p[6:8], m[6:8], d[7:8]], axis=0)
    down = jnp.concatenate([p[0:2], m[0:2], d[0:1]], axis=0)
    left, right = moved(up, 1, 0), moved(down, -1, 0)
    c1, c2, up, down = call(
        coarse_coefficients, [(4, 8, 512), (2, 8, 128)] + [(8, 8, 1024)] * 2, [], p, d, m
    )
    c_left, c_right = moved(up, 1, 0), moved(down, -1, 0)
    to_left, to_right = call(pack_zero_own, [(8, 8, 1024)] * 2, [], p, d, m)
    nleft, nright = moved(to_right, 0, 1), moved(to_left, 0, -1)
    left, right, nleft, nright = lax.optimization_barrier((left, right, nleft, nright))
    to_left, to_right = call(pack_zero_edge, [(4, 8, 1024)] * 2, [], left, right)
    nleft_edge, nright_edge = moved(to_right, 0, 1), moved(to_left, 0, -1)
    big, own, halo = (14, 24, 1024), (14, 16, 1024), (14, 8, 1024)
    alone = call(level_zero_own, [own] * 7, [], p, d, m, left, right, flops=20_000_000)
    f0, s1, up, down, *zero = call(
        level_zero,
        [(8, 16, 1024), (4, 8, 512)] + [(3, 8, 512)] * 2 + [halo] + [big] * 5,
        [big] * 2 + [halo] + [big] * 2,
        *alone, c_left, c_right, nleft, nright, nleft_edge, nright_edge,
        flops=30_000_000,
    )
    zero = [alone[1], *zero]
    left1, right1 = moved(up, 1, 0), moved(down, -1, 0)
    to_left, to_right = call(pack_one, [(10, 8, 512)] * 2, [], s1, c1, left1, right1, c_left, c_right)
    nleft1, nright1 = moved(to_right, 0, 1), moved(to_left, 0, -1)
    mid = (12, 16, 512)
    f1, s2, up, down, *one = call(
        level_one,
        [(4, 8, 512), (2, 8, 128)] + [(8, 8, 1024)] * 2 + [mid] * 6,
        [mid] * 2,
        s1, c1, left1, right1, c_left, c_right, nleft1, nright1, f0,
        flops=10_000_000,
    )
    hleft, hright = moved(up, 1, 0), moved(down, -1, 0)
    mine = gathered(s2, c2)
    other = other_core(mine)
    whole, small = (34, 32, 256), (16, 16, 128)
    *two, s3, c3 = call(level_two, [whole] * 8 + [small] * 2, [whole], mine, other, flops=1000)
    to_left, to_right = call(pack_up_own, [(5, 8, 1024)] * 2, [], f0, f1)
    nhleft, nhright = moved(to_right, 0, 1), moved(to_left, 0, -1)
    s3, hleft, hright, nhleft, nhright = lax.optimization_barrier((s3, hleft, hright, nhleft, nhright))
    to_left, to_right = call(pack_up_edge, [(4, 8, 1024)] * 2, [], hleft, hright)
    edges = [moved(to_right, 0, 1), moved(to_left, 0, -1)]
    (e2,) = call(coarse_levels, [(6, 8, 256)], [small] + [whole] * 2, s3, c3, *two, flops=1000)
    return call(
        level_up,
        [(8, 16, 1024)] * 2,
        [big] * 2 + [mid] * 2 + [(8, 16, 1024)],
        *zero, *one, f0, f1, hleft, hright, nhleft, nhright, *edges, e2,
        flops=30_000_000,
        copies=3,
    )


def solution(mesh):
    wide, narrow = mesh.axis_names
    devices = mesh.devices.reshape(mesh.shape[wide], mesh.shape[narrow] // 2, 2)
    spec = P("wide", ("ny", "core"), None)
    return jax.shard_map(
        lambda p, d, m: tuple(per_device(p, d, m)),
        mesh=Mesh(devices, AX),
        in_specs=(spec,) * 3,
        out_specs=(spec,) * 2,
        check_vma=False,
    )
```

```python
import math

import jax
import jax.numpy as jnp
from jax import lax
from jax.experimental import pallas as pl
from jax.experimental.pallas import tpu as pltpu
from jax.sharding import Mesh, PartitionSpec as P

OMEGA = 0.8
AX = ("wide", "ny", "core")
F32 = jnp.float32
SPARE = 4 * 1024 * 1024


def iota(shape, dim):
    return lax.broadcasted_iota(jnp.int32, shape, dim)


def following(x, dim):
    return pltpu.roll(x, x.shape[dim] - 1, dim)


def preceding(x, dim):
    return pltpu.roll(x, 1, dim)


def lanes(x, r, k):
    if callable(x):
        return x(r, k)
    if isinstance(x, tuple):
        return jnp.concatenate([lanes(part, r, k) for part in x], axis=0)
    return x[r, :, 128 * k : 128 * k + 128]


def row_operator(v, r, c, fa, fb, fz):
    count = v.shape[2] // 128
    lane = iota((v.shape[1], 128), 1)
    here = lanes(v, r, 0)
    turned = pltpu.roll(here, 127, 1)
    out = []
    for k in range(count):
        if k + 1 < count:
            later = lanes(v, r, k + 1)
            later_turned = pltpu.roll(later, 127, 1)
        else:
            later, later_turned = None, 0.0
        gz = lanes(fz, r, k) * (jnp.where(lane == 127, later_turned, turned) - here)
        gz_turned = pltpu.roll(gz, 1, 1)
        if k == 0:
            gz_before = 0.5 * lanes(c, r, 0) * here
        gb = lanes(fb, r, k) * (following(here, 0) - here)
        a = lanes(fa, r, k) * (here - lanes(v, r + 1, k)) + lanes(fa, r - 1, k) * (here - lanes(v, r - 1, k))
        a = a + (preceding(gb, 0) - gb) + (jnp.where(lane == 0, gz_before, gz_turned) - gz)
        out.append(a)
        here, turned, gz_before = later, later_turned, gz_turned
    return out


def row_faces(r, c, fa, fb, fz, w):
    count = c.shape[2] // 128
    cols = c.shape[1]
    lane = iota((cols, 128), 1)
    here = lanes(c, r, 0)
    turned = pltpu.roll(here, 127, 1)
    for k in range(count):
        if k + 1 < count:
            later = lanes(c, r, k + 1)
            later_turned = pltpu.roll(later, 127, 1)
        else:
            later, later_turned = None, 0.0
        at = slice(128 * k, 128 * k + 128)
        z = 0.5 * (here + jnp.where(lane == 127, later_turned, turned))
        z_turned = pltpu.roll(z, 1, 1)
        if k == 0:
            z_before = 0.5 * here
        y = 0.5 * (here + following(here, 0))
        diagonal = 0.5 * (here + lanes(c, r - 1, k)) + 0.5 * (here + lanes(c, r + 1, k))
        diagonal = diagonal + (y + preceding(y, 0)) + (z + jnp.where(lane == 0, z_before, z_turned))
        fa[r, :, at] = 0.5 * (here + lanes(c, r + 1, k))
        fb[r, :, at], fz[r, :, at] = y, z
        w[r, :, at] = jnp.where(here > 0.0, OMEGA / diagonal, 0.0)
        here, turned, z_before = later, later_turned, z_turned


def over_rows(lo, hi, step, body):
    whole = (hi - lo) // step

    def some(i, carry):
        for j in range(step):
            body(lo + i * step + j)
        return carry

    if whole > 1:
        lax.fori_loop(0, whole, some, 0)
        lo = lo + whole * step
    for r in range(lo, hi):
        body(r)


def half_compress(low, high, dim):
    length = low.shape[dim]
    at = iota(low.shape, dim)
    index = (2 * at) % length
    first = jnp.take_along_axis(low, index, axis=dim)
    if high is None:
        return jnp.where(at < length // 2, first, 0.0)
    return jnp.where(at < length // 2, first, jnp.take_along_axis(high, index, axis=dim))


def half_columns(x):
    x = x + following(x, 0)
    tiles = x.shape[0] // 8
    part = lambda t: x[8 * t : 8 * t + 8]
    if tiles == 1:
        return half_compress(x, None, 0)
    x = [half_compress(part(2 * t), part(2 * t + 1), 0) for t in range(tiles // 2)]
    return x[0] if len(x) == 1 else jnp.concatenate(x, axis=0)


def level_one_row(x, r):
    return x[6 + r // 2][:, 512 * (r % 2) : 512 * (r % 2) + 512]


def coarse_sum(first, second, split=False):
    halves = [half_columns(x + y) for x, y in zip(first, second)]
    halves = [x + following(x, 1) for x in halves]
    if split:
        lane = iota((8, 128), 1)
        out = []
        for odd in range(2):
            index = (4 * lane + 2 * odd) % 128
            picked = jnp.take_along_axis(halves[0], index, axis=1)
            for k in range(1, 4):
                picked = jnp.where(lane >= 32 * k, jnp.take_along_axis(halves[k], index, axis=1), picked)
            out.append(picked)
        return out
    if len(halves) == 1:
        return [by_tile(halves[0], None)]
    return [by_tile(halves[k], halves[k + 1]) for k in range(0, len(halves), 2)]


def by_tile(low, high):
    tiles = [
        half_compress(low[8 * t : 8 * t + 8], None if high is None else high[8 * t : 8 * t + 8], 1)
        for t in range(low.shape[0] // 8)
    ]
    return tiles[0] if len(tiles) == 1 else jnp.concatenate(tiles, axis=0)


def blocks_of(x):
    return [x[:, 128 * k : 128 * k + 128] for k in range(x.shape[1] // 128)]


def repeat_lanes(x, block):
    source = block // 2
    index = iota((8, 128), 1) // 2 + 64 * (block % 2)
    return jnp.take_along_axis(x[:, 128 * source : 128 * source + 128], index, axis=1)


def take_rows(x, index):
    pieces = [
        jnp.take_along_axis(x[:, k : k + 128], index, axis=0) for k in range(0, x.shape[1], 128)
    ]
    return pieces[0] if len(pieces) == 1 else jnp.concatenate(pieces, axis=1)


def widen(x, blocks):
    pieces = [repeat_lanes(x, k) for k in range(blocks)]
    return pieces[0] if len(pieces) == 1 else jnp.concatenate(pieces, axis=1)


def widen_split(x):
    lane = iota((8, 128), 1)
    pieces = []
    for k in range(4):
        index = 32 * k + lane // 4
        even = jnp.take_along_axis(x[:, :128], index, axis=1)
        odd = jnp.take_along_axis(x[:, 128:], index, axis=1)
        pieces.append(jnp.where(lane // 2 % 2 == 0, even, odd))
    return jnp.concatenate(pieces, axis=1)


def scalars():
    wide, ny, core = lax.axis_index("wide"), lax.axis_index("ny"), lax.axis_index("core")
    sizes = [lax.axis_size(name) for name in AX]
    narrow = ny * sizes[2] + core
    inside = [
        jnp.where(flag, 1.0, 0.0).astype(F32)
        for flag in (wide > 0, wide < sizes[0] - 1, narrow > 0, narrow < sizes[1] * sizes[2] - 1)
    ]
    return wide, narrow, core, inside


def call(kernel, outs, scratch, *args, flops=1_000_000, copies=0):
    vmem = pl.BlockSpec(memory_space=pltpu.VMEM)
    size = 4 * sum(a.size for a in args)
    held = size + 4 * sum(math.prod(s) for s in outs + scratch)
    return pl.pallas_call(
        kernel,
        out_shape=[jax.ShapeDtypeStruct(s, F32) for s in outs],
        in_specs=[vmem] * len(args),
        out_specs=[pl.BlockSpec(memory_space=pltpu.HBM) if copies else vmem] * len(outs),
        scratch_shapes=[pltpu.VMEM(s, F32) for s in scratch] + [pltpu.SemaphoreType.DMA((copies,))] * (copies > 0),
        compiler_params=pltpu.CompilerParams(vmem_limit_bytes=held + SPARE),
        cost_estimate=pl.CostEstimate(flops=flops, bytes_accessed=0 if flops == 1000 else size, transcendentals=0),
    )(*args)


def before_exchange(p, d, m, c1, c2, up, down, to_left, to_right):
    pack_zero_own(p, d, m, to_left, to_right)
    for n, (x, last, first) in enumerate(((p, 5, 2), (m, 5, 2), (d, 6, 1))):
        for t in range(2):
            up[2 * n + t], down[2 * n + t] = x[last, 8 * t : 8 * t + 8], x[first, 8 * t : 8 * t + 8]
    for i in range(4):
        x = coarse_sum(blocks_of(m[2 * i]), blocks_of(m[2 * i + 1]))
        for k, a in enumerate(x):
            c1[i, :, 128 * k : 128 * k + 128] = 0.125 * a
    for i in range(2):
        even, odd = coarse_sum(blocks_of(c1[2 * i]), blocks_of(c1[2 * i + 1]), True)
        c2[i] = 0.125 * (even + pltpu.roll(odd, 4, 0))
        both = jnp.concatenate([c1[2 * i], c1[2 * i + 1]], axis=1)
        up[6 + i], down[6 + i] = both, both


def columns_zero(vp, vm, vd, side):
    at = iota((8, 1024), 0)
    if side == 0:
        vm, vd = pltpu.roll(vm, 3, 0), pltpu.roll(vd, 6, 0)
        return jnp.where(at < 3, vp, jnp.where(at < 6, vm, vd))
    vm, vd = pltpu.roll(vm, 5, 0), pltpu.roll(vd, 2, 0)
    return jnp.where(at >= 5, vp, jnp.where(at >= 2, vm, vd))


def pack_zero_own(p, d, m, to_left, to_right):
    for a in range(8):
        for side, out in ((0, to_left), (1, to_right)):
            tile = slice(8 * side, 8 * side + 8)
            out[a] = columns_zero(p[a, tile], m[a, tile], d[a, tile], side)


def pack_zero_edge(left, right, to_left, to_right):
    _, _, _, (low, high, _, _) = scalars()
    for side, out in ((0, to_left), (1, to_right)):
        tile = slice(8 * side, 8 * side + 8)
        for i in range(2):
            nothing = jnp.zeros((8, 1024), F32)
            vd = (left[4, tile] if i == 1 else nothing), (right[4, tile] if i == 0 else nothing)
            out[i] = columns_zero(left[i, tile], left[2 + i, tile], vd[0], side) * low
            out[2 + i] = columns_zero(right[i, tile], right[2 + i, tile], vd[1], side) * high


def faces(c, rows, fa, fb, fz, w, step):
    for k in range(c.shape[2] // 128):
        at = slice(128 * k, 128 * k + 128)
        fa[rows[0] - 1, :, at] = 0.5 * (c[rows[0] - 1, :, at] + c[rows[0], :, at])
    over_rows(rows[0], rows[1], step, lambda r: row_faces(r, c, fa, fb, fz, w))


def sweep(source, target, s, c, fa, fb, fz, w, rows, step):
    def one(r):
        for k, a in enumerate(row_operator(source, r, c, fa, fb, fz)):
            at = slice(128 * k, 128 * k + 128)
            target[r, :, at] = source[r, :, at] + w[r, :, at] * (lanes(s, r, k) - a)

    over_rows(rows[0], rows[1], step, one)


def residual_row(v, s, c, fa, fb, fz, r, cols):
    return [
        (lanes(s, r, k) - a)[0:cols]
        for k, a in enumerate(row_operator(v, r, c, fa, fb, fz))
    ]


def across(r, v, c, s, fa, fz, diagonal, left_over, cols=slice(None)):
    lane = iota(lanes(c, r, 0).shape, 1)
    count = fa.shape[2] // 128
    turn = lambda x, k: pltpu.roll(lanes(x, r, k), 127, 1) if k < count else 0.0
    here, there, c_next, v_next = lanes(c, r, 0), lanes(v, r, 0), turn(c, 0), turn(v, 0)
    for k in range(count):
        at = slice(128 * k, 128 * k + 128)
        c_later, v_later = turn(c, k + 1), turn(v, k + 1)
        z = 0.5 * (here + jnp.where(lane == 127, c_later, c_next))
        flux = z * (jnp.where(lane == 127, v_later, v_next) - there)
        z_turned, flux_turned = pltpu.roll(z, 1, 1), pltpu.roll(flux, 1, 1)
        if k == 0:
            z_before, flux_before = 0.5 * here, 0.5 * here * there
        above, below = 0.5 * (here + lanes(c, r + 1, k)), 0.5 * (here + lanes(c, r - 1, k))
        fa[r, cols, at], fz[r, cols, at] = above, z
        diagonal[r, cols, at] = above + below + (z + jnp.where(lane == 0, z_before, z_turned))
        a = above * (there - lanes(v, r + 1, k)) + below * (there - lanes(v, r - 1, k))
        a = a + (jnp.where(lane == 0, flux_before, flux_turned) - flux)
        left_over[r, cols, at] = lanes(s, r, k) - a
        if k + 1 < count:
            here, there = lanes(c, r, k + 1), lanes(v, r, k + 1)
        c_next, v_next, z_before, flux_before = c_later, v_later, z_turned, flux_turned


def level_zero_own(p, d, m, left, right, v, me, de, fa, fz, diagonal, left_over):
    _, _, _, (low, high, _, _) = scalars()
    for r in range(1, 13):
        a = r - 3
        if a < 0:
            v[r], me[r] = left[r - 1] * low, left[r + 1] * low
        elif a < 8:
            v[r], me[r], de[r] = p[a], m[a], d[a]
        else:
            v[r], me[r] = right[a - 8] * high, right[a - 6] * high
    de[2], de[11] = left[4] * low, right[4] * high
    fa[1] = 0.5 * (me[1] + me[2])
    over_rows(2, 12, 2, lambda r: across(r, v, me, de, fa, fz, diagonal, left_over))


def level_zero(
    own_v, own_me, own_de, own_fa, own_fz, own_diagonal, own_left_over, left, right, nleft, nright,
    nleft_edge, nright_edge,
    field, s1, up, down, me, de, fa, fz, fb, w, v, u, beside, diagonal, left_over,
):
    _, _, _, (low, high, nlow, nhigh) = scalars()
    at = iota((8, 1024), 0)
    own, halo = slice(0, 16), slice(16, 24)
    nothing = jnp.zeros((8, 1024), F32)
    for r in range(14):
        if r in (0, 13):
            beside[r], me[r], de[r, halo] = nothing, nothing, nothing
            continue
        if 3 <= r < 11:
            x, y = nright[r - 3] * nhigh, nleft[r - 3] * nlow
        else:
            e = r - 1 if r < 3 else r - 9
            x, y = nright_edge[e] * nhigh, nleft_edge[e] * nlow
        beside[r] = jnp.where(at < 3, x, jnp.where(at >= 5, y, 0.0))
        x3, y3 = pltpu.roll(x, 5, 0), pltpu.roll(y, 3, 0)
        me[r] = jnp.where(at < 3, x3, jnp.where(at >= 5, y3, 0.0))
        x6, y6 = pltpu.roll(x, 2, 0), pltpu.roll(y, 6, 0)
        de[r, halo] = jnp.where(at < 2, x6, jnp.where(at >= 6, y6, 0.0))

    def late(first):
        rows = (own_v, own_me)[first // 2]

        def row(r, k):
            if r not in (0, 13):
                return lanes(rows, r, k)
            parts = [(left if r == 0 else right)[first + t, :, 128 * k : 128 * k + 128] for t in range(2)]
            return jnp.concatenate(parts, axis=0) * (low if r == 0 else high)

        return row

    edge_v, edge_c = late(0), late(2)
    for t in range(2):
        de[1, 8 * t : 8 * t + 8], de[12, 8 * t : 8 * t + 8] = left[4 + t] * low, right[4 + t] * high
    for k in range(8):
        lane = slice(128 * k, 128 * k + 128)
        fa[0, own, lane] = 0.5 * (edge_c(0, k) + edge_c(1, k))
    fa[0, halo] = 0.5 * me[1]
    de_own = lambda r, k: de[r, own, 128 * k : 128 * k + 128]
    de_halo = lambda r, k: de[r, halo, 128 * k : 128 * k + 128]
    for r in (1, 12):
        across(r, edge_v, edge_c, de_own, fa, fz, diagonal, left_over, own)

    def one(r, edge=False):
        across(r, beside, me, de_halo, fa, fz, diagonal, left_over, halo)
        if not edge:
            de[r, own], fa[r, own], fz[r, own] = own_de[r], own_fa[r], own_fz[r]
        for k in range(8):
            lane = slice(128 * k, 128 * k + 128)
            there, here = lanes((own_v, beside), r, k), lanes((own_me, me), r, k)
            total, rest = [
                x[r, :, lane] if edge else jnp.concatenate([y[r, :, lane], x[r, halo, lane]], axis=0)
                for x, y in ((diagonal, own_diagonal), (left_over, own_left_over))
            ]
            y = 0.5 * (here + following(here, 0))
            flux = y * (following(there, 0) - there)
            total = total + (y + preceding(y, 0))
            factor = jnp.where(here > 0.0, OMEGA / total, 0.0)
            fb[r, :, lane], w[r, :, lane] = y, factor
            u[r, :, lane] = there + factor * (rest - (preceding(flux, 0) - flux))

    one(1, True)
    over_rows(2, 12, 5, one)
    one(12, True)
    me = (own_me, me)
    sweep(u, v, de, me, fa, fb, fz, w, (2, 12), 3)
    field[...] = v[3:11, 0:16]

    def coarse(i, carry):
        r = 2 * i + 3
        x = residual_row(v, de, me, fa, fb, fz, r, 16)
        y = residual_row(v, de, me, fa, fb, fz, r + 1, 16)
        for k, a in enumerate(coarse_sum(x, y)):
            s1[i, :, 128 * k : 128 * k + 128] = 0.5 * a
        return carry

    lax.fori_loop(0, 4, coarse, 0)
    up[...], down[...] = s1[1:4], s1[0:3]


def pack_one(s, c, left, right, c_left, c_right, to_left, to_right):
    _, _, _, (low, high, _, _) = scalars()
    at = iota((8, 512), 0)
    for r in range(1, 11):
        a = r - 4
        if a < 0:
            vc = level_one_row(c_left, r) * low
            vs = left[r - 1] * low if r > 0 else jnp.zeros_like(vc)
        elif a < 4:
            vs, vc = s[a], c[a]
        else:
            vc = level_one_row(c_right, a - 4) * high
            vs = right[a - 4] * high if a < 7 else jnp.zeros_like(vc)
        to_left[r - 1] = jnp.where(at < 4, vc, pltpu.roll(vs, 4, 0))
        to_right[r - 1] = jnp.where(at >= 4, vc, pltpu.roll(vs, 4, 0))


def level_one(s, c, left, right, c_left, c_right, nleft, nright, f0, field, s2, up, down, se, ce, fa, fb, fz, w, v, u):
    _, _, _, (low, high, nlow, nhigh) = scalars()
    at = iota((8, 512), 0)
    for r in range(12):
        a = r - 4
        if a < 0:
            ce[r, 0:8] = level_one_row(c_left, r) * low
            se[r, 0:8] = left[r - 1] * low if r > 0 else jnp.zeros((8, 512), F32)
        elif a < 4:
            se[r, 0:8], ce[r, 0:8] = s[a], c[a]
        else:
            ce[r, 0:8] = level_one_row(c_right, a - 4) * high
            se[r, 0:8] = right[a - 4] * high if a < 7 else jnp.zeros((8, 512), F32)
        if r in (0, 11):
            ce[r, 8:16] = se[r, 8:16] = jnp.zeros((8, 512), F32)
            continue
        x, y = nright[r - 1] * nhigh, nleft[r - 1] * nlow
        ce[r, 8:16] = jnp.where(at < 4, x, y)
        se[r, 8:16] = jnp.where(at < 4, pltpu.roll(x, 4, 0), pltpu.roll(y, 4, 0))
    faces(ce, (1, 11), fa, fb, fz, w, 5)

    for r in range(2, 10):
        u[r] = w[r] * se[r]
    sweep(u, v, se, ce, fa, fb, fz, w, (3, 9), 3)
    field[...] = v[4:8, 0:8]
    for i in range(2):
        r = 2 * i + 4
        x = residual_row(v, se, ce, fa, fb, fz, r, 8)
        y = residual_row(v, se, ce, fa, fb, fz, r + 1, 8)
        even, odd = coarse_sum(x, y, True)
        s2[i] = 0.5 * (even + pltpu.roll(odd, 4, 0))
    for r in range(3):
        for t in range(2):
            up[2 * r + t] = f0[5 + r, 8 * t : 8 * t + 8]
            down[2 * r + t] = f0[r, 8 * t : 8 * t + 8]
    for r in range(2):
        both = jnp.concatenate([field[2 * r], field[2 * r + 1]], axis=1)
        up[6 + r] = both
        down[6 + r] = both


def two_rows(x, y, side):
    at = iota((8, 1024), 0)
    return jnp.where(at < 4 if side == 0 else at >= 4, x, pltpu.roll(y, 4, 0))


def pack_up_own(f0, f1, to_left, to_right):
    for side, out in ((0, to_left), (1, to_right)):
        tile = slice(8 * side, 8 * side + 8)
        for t in range(4):
            out[t] = two_rows(f0[2 * t, tile], f0[2 * t + 1, tile], side)
        pair = [jnp.concatenate([f1[2 * k], f1[2 * k + 1]], axis=1) for k in range(2)]
        out[4] = two_rows(pair[0], pair[1], side)


def pack_up_edge(left, right, to_left, to_right):
    _, _, _, (low, high, _, _) = scalars()
    for side, out in ((0, to_left), (1, to_right)):
        out[0] = two_rows(left[2 + side], left[4 + side], side) * low
        out[1] = two_rows(right[side], right[2 + side], side) * high
        out[2] = two_rows(left[6], left[7], side) * low
        out[3] = two_rows(right[6], right[7], side) * high


def tile_up(own, edge, t):
    if t in (0, 5, 6, 8):
        return edge[(0, 5, 6, 8).index(t)]
    return own[4 if t == 7 else t - 1]


def level_up(
    own_me, me, de, fa, fz, fb, w, se, ce, fa1, fb1, fz1, w1,
    f0, f1, left, right, nleft, nright, nleft_edge, nright_edge, e2,
    out, res, v, u, v1, u1, kept, sent,
):
    _, _, _, (low, high, nlow, nhigh) = scalars()
    at = iota((8, 512), 0)
    half = iota((8, 128), 0)
    for r in range(12):
        if r < 4:
            f = left[6 + r // 2][:, 512 * (r % 2) : 512 * (r % 2) + 512] * low
        elif r < 8:
            f = f1[r - 4]
        else:
            f = right[2 + r // 2][:, 512 * (r % 2) : 512 * (r % 2) + 512] * high
        half_tile = slice(512 * (r % 2), 512 * (r % 2) + 512)
        x = tile_up(nright, nright_edge, 6 + r // 4)[:, half_tile] * nhigh
        y = tile_up(nleft, nleft_edge, 6 + r // 4)[:, half_tile] * nlow
        if r % 4 > 1:
            x, y = pltpu.roll(x, 4, 0), pltpu.roll(y, 4, 0)
        g = jnp.where(at < 4, x, y)
        e = e2[r // 2]
        own = widen_split(take_rows(e, 2 + half // 2))
        beside = widen_split(take_rows(e, jnp.where(half < 4, 6 + half // 2, (half - 4) // 2)))
        v1[r, 0:8] = f + jnp.where(ce[r, 0:8] > 0.0, own, 0.0)
        v1[r, 8:16] = g + jnp.where(ce[r, 8:16] > 0.0, beside, 0.0)
    sweep(v1, u1, se, ce, fa1, fb1, fz1, w1, (1, 11), 5)
    sweep(u1, v1, se, ce, fa1, fb1, fz1, w1, (2, 10), 4)
    zero = iota((8, 1024), 0)
    for r in range(14):
        if r < 3:
            f = [left[2 * r] * low, left[2 * r + 1] * low]
        elif r < 11:
            f = [f0[r - 3, 0:8], f0[r - 3, 8:16]]
        else:
            f = [right[2 * (r - 11)] * high, right[2 * (r - 11) + 1] * high]
        if r in (0, 13):
            f.append(jnp.zeros((8, 1024), F32))
        else:
            t = (r - 1) // 2
            x, y = tile_up(nright, nright_edge, t) * nhigh, tile_up(nleft, nleft_edge, t) * nlow
            if r % 2 == 0:
                x, y = pltpu.roll(x, 4, 0), pltpu.roll(y, 4, 0)
            f.append(jnp.where(zero < 3, x, jnp.where(zero >= 5, y, 0.0)))
        e = v1[(r + 5) // 2]
        pieces = (
            (e[0:8], half // 2),
            (e[0:8], 4 + half // 2),
            (e[8:16], jnp.where(half < 4, half // 2, 4 + half // 2)),
        )
        for t, (part, index) in enumerate(pieces):
            fine = widen(take_rows(part, index), 8)
            tile = slice(8 * t, 8 * t + 8)
            inside = own_me[min(max(r, 1), 12), tile] if t < 2 else me[r]
            v[r, tile] = f[t] + jnp.where(inside > 0.0, fine, 0.0)

    me = (own_me, me)
    sweep(v, u, de, me, fa, fb, fz, w, (1, 13), 3)
    sweep(u, v, de, me, fa, fb, fz, w, (2, 12), 3)
    first = pltpu.make_async_copy(v.at[3:11, 0:16], out, sent.at[0])
    first.start()

    def final(r):
        for k, x in enumerate(residual_row(v, de, me, fa, fb, fz, r, 16)):
            kept[r - 3, :, 128 * k : 128 * k + 128] = x

    over_rows(3, 7, 2, final)
    second = pltpu.make_async_copy(kept.at[0:4], res.at[0:4], sent.at[1])
    second.start()
    over_rows(7, 11, 2, final)
    third = pltpu.make_async_copy(kept.at[4:8], res.at[4:8], sent.at[2])
    third.start()
    for copy in (first, second, third):
        copy.wait()


def shifted(x, step):
    zero = jnp.zeros((1,) + x.shape[1:], F32)
    return jnp.concatenate([x[1:], zero] if step > 0 else [zero, x[:-1]], axis=0)


class Whole:
    def __init__(self, c, cols, length):
        b, z = iota(c.shape, 1), iota(c.shape, 2)
        valid = (b < cols) & (z < length)
        self.fa = 0.5 * (c + shifted(c, 1))
        self.fa_below = 0.5 * (c + shifted(c, -1))
        self.fb = jnp.where(b < cols - 1, 0.5 * (c + following(c, 1)), 0.0)
        self.fz = jnp.where(z < length - 1, 0.5 * (c + following(c, 2)), 0.0)
        half = 0.5 * c
        self.ends = jnp.where(b == 0, half, 0.0) + jnp.where(b == cols - 1, half, 0.0)
        self.ends = self.ends + jnp.where(z == 0, half, 0.0) + jnp.where(z == length - 1, half, 0.0)
        diagonal = self.fa + self.fa_below + self.fb + preceding(self.fb, 1)
        diagonal = diagonal + self.fz + preceding(self.fz, 2) + self.ends
        self.w = jnp.where(valid, OMEGA / diagonal, 0.0)

    def operator(self, v):
        gb = self.fb * (following(v, 1) - v)
        gz = self.fz * (following(v, 2) - v)
        out = self.fa * (v - shifted(v, 1)) + self.fa_below * (v - shifted(v, -1)) + self.ends * v
        return out + (preceding(gb, 1) - gb) + (preceding(gz, 2) - gz)

    def sweep(self, v, s):
        return v + self.w * (s - self.operator(v))


def coarsen_whole(x):
    return jnp.stack([coarse_sum([x[a]], [x[a + 1]])[0] for a in range(0, x.shape[0], 2)])


def refine_row(x, cols_tiles, lanes_too):
    half = iota((8, 128), 0)
    tiles = []
    for t in range(cols_tiles):
        source = x[8 * (t // 2) : 8 * (t // 2) + 8]
        tile = take_rows(source, half // 2 + 4 * (t % 2))
        tiles.append(widen(tile, 1) if lanes_too else tile)
    return tiles[0] if cols_tiles == 1 else jnp.concatenate(tiles, axis=0)


def refine_whole(x, cols_tiles):
    rows = [refine_row(x[a], cols_tiles, True) for a in range(x.shape[0])]
    return jnp.stack([rows[a // 2] for a in range(2 * x.shape[0])])


def multiply(x, y):
    out = [[None] * 4 for _ in range(4)]
    for i in range(4):
        for j in range(4):
            for k in range(4):
                if x[i][k] is not None and y[k][j] is not None:
                    term = x[i][k] * y[k][j]
                    out[i][j] = term if out[i][j] is None else out[i][j] + term
    return out


def apply(x, y):
    out = []
    for i in range(4):
        total = None
        for k in range(4):
            if x[i][k] is not None:
                term = x[i][k] * y[k]
                total = term if total is None else total + term
        out.append(total)
    return out


def inverse(x):
    x = [[jnp.zeros((8, 128), F32) if e is None else e for e in line] for line in x]
    for k in range(4):
        pivot = 1.0 / x[k][k]
        line = [pivot if j == k else x[k][j] * pivot for j in range(4)]
        for i in range(4):
            if i != k:
                factor = x[i][k]
                x[i] = [-factor * pivot if j == k else x[i][j] - factor * line[j] for j in range(4)]
        x[k] = line
    return x


def each(x, move):
    return [[None if e is None else move(e) for e in line] for line in x]


def exact(s, c):
    length = 16
    lane = iota((8, 128), 1)
    row = iota((8, 128), 0)
    valid = lane < length

    def line(x, a, b):
        picked = jnp.take_along_axis(x[a], jnp.full((8, 128), b, jnp.int32), axis=0)
        return jnp.where(valid, picked, 0.0)

    cs = [line(c, k // 2, k % 2) for k in range(4)]
    rhs = [line(s, k // 2, k % 2) for k in range(4)]
    below = [[None] * 4 for _ in range(4)]
    above = [[None] * 4 for _ in range(4)]
    centre = [[None] * 4 for _ in range(4)]
    for k in range(4):
        here = cs[k]
        upper = 0.5 * (here + following(here, 1))
        lower = 0.5 * (here + preceding(here, 1))
        fa, fb = 0.5 * (here + cs[k ^ 2]), 0.5 * (here + cs[k ^ 1])
        diagonal = upper + lower + fa + fb + here
        centre[k][k] = jnp.where(valid, diagonal, 1.0)
        centre[k][k ^ 2], centre[k][k ^ 1] = -fa, -fb
        above[k][k] = jnp.where(lane < length - 1, -upper, 0.0)
        below[k][k] = jnp.where((lane > 0) & valid, -lower, 0.0)
    step = 1
    while step < length:
        ahead = lambda e, step=step: pltpu.roll(e, 128 - step, 1)
        behind = lambda e, step=step: pltpu.roll(e, step, 1)
        solved = inverse(centre)
        t, u, q = multiply(solved, below), multiply(solved, above), apply(solved, rhs)
        t_ahead, u_behind = each(t, ahead), each(u, behind)
        x, y = multiply(below, u_behind), multiply(above, t_ahead)
        centre = [
            [jnp.zeros((8, 128), F32) if centre[i][j] is None else centre[i][j] for j in range(4)]
            for i in range(4)
        ]
        centre = [[centre[i][j] - x[i][j] - y[i][j] for j in range(4)] for i in range(4)]
        x, y = apply(below, [behind(e) for e in q]), apply(above, [ahead(e) for e in q])
        rhs = [rhs[i] - x[i] - y[i] for i in range(4)]
        if 2 * step < length:
            below = each(multiply(below, each(t, behind)), lambda e: -e)
            above = each(multiply(above, each(u, ahead)), lambda e: -e)
        step *= 2
    solved = [jnp.where(valid, e, 0.0) for e in apply(inverse(centre), rhs)]
    return jnp.stack(
        [
            jnp.where(row == 0, solved[2 * a], jnp.where(row == 1, solved[2 * a + 1], 0.0))
            for a in range(2)
        ]
    )


def descend(s, c, cols, length):
    if c.shape[0] == 2:
        return exact(s, c)
    level = Whole(c, cols, length)
    v = level.w * s
    v = level.sweep(v, s)
    r = s - level.operator(v)
    e = descend(0.5 * coarsen_whole(r), 0.125 * coarsen_whole(c), cols // 2, length // 2)
    v = v + refine_whole(e, c.shape[1] // 8)
    v = level.sweep(v, s)
    return level.sweep(v, s)


def split_before(last, first_lane):
    lane = iota(last.shape, 1)
    return jnp.where(lane == 0, first_lane, pltpu.roll(last, 1, 1))


def split_after(first):
    lane = iota(first.shape, 1)
    return jnp.where(lane == 127, 0.0, pltpu.roll(first, 127, 1))


def split_operator(v, r, c, fa, fb, fz, ends):
    here = [lanes(v, r, k) for k in range(2)]
    after = [here[1], split_after(here[0])]
    gz = [lanes(fz, r, k) * (after[k] - here[k]) for k in range(2)]
    before = [split_before(gz[1], 0.5 * lanes(c, r, 0) * here[0]), gz[0]]
    out = []
    for k in range(2):
        gb = lanes(fb, r, k) * (following(here[k], 0) - here[k])
        a = lanes(fa, r, k) * (here[k] - lanes(v, r + 1, k)) + lanes(fa, r - 1, k) * (here[k] - lanes(v, r - 1, k))
        a = a + lanes(ends, r, k) * here[k]
        out.append(a + (preceding(gb, 0) - gb) + (before[k] - gz[k]))
    return out


def split_sweep(source, target, s, c, fa, fb, fz, ends, w, r):
    for k, a in enumerate(split_operator(source, r, c, fa, fb, fz, ends)):
        at = slice(128 * k, 128 * k + 128)
        target[r, :, at] = source[r, :, at] + w[r, :, at] * (s[r, :, at] - a)


def level_two(mine, other, s, c, v, fa, fb, fz, ends, w, s3, c3, u):
    _, _, core, _ = scalars()
    strips = mine.shape[0] // 16
    rows, cols = 32, 8 * strips
    first = iota((8, 128), 0) < 4
    edge = jnp.zeros((cols, 256), F32)
    for x in (c, v, u):
        x[0], x[rows + 1] = edge, edge

    def place(target, r, y, near, far):
        target[r, 8 * y : 8 * y + 8, 0:128] = jnp.where(first, near, pltpu.roll(far, 4, 0))
        target[r, 8 * y : 8 * y + 8, 128:256] = jnp.where(first, pltpu.roll(near, 4, 0), far)

    def load(k):
        for y in range(strips):
            at = k * strips + y
            for i in range(2):
                r = 2 * k + i + 1
                for n, target in enumerate((s, c)):
                    x, z = mine[at, n, i], other[at, n, i]
                    place(target, r, y, jnp.where(core == 0, x, z), jnp.where(core == 0, z, x))

    over_rows(0, rows // 2, 2, load)
    fa[0] = 0.5 * c[1]
    b = iota((cols, 128), 0)

    def one(r):
        here = [lanes(c, r, k) for k in range(2)]
        z = [0.5 * (here[0] + here[1]), 0.5 * (here[1] + split_after(here[0]))]
        before = [split_before(z[1], 0.5 * here[0]), z[0]]
        for k in range(2):
            at = slice(128 * k, 128 * k + 128)
            x, h = here[k], 0.5 * here[k]
            y = jnp.where(b == cols - 1, 0.0, 0.5 * (x + following(x, 0)))
            e = jnp.where((b == 0) | (b == cols - 1), h, 0.0)
            above = h + 0.5 * lanes(c, r + 1, k)
            diagonal = above + (h + 0.5 * lanes(c, r - 1, k)) + (y + preceding(y, 0)) + (z[k] + before[k]) + e
            factor = OMEGA / diagonal
            fa[r, :, at], fb[r, :, at], fz[r, :, at] = above, y, z[k]
            ends[r, :, at], w[r, :, at] = e, factor
            u[r, :, at] = factor * s[r, :, at]

    over_rows(1, rows + 1, 8, one)
    over_rows(1, rows + 1, 16, lambda r: split_sweep(u, v, s, c, fa, fb, fz, ends, w, r))

    def coarse(i):
        total = None
        for r in (2 * i + 1, 2 * i + 2):
            for k, a in enumerate(split_operator(v, r, c, fa, fb, fz, ends)):
                x = lanes(s, r, k) - a
                total = x if total is None else total + x
        s3[i] = 0.5 * half_columns(total)
        total = (lanes(c, 2 * i + 1, 0) + lanes(c, 2 * i + 1, 1)) + (lanes(c, 2 * i + 2, 0) + lanes(c, 2 * i + 2, 1))
        c3[i] = 0.125 * half_columns(total)

    over_rows(0, rows // 2, 4, coarse)


def coarse_levels(s3, c3, s, c, v, fa, fb, fz, ends, w, e2, e3, u, t):
    wide, narrow, _, _ = scalars()
    rows, cols = s.shape[0] - 2, s.shape[1]
    e3[...] = descend(s3[...], c3[...], cols // 2, 128)
    row = lambda step: jnp.clip(2 * wide + step, 0, rows - 1) + 1
    u[0], u[rows + 1], t[0], t[rows + 1] = v[0], v[0], v[0], v[0]
    for i in range(-2, 3):
        k = jnp.clip(wide + i, 0, rows // 2 - 1)
        e = refine_row(e3[k], cols // 8, False)
        for r in (2 * k + 1, 2 * k + 2):
            for half in range(2):
                at = slice(128 * half, 128 * half + 128)
                u[r, :, at] = v[r, :, at] + e
    for i in range(-3, 5):
        split_sweep(u, t, s, c, fa, fb, fz, ends, w, row(i))
    for i in range(-2, 4):
        split_sweep(t, u, s, c, fa, fb, fz, ends, w, row(i))
    for i in range(6):
        turned = pltpu.roll(u[row(i - 2)], lax.rem(cols + 2 - 4 * narrow, cols), 0)
        e2[i] = turned[0:8]


def moved(x, wide_step, narrow_step):
    w, y, k = [lax.axis_size(name) for name in AX]
    n = y * k
    pairs = [
        (i * n + j, ((i + wide_step) % w) * n + (j + narrow_step) % n)
        for i in range(w)
        for j in range(n)
    ]
    return lax.ppermute(x, AX, pairs)


def other_core(x):
    w, y, k = [lax.axis_size(name) for name in AX]
    return lax.ppermute(x, AX, [(i, i ^ 1) for i in range(w * y * k)])


def gathered(s2, c2):
    both = jnp.stack([s2, c2])
    chips = lax.axis_size("wide") * lax.axis_size("ny")
    return lax.all_to_all(jnp.broadcast_to(both[None], (chips,) + both.shape), ("wide", "ny"), 0, 0, tiled=True)


def per_device(p, d, m):
    up = jnp.concatenate([p[6:8], m[6:8], d[7:8]], axis=0)
    down = jnp.concatenate([p[0:2], m[0:2], d[0:1]], axis=0)
    left, right = moved(up, 1, 0), moved(down, -1, 0)
    c1, c2, up, down, to_left, to_right = call(
        before_exchange, [(4, 8, 512), (2, 8, 128)] + [(8, 8, 1024)] * 4, [], p, d, m
    )
    c_left, c_right = moved(up, 1, 0), moved(down, -1, 0)
    nleft, nright = moved(to_right, 0, 1), moved(to_left, 0, -1)
    left, right, nleft, nright = lax.optimization_barrier((left, right, nleft, nright))
    to_left, to_right = call(pack_zero_edge, [(4, 8, 1024)] * 2, [], left, right)
    nleft_edge, nright_edge = moved(to_right, 0, 1), moved(to_left, 0, -1)
    big, own, halo = (14, 24, 1024), (14, 16, 1024), (14, 8, 1024)
    alone = call(level_zero_own, [own] * 7, [], p, d, m, left, right, flops=20_000_000)
    f0, s1, up, down, *zero = call(
        level_zero,
        [(8, 16, 1024), (4, 8, 512)] + [(3, 8, 512)] * 2 + [halo] + [big] * 5,
        [big] * 2 + [halo] + [big] * 2,
        *alone, c_left, c_right, nleft, nright, nleft_edge, nright_edge,
        flops=30_000_000,
    )
    zero = [alone[1], *zero]
    left1, right1 = moved(up, 1, 0), moved(down, -1, 0)
    to_left, to_right = call(pack_one, [(10, 8, 512)] * 2, [], s1, c1, left1, right1, c_left, c_right)
    nleft1, nright1 = moved(to_right, 0, 1), moved(to_left, 0, -1)
    mid = (12, 16, 512)
    f1, s2, up, down, *one = call(
        level_one,
        [(4, 8, 512), (2, 8, 128)] + [(8, 8, 1024)] * 2 + [mid] * 6,
        [mid] * 2,
        s1, c1, left1, right1, c_left, c_right, nleft1, nright1, f0,
        flops=10_000_000,
    )
    hleft, hright = moved(up, 1, 0), moved(down, -1, 0)
    mine = gathered(s2, c2)
    other = other_core(mine)
    whole, small = (34, 32, 256), (16, 16, 128)
    *two, s3, c3 = call(level_two, [whole] * 8 + [small] * 2, [whole], mine, other, flops=1000)
    to_left, to_right = call(pack_up_own, [(5, 8, 1024)] * 2, [], f0, f1)
    nhleft, nhright = moved(to_right, 0, 1), moved(to_left, 0, -1)
    s3, hleft, hright, nhleft, nhright = lax.optimization_barrier((s3, hleft, hright, nhleft, nhright))
    to_left, to_right = call(pack_up_edge, [(4, 8, 1024)] * 2, [], hleft, hright)
    edges = [moved(to_right, 0, 1), moved(to_left, 0, -1)]
    (e2,) = call(coarse_levels, [(6, 8, 256)], [small] + [whole] * 2, s3, c3, *two, flops=1000)
    return call(
        level_up,
        [(8, 16, 1024)] * 2,
        [big] * 2 + [mid] * 2 + [(8, 16, 1024)],
        *zero, *one, f0, f1, hleft, hright, nhleft, nhright, *edges, e2,
        flops=30_000_000,
        copies=3,
    )


def solution(mesh):
    wide, narrow = mesh.axis_names
    devices = mesh.devices.reshape(mesh.shape[wide], mesh.shape[narrow] // 2, 2)
    spec = P("wide", ("ny", "core"), None)
    return jax.shard_map(
        lambda p, d, m: tuple(per_device(p, d, m)),
        mesh=Mesh(devices, AX),
        in_specs=(spec,) * 3,
        out_specs=(spec,) * 2,
        check_vma=False,
    )
```
